32 devices in a mesh: win: 4 (over y, x), seq: 8 (over z, core).
Axes of the slice: x: 2, y: 2, z: 4, core: 2. Of those that a mesh axis runs over, the one named last changes fastest.
Arguments:
- tokens: bfloat16 [16, 2048, 1024], P('win', 'seq'), may hold values from -6 to 6
- condition: bfloat16 [16, 2048, 1024], P('win', 'seq'), may hold values from -4 to 4
- valid_mask: int32 [16, 2048], P('win', 'seq'), may hold values from 0 to 1, as said below
- w_qkv: bfloat16 [1024, 3072], P(('win', 'seq')), may hold values from -0.1875 to 0.1875
- w_out: bfloat16 [1024, 1024], P(('win', 'seq')), may hold values from -1.5 to 1.5
- w_fc: bfloat16 [1024, 4096], P(('win', 'seq')), may hold values from -0.1875 to 0.1875
- w_down: bfloat16 [4096, 1024], P(('win', 'seq')), may hold values from -0.09375 to 0.09375
- norm_gains: bfloat16 [2, 1024], P(None, ('win', 'seq')), may hold values from 0.099609375 to 1.8984375
- biases: bfloat16 [6, 1024], P(None, ('win', 'seq')), may hold values from -2 to 2
- fc_bias: bfloat16 [4096], P(('win', 'seq')), may hold values from -2 to 2
- cotangent: bfloat16 [16, 2048, 1024], P('win', 'seq'), may hold values from -6 to 6
Outputs:
- output: bfloat16 [16, 2048, 1024], P('win', 'seq')
- grad_input: bfloat16 [16, 2048, 1024], P('win', 'seq')
- grad_w_qkv: float32 [1024, 3072], P(('win', 'seq'))
- grad_w_out: float32 [1024, 1024], P(('win', 'seq'))
- grad_w_fc: float32 [1024, 4096], P(('win', 'seq'))
- grad_w_down: float32 [4096, 1024], P(('win', 'seq'))
- grad_gains: float32 [2, 1024], P(None, ('win', 'seq'))
- grad_biases: float32 [6, 1024], P(None, ('win', 'seq'))
- grad_fc_bias: float32 [4096], P(('win', 'seq'))
The draws below stay inside these ranges and needn't reach their ends.
Inputs may be any that keep to these rules, and one draw needn't show every extreme that they name: `valid_mask`: in each window the positions with 1 come first and those with 0 after them; in each aligned group of 4 windows one window is all ones.
All inputs are finite; a program needn't handle non-finite values.
Results may differ from the reference program's by a relative error of at most 0.012.
Values may be sent and summed in bfloat16 or wider, within the bound.
A program may use at most 256 MiB of HBM per device.

```python
import jax
import jax.numpy as jnp
from jax import lax

D = 1024
FF = 4096
HEADS = 16
HDIM = 64
BLOCK = 128
WPW = 4
WINDOWS = 16
WLEN = 2048


def draw_valid_mask(key, part):
    key = jax.random.fold_in(key, 7)
    first_key, second_key = jax.random.split(key)
    lengths = jax.random.randint(first_key, (WINDOWS,), 1, WLEN + 1)
    chosen = jax.random.randint(second_key, (WINDOWS // WPW,), 0, WPW)
    slot_index = jnp.arange(WINDOWS) % WPW
    group_full = jnp.repeat(chosen, WPW, total_repeat_length=WINDOWS)
    lengths = jnp.where(slot_index == group_full, WLEN, lengths)
    position = jnp.arange(WLEN)
    return (position[None, :] < lengths[:, None]).astype(jnp.int32)


def level_of(key, shape, shards, low, high):
    def one(dim, parts):
        steps = jax.random.uniform(jax.random.fold_in(jax.random.fold_in(key, 6), dim), (parts,), jnp.float32, low / len(shards), high / len(shards))
        return jnp.repeat(jnp.exp(steps), shape[dim] // parts).reshape((-1,) + (1,) * (len(shape) - dim - 1))

    gain = one(*shards[0])
    for cut in shards[1:]:
        gain = gain * one(*cut)
    return gain


def scatter_about(own_key, shape, width, most, shards=(), held_as=jnp.bfloat16):
    values = width * jax.random.normal(own_key, shape, jnp.float32)
    if shards:
        values = values * level_of(own_key, shape, shards, -0.22, 0.18)
    return jnp.clip(values, -most, most).astype(held_as)


def setup_inputs(seed: int = 0) -> dict:
    streams_of = jax.random.split(jax.random.key(seed), 12)
    return {
        "tokens": scatter_about(streams_of[0], (WINDOWS, WLEN, D), 1.0, 6.0, ((0, 4), (1, 8))),
        "condition": scatter_about(streams_of[1], (WINDOWS, WLEN, D), 0.5, 4.0, ((0, 4), (1, 8))),
        "valid_mask": draw_valid_mask(jax.random.fold_in(streams_of[11], 71), 0),
        "w_qkv": scatter_about(streams_of[3], (D, 3 * D), D ** -0.5, 0.1875, ((0, 32),)),
        "w_out": scatter_about(streams_of[4], (D, D), (D // 64) ** -0.5, 1.5, ((0, 32),)),
        "w_fc": scatter_about(streams_of[5], (D, FF), D ** -0.5, 0.1875, ((0, 32),)),
        "w_down": scatter_about(streams_of[6], (FF, D), FF ** -0.5, 0.09375, ((0, 32),)),
        "norm_gains": jnp.clip(1.0 + 0.18 * jax.random.normal(streams_of[7], (2, D), jnp.float32), 0.099609375, 1.8984375).astype(jnp.bfloat16),
        "biases": scatter_about(streams_of[8], (6, D), 0.3, 2.0, ((1, 32),)),
        "fc_bias": scatter_about(streams_of[9], (FF,), 0.3, 2.0, ((0, 32),)),
        "cotangent": scatter_about(streams_of[10], (WINDOWS, WLEN, D), 1.0, 6.0, ((0, 4), (1, 8))),
    }


@jax.custom_vjp
def low(v):
    return lax.optimization_barrier(v.astype(jnp.bfloat16)).astype(jnp.float32)

@jax.custom_vjp
def low_back(v):
    return v

def low_keep(v):
    return (low(v), None)

def low_pass(kept, grad):
    return (grad,)

def back_keep(v):
    return (v, None)

def back_low(kept, grad):
    return (low(grad),)
low.defvjp(low_keep, low_pass)
low_back.defvjp(back_keep, back_low)

def layer_norm(rows_in, gain_vec, shift_vec):
    row_mean = lax.optimization_barrier(jnp.mean(rows_in, axis=-1, keepdims=True))
    centered = rows_in - row_mean
    row_var = lax.optimization_barrier(jnp.mean(centered * centered, axis=-1, keepdims=True))
    return centered * lax.rsqrt(row_var + 1e-05) * gain_vec + shift_vec

def layer_block(params, hidden_in, cond_in, keep_rows):
    w_qkv, w_out, w_fc, w_down, norm_gains, biases, fc_bias = params
    highest = lax.Precision.HIGHEST
    model_width = hidden_in.shape[1]
    length = hidden_in.shape[0]
    hidden = hidden_in + cond_in
    normed = low(layer_norm(hidden, norm_gains[0], biases[0]))
    projected = jnp.dot(normed, w_qkv, precision=highest)
    queries = low(low_back(projected[:, :model_width] + biases[1]))
    key_rows = low(low_back(projected[:, model_width:2 * model_width]))
    values = low(low_back(projected[:, 2 * model_width:] + biases[2]))
    head_shape = (length // BLOCK, BLOCK, HEADS, HDIM)
    scores = jnp.einsum('bqhd,bkhd->bhqk', queries.reshape(head_shape), key_rows.reshape(head_shape), precision=highest) * 0.125
    scores = low_back(scores)
    causal = jnp.arange(BLOCK)[:, None] >= jnp.arange(BLOCK)[None, :]
    scores = jnp.where(causal, scores, -1e+30)
    probs = low(jax.nn.softmax(scores, axis=-1))
    mixed = jnp.einsum('bhqk,bkhd->bqhd', probs, values.reshape(head_shape), precision=highest).reshape(length, model_width)
    mixed = low(low_back(mixed))
    attended = low_back(jnp.dot(mixed, w_out, precision=highest) + biases[3])
    after_attn = hidden + attended
    normed_two = low(layer_norm(after_attn, norm_gains[1], biases[4]))
    pre_gelu = low_back(jnp.dot(normed_two, w_fc, precision=highest) + fc_bias)
    gelu_out = low(jax.nn.gelu(pre_gelu, approximate=False))
    mlp_out = low_back(jnp.dot(gelu_out, w_down, precision=highest) + biases[5])
    return (after_attn + mlp_out) * keep_rows[:, None]

def reference(tokens, condition, valid_mask, w_qkv, w_out, w_fc, w_down, norm_gains, biases, fc_bias, cotangent):
    params = tuple((item.astype(jnp.float32) for item in (w_qkv, w_out, w_fc, w_down, norm_gains, biases, fc_bias)))

    def one_window(totals, window):
        tok_win, cond_win, mask_win, cot_win = window
        keep_rows = mask_win.astype(jnp.float32)

        def forward(param_set, hidden_in, cond_in):
            return layer_block(param_set, hidden_in, cond_in, keep_rows)
        out_win, backward = jax.vjp(forward, params, tok_win.astype(jnp.float32), cond_win.astype(jnp.float32))
        grad_params, grad_hidden, grad_cond = backward(cot_win.astype(jnp.float32))
        totals = jax.tree.map(lambda first, second: first + second, totals, grad_params)
        return (totals, (out_win.astype(jnp.bfloat16), grad_hidden.astype(jnp.bfloat16)))
    zeros = jax.tree.map(jnp.zeros_like, params)
    grads, (output, grad_input) = lax.scan(one_window, zeros, (tokens, condition, valid_mask, cotangent))
    return (output, grad_input, grads[0], grads[1], grads[2], grads[3], grads[4], grads[5], grads[6])
```

```python
import functools
from functools import partial

import jax
import jax.numpy as jnp
from jax import lax
from jax.experimental import pallas as pl
from jax.experimental.pallas import tpu as pltpu
from jax.sharding import PartitionSpec as P

MESH = pl.DeviceIdType.MESH
ALL = slice(None)


class Place:
    def __init__(self):
        win, seq = lax.axis_index("win"), lax.axis_index("seq")
        self.y, self.x = win // 2, win % 2
        self.z, self.c = seq // 2, seq % 2

    def device(self, y=None, x=None, z=None, c=None):
        y = self.y if y is None else y
        x = self.x if x is None else x
        z = self.z if z is None else z
        c = self.c if c is None else c
        return (y * 2 + x, z * 2 + c)

    def partner(self, dim):
        if dim == "x":
            return self.device(x=1 - self.x)
        if dim == "y":
            return self.device(y=1 - self.y)
        return self.device(c=1 - self.c)


def greet(place):
    barrier = pltpu.get_barrier_semaphore()
    others = [place.partner(dim) for dim in "xyc"]
    others += [place.device(z=(place.z + t) % 4) for t in (1, 2, 3)]
    for device in others:
        pl.semaphore_signal(barrier, inc=1, device_id=device, device_id_type=MESH)
    pl.semaphore_wait(barrier, 6)


def guarded(cond, thunk):
    if cond is None:
        thunk()
    else:
        pl.when(cond)(thunk)


class Gather:
    def __init__(self, place, view, order, send, recv, slack=0):
        self.p, self.view, self.send, self.recv = place, view, send, recv
        self.order, self.sent = order, []
        self.ticks = self.plan(slack)

    def region(self, got, **at):
        p = self.p
        pick = lambda d, own: at[d] if d in at else (ALL if d in got else own)
        return self.view(pick("y", p.y), pick("x", p.x), pick("z", p.z), at.get("c", p.c))

    def copy(self, region, device, number):
        return pltpu.make_async_remote_copy(
            region, region, self.send.at[number], self.recv.at[number],
            device_id=device, device_id_type=MESH)

    def push(self, cond, make, device, number):
        def go():
            self.copy(make(), device, number).start()
        guarded(cond, go)

        def end():
            self.copy(make(), device, number).wait_send()
        self.sent.append((cond, end))

    def take(self, cond, make, number):
        def go():
            self.copy(make(), self.p.device(c=1 - self.p.c), number).wait_recv()
        guarded(cond, go)

    def both(self, cond, other):
        return other if cond is None else jnp.logical_and(cond, other)

    def line_push(self, got, cond):
        for t in (1, 2, 3):
            self.push(cond, lambda: self.region(got), self.p.device(z=(self.p.z + t) % 4), 1 + t)

    def line_take(self, got, cond):
        for t in (1, 2, 3):
            self.take(cond, lambda t=t: self.region(got, z=(self.p.z + 4 - t) % 4), 1 + t)

    def plan(self, slack):
        out = []
        p = self.p
        orders = {0: (("xzy", None),), 1: (("yzx", None),),
                  2: (("zxy", p.c == 0), ("zyx", p.c == 1))}[self.order]
        lists = []
        for order, cond in orders:
            ticks = [[]]
            got = ""
            ex = 0
            for dim in order:
                if dim == "z":
                    ticks[-1].append(functools.partial(self.line_push, got, cond))
                    ticks.append([])
                    ticks[-1].append(functools.partial(self.line_take, got, cond))
                else:
                    ticks[-1].append(functools.partial(
                        self.push, cond, functools.partial(self.region, got), p.partner(dim), ex))
                    if ex == 1:
                        ticks.extend([] for _ in range(slack))
                    ticks.append([])
                    own = p.x if dim == "x" else p.y
                    ticks[-1].append(functools.partial(
                        self.take, cond, functools.partial(self.region, got, **{dim: 1 - own}), ex))
                    ex += 1
                got += dim
            ticks[-1].append(functools.partial(self.push, cond, functools.partial(self.region, "xyz"),
                                               p.partner("c"), 8))
            ticks.append([])
            ticks[-1].append(functools.partial(self.take, cond,
                                               functools.partial(self.region, "xyz", c=1 - p.c), 8))
            lists.append(ticks)
        n = max(len(t) for t in lists)
        for i in range(n):
            thunks = [f for t in lists if i < len(t) for f in t[i]]
            out.append(thunks)
        return out

    def tick(self, i):
        for f in self.ticks[i]:
            f()

    def finish(self):
        for cond, end in self.sent:
            guarded(cond, end)


def run_ticks(pieces, starts):
    last = max(s + len(p.ticks) for p, s in zip(pieces, starts))
    for now in range(last):
        for p, s in zip(pieces, starts):
            if 0 <= now - s < len(p.ticks):
                p.tick(now - s)
    for p in pieces:
        p.finish()


class Scatter:
    def __init__(self, place, slot, bufs, order, send, recv, put):
        self.p, self.slot, self.bufs, self.put = place, slot, bufs, put
        self.send, self.recv, self.sent = send, recv, []
        self.ticks = self.plan(order)

    def region(self, left, **at):
        p = self.p
        pick = lambda d, own: at[d] if d in at else (ALL if d in left else own)
        return self.slot.at[pick("y", p.y), pick("x", p.x), pick("z", p.z), at.get("c", p.c)]

    def push(self, cond, make, buf, device, number):
        def copy():
            return pltpu.make_async_remote_copy(
                make(), buf, self.send.at[number], self.recv.at[number],
                device_id=device, device_id_type=MESH)
        guarded(cond, lambda: copy().start())
        self.sent.append((cond, lambda: copy().wait_send()))

    def take(self, cond, makes, bufs, numbers, last):
        def go():
            for buf, number in zip(bufs, numbers):
                pltpu.make_async_remote_copy(
                    buf, buf, self.send.at[number], self.recv.at[number],
                    device_id=self.p.partner("c"), device_id_type=MESH).wait_recv()
            region = makes()
            shape = region.shape
            outer = [()]
            while len(shape) - len(outer[0]) > 3:
                outer = [o + (i,) for o in outer for i in range(shape[len(o)])]
            for o in outer:
                total = region[o + (Ellipsis,)].astype(jnp.float32)
                for buf in bufs:
                    total = total + buf[o + (Ellipsis,)].astype(jnp.float32)
                if last:
                    self.put(total)
                else:
                    region[o + (Ellipsis,)] = total.astype(region.dtype)
        guarded(cond, go)

    def plan(self, order):
        p = self.p
        core, first, second, line = self.bufs
        variants = {0: (("yzx", None),), 1: (("xzy", None),),
                    2: (("yxz", p.c == 0), ("xyz", p.c == 1))}[order]
        ticks = [[] for _ in range(5)]
        for dims, cond in variants:
            left = "xyz"
            ticks[0].append(functools.partial(
                self.push, cond, lambda: self.region("xyz", c=1 - p.c), core, p.partner("c"), 0))
            ticks[1].append(functools.partial(
                self.take, cond, lambda: self.region("xyz"), [core], [0], False))
            for i, dim in enumerate(dims):
                rest = left.replace(dim, "")
                last = i == 2
                mine = functools.partial(self.region, rest)
                if dim == "z":
                    bufs = [line.at[t - 1] if rest else line.at[t - 1, 0] for t in (1, 2, 3)]
                    for t in (1, 2, 3):
                        to = (p.z + t) % 4
                        ticks[i + 1].append(functools.partial(
                            self.push, cond, functools.partial(self.region, rest, z=to),
                            bufs[t - 1], p.device(z=to), 2 + t))
                    ticks[i + 2].append(functools.partial(
                        self.take, cond, mine, bufs, [3, 4, 5], last))
                else:
                    buf = first if i == 0 else (second if i == 1 else second.at[0])
                    number = 1 if i == 0 else 2
                    own = p.x if dim == "x" else p.y
                    ticks[i + 1].append(functools.partial(
                        self.push, cond, functools.partial(self.region, rest, **{dim: 1 - own}),
                        buf, p.partner(dim), number))
                    ticks[i + 2].append(functools.partial(
                        self.take, cond, mine, [buf], [number], last))
                left = rest
        return ticks

    def tick(self, i):
        for f in self.ticks[i]:
            f()

    def finish(self):
        for cond, end in self.sent:
            guarded(cond, end)


SCATTER_SEMS = 6
GATHER_SEMS = 9


def scatter_bufs(count, rows, cols, dtype=jnp.bfloat16):
    return [pltpu.VMEM((count, 2, 2, 4, rows, cols), dtype), pltpu.VMEM((count, 2, 4, rows, cols), dtype),
            pltpu.VMEM((count, 4, rows, cols), dtype), pltpu.VMEM((count, 3, 2, rows, cols), dtype),
            pltpu.SemaphoreType.DMA((count, SCATTER_SEMS)), pltpu.SemaphoreType.DMA((count, SCATTER_SEMS))]


HEADS = 16
BLOCK = 128


def layer_norm(rows_in, gain_vec, shift_vec):
    row_mean = jnp.mean(rows_in, axis=-1, keepdims=True)
    centered = rows_in - row_mean
    row_var = jnp.mean(centered * centered, axis=-1, keepdims=True)
    return centered * lax.rsqrt(row_var + 1e-05) * gain_vec + shift_vec


def outer_sum(first, second):
    return lax.dot_general(
        first, second, (((0,), (0,)), ((), ())), preferred_element_type=jnp.float32
    )


def times_transposed(first, second):
    return lax.dot_general(
        first, second, (((1,), (1,)), ((), ())), preferred_element_type=jnp.float32
    )


def masked_scores(queries_h, keys_h):
    scores = (
        jnp.einsum("bqhd,bkhd->bhqk", queries_h, keys_h, preferred_element_type=jnp.float32) * 0.125
    )
    causal = lax.broadcasted_iota(jnp.int32, scores.shape, 2) >= lax.broadcasted_iota(
        jnp.int32, scores.shape, 3
    )
    return jnp.where(causal, scores, -1e30)


def plain_body(
    tokens,
    condition,
    valid_mask,
    w_qkv,
    w_out,
    w_fc,
    w_down,
    norm_gains,
    biases,
    fc_bias,
    cotangent,
):
    window_count, span_rows, model_width = tokens.shape
    row_total = window_count * span_rows
    head_size = model_width // HEADS
    head_shape = (row_total // BLOCK, BLOCK, HEADS, head_size)
    keep_rows = valid_mask.reshape(row_total, 1).astype(jnp.float32)
    hidden = tokens.reshape(row_total, model_width).astype(jnp.float32) + condition.reshape(
        row_total, model_width
    ).astype(jnp.float32)
    full_qkv, full_out, full_gains, full_biases = (
        lax.all_gather(w_qkv, ("win", "seq"), axis=0, tiled=True),
        lax.all_gather(w_out, ("win", "seq"), axis=0, tiled=True),
        lax.all_gather(norm_gains, ("win", "seq"), axis=1, tiled=True),
        lax.all_gather(biases, ("win", "seq"), axis=1, tiled=True),
    )
    gain_f = full_gains.astype(jnp.float32)
    bias_f = full_biases.astype(jnp.float32)
    normed_f, norm_back_one = jax.vjp(layer_norm, hidden, gain_f[0], bias_f[0])
    normed = normed_f.astype(jnp.bfloat16)
    projected = jnp.dot(normed, full_qkv, preferred_element_type=jnp.float32)
    queries = (projected[:, :model_width] + bias_f[1]).astype(jnp.bfloat16).reshape(head_shape)
    key_rows = projected[:, model_width : 2 * model_width].astype(jnp.bfloat16).reshape(head_shape)
    values = (projected[:, 2 * model_width :] + bias_f[2]).astype(jnp.bfloat16).reshape(head_shape)
    scores = masked_scores(queries, key_rows)
    row_max = jnp.max(scores, axis=-1, keepdims=True)
    log_total = row_max + jnp.log(jnp.sum(jnp.exp(scores - row_max), axis=-1, keepdims=True))
    probs = jnp.exp(scores - log_total).astype(jnp.bfloat16)
    mixed = jnp.einsum("bhqk,bkhd->bqhd", probs, values, preferred_element_type=jnp.float32)
    mixed = mixed.reshape(row_total, model_width).astype(jnp.bfloat16)
    after_attn = hidden + jnp.dot(mixed, full_out, preferred_element_type=jnp.float32) + bias_f[3]
    full_fc, full_down, full_fc_bias = (
        lax.all_gather(w_fc, ("win", "seq"), axis=0, tiled=True),
        lax.all_gather(w_down, ("win", "seq"), axis=0, tiled=True),
        lax.all_gather(fc_bias, ("win", "seq"), axis=0, tiled=True),
    )
    normed_two_f, norm_back_two = jax.vjp(layer_norm, after_attn, gain_f[1], bias_f[4])
    normed_two = normed_two_f.astype(jnp.bfloat16)
    pre_gelu = jnp.dot(
        normed_two, full_fc, preferred_element_type=jnp.float32
    ) + full_fc_bias.astype(jnp.float32)
    gelu_f, gelu_back = jax.vjp(partial(jax.nn.gelu, approximate=False), pre_gelu)
    gelu_out = gelu_f.astype(jnp.bfloat16)
    final_rows = (
        after_attn + jnp.dot(gelu_out, full_down, preferred_element_type=jnp.float32) + bias_f[5]
    )
    output = (final_rows * keep_rows).astype(jnp.bfloat16).reshape(tokens.shape)
    back_fc, back_down = (
        lax.all_gather(w_fc, ("win", "seq"), axis=0, tiled=True),
        lax.all_gather(w_down, ("win", "seq"), axis=0, tiled=True),
    )
    grad_final = cotangent.reshape(row_total, model_width).astype(jnp.float32) * keep_rows
    grad_mlp = grad_final.astype(jnp.bfloat16)
    grad_down_local = outer_sum(gelu_out, grad_mlp)
    grad_down_bias = jnp.sum(grad_mlp.astype(jnp.float32), axis=0)
    grad_gelu = times_transposed(grad_mlp, back_down)
    grad_pre = gelu_back(grad_gelu)[0].astype(jnp.bfloat16)
    grad_fc_local = outer_sum(normed_two, grad_pre)
    grad_fc_bias_local = jnp.sum(grad_pre.astype(jnp.float32), axis=0)
    grad_w_fc, grad_w_down, grad_fc_bias = (
        lax.psum_scatter(grad_fc_local, ("win", "seq"), scatter_dimension=0, tiled=True),
        lax.psum_scatter(grad_down_local, ("win", "seq"), scatter_dimension=0, tiled=True),
        lax.psum_scatter(grad_fc_bias_local, ("win", "seq"), scatter_dimension=0, tiled=True),
    )
    grad_normed_two = times_transposed(grad_pre, back_fc)
    grad_after_norm, grad_gain_two, grad_shift_two = norm_back_two(grad_normed_two)
    grad_after = grad_final + grad_after_norm
    back_qkv, back_out = (
        lax.all_gather(w_qkv, ("win", "seq"), axis=0, tiled=True),
        lax.all_gather(w_out, ("win", "seq"), axis=0, tiled=True),
    )
    grad_attn = grad_after.astype(jnp.bfloat16)
    grad_out_local = outer_sum(mixed, grad_attn)
    grad_out_bias = jnp.sum(grad_attn.astype(jnp.float32), axis=0)
    grad_mixed = times_transposed(grad_attn, back_out).astype(jnp.bfloat16).reshape(head_shape)
    probs_full = jnp.exp(masked_scores(queries, key_rows) - log_total)
    grad_probs = jnp.einsum(
        "bqhd,bkhd->bhqk", grad_mixed, values, preferred_element_type=jnp.float32
    )
    grad_values = jnp.einsum(
        "bhqk,bqhd->bkhd", probs, grad_mixed, preferred_element_type=jnp.float32
    )
    grad_values = grad_values.reshape(row_total, model_width).astype(jnp.bfloat16)
    grad_scores = probs_full * (
        grad_probs - jnp.sum(probs_full * grad_probs, axis=-1, keepdims=True)
    )
    grad_scores = grad_scores.astype(jnp.bfloat16)
    grad_queries = (
        jnp.einsum("bhqk,bkhd->bqhd", grad_scores, key_rows, preferred_element_type=jnp.float32)
        * 0.125
    )
    grad_keys = (
        jnp.einsum("bhqk,bqhd->bkhd", grad_scores, queries, preferred_element_type=jnp.float32)
        * 0.125
    )
    grad_queries = grad_queries.reshape(row_total, model_width).astype(jnp.bfloat16)
    grad_keys = grad_keys.reshape(row_total, model_width).astype(jnp.bfloat16)
    grad_query_bias = jnp.sum(grad_queries.astype(jnp.float32), axis=0)
    grad_value_bias = jnp.sum(grad_values.astype(jnp.float32), axis=0)
    grad_projected = jnp.concatenate([grad_queries, grad_keys, grad_values], axis=1)
    grad_qkv_local = outer_sum(normed, grad_projected)
    grad_normed = times_transposed(grad_projected, back_qkv)
    grad_hidden_norm, grad_gain_one, grad_shift_one = norm_back_one(grad_normed)
    grad_input = (grad_after + grad_hidden_norm).astype(jnp.bfloat16).reshape(tokens.shape)
    gains_local = jnp.stack([grad_gain_one, grad_gain_two])
    biases_local = jnp.stack(
        [
            grad_shift_one,
            grad_query_bias,
            grad_value_bias,
            grad_out_bias,
            grad_shift_two,
            grad_down_bias,
        ]
    )
    grad_w_qkv, grad_w_out, grad_gains, grad_biases = (
        lax.psum_scatter(grad_qkv_local, ("win", "seq"), scatter_dimension=0, tiled=True),
        lax.psum_scatter(grad_out_local, ("win", "seq"), scatter_dimension=0, tiled=True),
        lax.psum_scatter(gains_local, ("win", "seq"), scatter_dimension=1, tiled=True),
        lax.psum_scatter(biases_local, ("win", "seq"), scatter_dimension=1, tiled=True),
    )
    return (
        output,
        grad_input,
        grad_w_qkv,
        grad_w_out,
        grad_w_fc,
        grad_w_down,
        grad_gains,
        grad_biases,
        grad_fc_bias,
    )


GATHER_ORDER = (2, 0, 2, 2, 1, 2)


def pack_small(gains, biases, fc_bias, rows, dtype):
    devices = fc_bias.shape[0] // 128
    eight = jnp.concatenate([gains, biases], axis=0)
    eight = eight.reshape(8, devices, 32).transpose(1, 0, 2).reshape(devices, 2, 128)
    packed = jnp.concatenate([eight, fc_bias.reshape(devices, 1, 128)], axis=1)
    return jnp.pad(packed, ((0, 0), (0, rows - 3), (0, 0))).astype(dtype)


def unpack_small(packed):
    devices = packed.shape[0]
    eight = packed[:, :2].reshape(devices, 8, 32).transpose(1, 0, 2).reshape(8, devices * 32)
    return eight[:2], eight[2:], packed[:, 2].reshape(devices * 128)


def gather_all(w_qkv, w_out, w_fc, w_down, norm_gains, biases, fc_bias):
    small = pack_small(norm_gains, biases, fc_bias, 16, jnp.bfloat16)[0]
    shards = (small, w_qkv, w_out, w_fc, w_down)
    cuts = [(0, (0, 16), (0, 128))]
    cuts += [(1, (0, 32), (i * 512, 512)) for i in range(6)]
    cuts += [(2, (0, 32), (i * 512, 512)) for i in range(2)]
    cuts += [(3, (0, 32), (i * 512, 512)) for i in range(8)]
    cuts += [(4, (i * 16, 16), (0, 1024)) for i in range(8)]
    count = len(cuts)

    def kernel(*refs):
        ins, fulls, (send, recv, local) = refs[:5], refs[5:10], refs[10:]
        place = Place()
        greet(place)
        own = [
            pltpu.make_async_copy(s, f.at[place.y, place.x, place.z, place.c], local.at[i])
            for i, (s, f) in enumerate(zip(ins, fulls))
        ]
        for c in own:
            c.start()
        for c in own:
            c.wait()

        def make(k):
            n, (r0, r), (c0, w) = cuts[k]
            view = lambda y, x, z, c: fulls[n].at[y, x, z, c, pl.ds(r0, r), pl.ds(c0, w)]
            return Gather(place, view, GATHER_ORDER[k % 6], send.at[k], recv.at[k], 1)

        run_ticks([make(k) for k in range(count)], [(k + 2) // 3 for k in range(count)])

    fulls = pl.pallas_call(
        kernel,
        out_shape=[jax.ShapeDtypeStruct((2, 2, 4, 2) + s.shape, s.dtype) for s in shards],
        in_specs=[pl.BlockSpec(memory_space=pl.ANY)] * 5,
        out_specs=[pl.BlockSpec(memory_space=pl.ANY)] * 5,
        scratch_shapes=[
            pltpu.SemaphoreType.DMA((count, GATHER_SEMS)),
            pltpu.SemaphoreType.DMA((count, GATHER_SEMS)),
            pltpu.SemaphoreType.DMA((5,)),
        ],
        compiler_params=pltpu.CompilerParams(collective_id=0, has_side_effects=True),
    )(*shards)
    mats = [f.reshape(-1, f.shape[-1]) for f in fulls[1:]]
    return (*mats, *unpack_small(fulls[0].reshape(32, 16, 128)))


def scatter_all(g_qkv, g_out, g_fc, g_down, gains, biases, fc_bias):
    small = pack_small(gains, biases, fc_bias, 8, jnp.float32)
    full = [g.astype(jnp.bfloat16) for g in (g_qkv, g_out, g_fc, g_down)]
    shapes = [(g.shape[0] // 32, g.shape[1]) for g in full]
    cuts = [
        (n, (r0, 32), (c0, 512))
        for n, (rows, cols) in enumerate(shapes)
        for r0 in range(0, rows, 32)
        for c0 in range(0, cols, 512)
    ]
    count, depth = len(cuts), 18

    def kernel(*refs):
        ins, outs, (slots, own, load_sem), rest = refs[:5], refs[5:10], refs[10:13], refs[13:]
        big, little = rest[:6], rest[6:]
        place = Place()
        greet(place)

        def make(k):
            n, (r0, r), (c0, w) = cuts[k]

            def put(value):
                outs[n + 1][pl.ds(r0, r), pl.ds(c0, w)] = value

            return Scatter(place, slots.at[k % depth], [b.at[k] for b in big[:4]],
                           GATHER_ORDER[k % 6], big[4].at[k], big[5].at[k], put)

        def put_small(value):
            outs[0][...] = value

        def load(k):
            n, (r0, r), (c0, w) = cuts[k]
            return pltpu.make_async_copy(
                ins[n + 1].at[:, :, :, :, pl.ds(r0, r), pl.ds(c0, w)],
                slots.at[k % depth], load_sem.at[k % depth])

        small_load = pltpu.make_async_copy(ins[0], own, load_sem.at[depth])
        small_load.start()
        pieces = [Scatter(place, own, [b.at[0] for b in little[:4]], 2,
                          little[4].at[0], little[5].at[0], put_small)]
        pieces += [make(k) for k in range(count)]
        loads = [small_load] + [load(k) for k in range(count)]
        groups = [[0, 1, 2, 3]] + [list(range(i, min(i + 3, count + 1))) for i in range(4, count + 1, 3)]
        for k in groups[0][1:]:
            loads[k].start()
        for now in range(len(groups) + 4):
            if now + 1 < len(groups):
                for k in groups[now + 1]:
                    loads[k].start()
            for age in range(4, -1, -1):
                if 0 <= now - age < len(groups):
                    for k in groups[now - age]:
                        if age == 0:
                            loads[k].wait()
                        pieces[k].tick(age)
                        if age == 4:
                            pieces[k].finish()

    out = pl.pallas_call(
        kernel,
        out_shape=[jax.ShapeDtypeStruct(s, jnp.float32) for s in [(8, 128)] + shapes],
        in_specs=[pl.BlockSpec(memory_space=pl.ANY)] * 5,
        out_specs=[pl.BlockSpec(memory_space=pltpu.VMEM)] * 5,
        scratch_shapes=[pltpu.VMEM((depth, 2, 2, 4, 2, 32, 512), jnp.bfloat16),
                        pltpu.VMEM((2, 2, 4, 2, 8, 128), jnp.float32),
                        pltpu.SemaphoreType.DMA((depth + 1,))]
        + scatter_bufs(count, 32, 512) + scatter_bufs(1, 8, 128, jnp.float32),
        compiler_params=pltpu.CompilerParams(
            collective_id=1, has_side_effects=True, vmem_limit_bytes=60 << 20),
    )(small.reshape(2, 2, 4, 2, 8, 128),
      *[g.reshape((2, 2, 4, 2) + s) for g, s in zip(full, shapes)])
    return (*out[1:], *unpack_small(out[0][None]))


def body(
    tokens,
    condition,
    valid_mask,
    w_qkv,
    w_out,
    w_fc,
    w_down,
    norm_gains,
    biases,
    fc_bias,
    cotangent,
):
    window_count, span_rows, model_width = tokens.shape
    row_total = window_count * span_rows
    head_size = model_width // HEADS
    head_shape = (row_total // BLOCK, BLOCK, HEADS, head_size)
    keep_rows = valid_mask.reshape(row_total, 1).astype(jnp.float32)
    hidden = tokens.reshape(row_total, model_width).astype(jnp.float32) + condition.reshape(
        row_total, model_width
    ).astype(jnp.float32)
    full_qkv, full_out, full_fc, full_down, full_gains, full_biases, full_fc_bias = gather_all(
        w_qkv, w_out, w_fc, w_down, norm_gains, biases, fc_bias
    )
    gain_f = full_gains.astype(jnp.float32)
    bias_f = full_biases.astype(jnp.float32)
    normed_f, norm_back_one = jax.vjp(layer_norm, hidden, gain_f[0], bias_f[0])
    normed = normed_f.astype(jnp.bfloat16)
    projected = jnp.dot(normed, full_qkv, preferred_element_type=jnp.float32)
    queries = (projected[:, :model_width] + bias_f[1]).astype(jnp.bfloat16).reshape(head_shape)
    key_rows = projected[:, model_width : 2 * model_width].astype(jnp.bfloat16).reshape(head_shape)
    values = (projected[:, 2 * model_width :] + bias_f[2]).astype(jnp.bfloat16).reshape(head_shape)
    scores = masked_scores(queries, key_rows)
    row_max = jnp.max(scores, axis=-1, keepdims=True)
    log_total = row_max + jnp.log(jnp.sum(jnp.exp(scores - row_max), axis=-1, keepdims=True))
    probs = jnp.exp(scores - log_total).astype(jnp.bfloat16)
    mixed = jnp.einsum("bhqk,bkhd->bqhd", probs, values, preferred_element_type=jnp.float32)
    mixed = mixed.reshape(row_total, model_width).astype(jnp.bfloat16)
    after_attn = hidden + jnp.dot(mixed, full_out, preferred_element_type=jnp.float32) + bias_f[3]
    normed_two_f, norm_back_two = jax.vjp(layer_norm, after_attn, gain_f[1], bias_f[4])
    normed_two = normed_two_f.astype(jnp.bfloat16)
    pre_gelu = jnp.dot(
        normed_two, full_fc, preferred_element_type=jnp.float32
    ) + full_fc_bias.astype(jnp.float32)
    gelu_f, gelu_back = jax.vjp(partial(jax.nn.gelu, approximate=False), pre_gelu)
    gelu_out = gelu_f.astype(jnp.bfloat16)
    final_rows = (
        after_attn + jnp.dot(gelu_out, full_down, preferred_element_type=jnp.float32) + bias_f[5]
    )
    output = (final_rows * keep_rows).astype(jnp.bfloat16).reshape(tokens.shape)
    back_fc, back_down, back_qkv, back_out = full_fc, full_down, full_qkv, full_out
    grad_final = cotangent.reshape(row_total, model_width).astype(jnp.float32) * keep_rows
    grad_mlp = grad_final.astype(jnp.bfloat16)
    grad_down_local = outer_sum(gelu_out, grad_mlp)
    grad_down_bias = jnp.sum(grad_mlp.astype(jnp.float32), axis=0)
    grad_gelu = times_transposed(grad_mlp, back_down)
    grad_pre = gelu_back(grad_gelu)[0].astype(jnp.bfloat16)
    grad_fc_local = outer_sum(normed_two, grad_pre)
    grad_fc_bias_local = jnp.sum(grad_pre.astype(jnp.float32), axis=0)
    grad_normed_two = times_transposed(grad_pre, back_fc)
    grad_after_norm, grad_gain_two, grad_shift_two = norm_back_two(grad_normed_two)
    grad_after = grad_final + grad_after_norm
    grad_attn = grad_after.astype(jnp.bfloat16)
    grad_out_local = outer_sum(mixed, grad_attn)
    grad_out_bias = jnp.sum(grad_attn.astype(jnp.float32), axis=0)
    grad_mixed = times_transposed(grad_attn, back_out).astype(jnp.bfloat16).reshape(head_shape)
    probs_full = jnp.exp(masked_scores(queries, key_rows) - log_total)
    grad_probs = jnp.einsum(
        "bqhd,bkhd->bhqk", grad_mixed, values, preferred_element_type=jnp.float32
    )
    grad_values = jnp.einsum(
        "bhqk,bqhd->bkhd", probs, grad_mixed, preferred_element_type=jnp.float32
    )
    grad_values = grad_values.reshape(row_total, model_width).astype(jnp.bfloat16)
    grad_scores = probs_full * (
        grad_probs - jnp.sum(probs_full * grad_probs, axis=-1, keepdims=True)
    )
    grad_scores = grad_scores.astype(jnp.bfloat16)
    grad_queries = (
        jnp.einsum("bhqk,bkhd->bqhd", grad_scores, key_rows, preferred_element_type=jnp.float32)
        * 0.125
    )
    grad_keys = (
        jnp.einsum("bhqk,bqhd->bkhd", grad_scores, queries, preferred_element_type=jnp.float32)
        * 0.125
    )
    grad_queries = grad_queries.reshape(row_total, model_width).astype(jnp.bfloat16)
    grad_keys = grad_keys.reshape(row_total, model_width).astype(jnp.bfloat16)
    grad_query_bias = jnp.sum(grad_queries.astype(jnp.float32), axis=0)
    grad_value_bias = jnp.sum(grad_values.astype(jnp.float32), axis=0)
    grad_projected = jnp.concatenate([grad_queries, grad_keys, grad_values], axis=1)
    grad_qkv_local = outer_sum(normed, grad_projected)
    grad_normed = times_transposed(grad_projected, back_qkv)
    grad_hidden_norm, grad_gain_one, grad_shift_one = norm_back_one(grad_normed)
    grad_input = (grad_after + grad_hidden_norm).astype(jnp.bfloat16).reshape(tokens.shape)
    gains_local = jnp.stack([grad_gain_one, grad_gain_two])
    biases_local = jnp.stack(
        [
            grad_shift_one,
            grad_query_bias,
            grad_value_bias,
            grad_out_bias,
            grad_shift_two,
            grad_down_bias,
        ]
    )
    grad_w_qkv, grad_w_out, grad_w_fc, grad_w_down, grad_gains, grad_biases, grad_fc_bias = scatter_all(
        grad_qkv_local, grad_out_local, grad_fc_local, grad_down_local,
        gains_local, biases_local, grad_fc_bias_local,
    )
    return (
        output,
        grad_input,
        grad_w_qkv,
        grad_w_out,
        grad_w_fc,
        grad_w_down,
        grad_gains,
        grad_biases,
        grad_fc_bias,
    )


def solution(mesh):
    fast = mesh.shape["win"] == 4 and mesh.shape["seq"] == 8
    return jax.shard_map(
        body if fast else plain_body,
        mesh=mesh,
        in_specs=(
            P("win", "seq", None),
            P("win", "seq", None),
            P("win", "seq"),
            P(("win", "seq"), None),
            P(("win", "seq"), None),
            P(("win", "seq"), None),
            P(("win", "seq"), None),
            P(None, ("win", "seq")),
            P(None, ("win", "seq")),
            P(("win", "seq")),
            P("win", "seq", None),
        ),
        out_specs=(
            P("win", "seq", None),
            P("win", "seq", None),
            P(("win", "seq"), None),
            P(("win", "seq"), None),
            P(("win", "seq"), None),
            P(("win", "seq"), None),
            P(None, ("win", "seq")),
            P(None, ("win", "seq")),
            P(("win", "seq")),
        ),
        check_vma=False,
    )
```

```python
import functools
from functools import partial

import jax
import jax.numpy as jnp
from jax import lax
from jax.experimental import pallas as pl
from jax.experimental.pallas import tpu as pltpu
from jax.sharding import PartitionSpec as P

MESH = pl.DeviceIdType.MESH
ALL = slice(None)


class Place:
    def __init__(self):
        win, seq = lax.axis_index("win"), lax.axis_index("seq")
        self.y, self.x = win // 2, win % 2
        self.z, self.c = seq // 2, seq % 2

    def device(self, y=None, x=None, z=None, c=None):
        y = self.y if y is None else y
        x = self.x if x is None else x
        z = self.z if z is None else z
        c = self.c if c is None else c
        return (y * 2 + x, z * 2 + c)

    def partner(self, dim):
        if dim == "x":
            return self.device(x=1 - self.x)
        if dim == "y":
            return self.device(y=1 - self.y)
        return self.device(c=1 - self.c)


def greet(place):
    barrier = pltpu.get_barrier_semaphore()
    others = [place.partner(dim) for dim in "xyc"]
    others += [place.device(z=(place.z + t) % 4) for t in (1, 2, 3)]
    for device in others:
        pl.semaphore_signal(barrier, inc=1, device_id=device, device_id_type=MESH)
    pl.semaphore_wait(barrier, 6)


def guarded(cond, thunk):
    if cond is None:
        thunk()
    else:
        pl.when(cond)(thunk)


class Gather:
    def __init__(self, place, view, order, send, recv, slack=0):
        self.p, self.view, self.send, self.recv = place, view, send, recv
        self.order, self.sent = order, []
        self.ticks = self.plan(slack)

    def region(self, got, **at):
        p = self.p
        pick = lambda d, own: at[d] if d in at else (ALL if d in got else own)
        return self.view(pick("y", p.y), pick("x", p.x), pick("z", p.z), at.get("c", p.c))

    def copy(self, region, device, number):
        return pltpu.make_async_remote_copy(
            region, region, self.send.at[number], self.recv.at[number],
            device_id=device, device_id_type=MESH)

    def push(self, cond, make, device, number):
        def go():
            self.copy(make(), device, number).start()
        guarded(cond, go)

        def end():
            self.copy(make(), device, number).wait_send()
        self.sent.append((cond, end))

    def take(self, cond, make, number):
        def go():
            self.copy(make(), self.p.device(c=1 - self.p.c), number).wait_recv()
        guarded(cond, go)

    def both(self, cond, other):
        return other if cond is None else jnp.logical_and(cond, other)

    def line_push(self, got, cond):
        for t in (1, 2, 3):
            self.push(cond, lambda: self.region(got), self.p.device(z=(self.p.z + t) % 4), 1 + t)

    def line_take(self, got, cond):
        for t in (1, 2, 3):
            self.take(cond, lambda t=t: self.region(got, z=(self.p.z + 4 - t) % 4), 1 + t)

    def plan(self, slack):
        out = []
        p = self.p
        orders = {0: (("xzy", None),), 1: (("yzx", None),),
                  2: (("zxy", p.c == 0), ("zyx", p.c == 1))}[self.order]
        lists = []
        for order, cond in orders:
            ticks = [[]]
            got = ""
            ex = 0
            for dim in order:
                if dim == "z":
                    ticks[-1].append(functools.partial(self.line_push, got, cond))
                    ticks.append([])
                    ticks[-1].append(functools.partial(self.line_take, got, cond))
                else:
                    ticks[-1].append(functools.partial(
                        self.push, cond, functools.partial(self.region, got), p.partner(dim), ex))
                    if ex == 1:
                        ticks.extend([] for _ in range(slack))
                    ticks.append([])
                    own = p.x if dim == "x" else p.y
                    ticks[-1].append(functools.partial(
                        self.take, cond, functools.partial(self.region, got, **{dim: 1 - own}), ex))
                    ex += 1
                got += dim
            ticks[-1].append(functools.partial(self.push, cond, functools.partial(self.region, "xyz"),
                                               p.partner("c"), 8))
            ticks.append([])
            ticks[-1].append(functools.partial(self.take, cond,
                                               functools.partial(self.region, "xyz", c=1 - p.c), 8))
            lists.append(ticks)
        n = max(len(t) for t in lists)
        for i in range(n):
            thunks = [f for t in lists if i < len(t) for f in t[i]]
            out.append(thunks)
        return out

    def tick(self, i):
        for f in self.ticks[i]:
            f()

    def finish(self):
        for cond, end in self.sent:
            guarded(cond, end)


def run_ticks(pieces, starts):
    last = max(s + len(p.ticks) for p, s in zip(pieces, starts))
    for now in range(last):
        for p, s in zip(pieces, starts):
            if 0 <= now - s < len(p.ticks):
                p.tick(now - s)
    for p in pieces:
        p.finish()


class Scatter:
    def __init__(self, place, slot, bufs, order, send, recv, put):
        self.p, self.slot, self.bufs, self.put = place, slot, bufs, put
        self.send, self.recv, self.sent = send, recv, []
        self.ticks = self.plan(order)

    def region(self, left, **at):
        p = self.p
        pick = lambda d, own: at[d] if d in at else (ALL if d in left else own)
        return self.slot.at[pick("y", p.y), pick("x", p.x), pick("z", p.z), at.get("c", p.c)]

    def push(self, cond, make, buf, device, number):
        def copy():
            return pltpu.make_async_remote_copy(
                make(), buf, self.send.at[number], self.recv.at[number],
                device_id=device, device_id_type=MESH)
        guarded(cond, lambda: copy().start())
        self.sent.append((cond, lambda: copy().wait_send()))

    def take(self, cond, makes, bufs, numbers, last):
        def go():
            for buf, number in zip(bufs, numbers):
                pltpu.make_async_remote_copy(
                    buf, buf, self.send.at[number], self.recv.at[number],
                    device_id=self.p.partner("c"), device_id_type=MESH).wait_recv()
            region = makes()
            shape = region.shape
            outer = [()]
            while len(shape) - len(outer[0]) > 3:
                outer = [o + (i,) for o in outer for i in range(shape[len(o)])]
            for o in outer:
                many = last or len(bufs) > 1
                total = region[o + (Ellipsis,)]
                total = total.astype(jnp.float32) if many else total
                for buf in bufs:
                    total = total + buf[o + (Ellipsis,)].astype(total.dtype)
                if last:
                    self.put(total)
                else:
                    region[o + (Ellipsis,)] = total.astype(region.dtype)
        guarded(cond, go)

    def plan(self, order):
        p = self.p
        core, first, second, line = self.bufs
        variants = {0: (("yzx", None),), 1: (("xzy", None),),
                    2: (("yxz", p.c == 0), ("xyz", p.c == 1))}[order]
        ticks = [[] for _ in range(5)]
        for dims, cond in variants:
            left = "xyz"
            ticks[0].append(functools.partial(
                self.push, cond, lambda: self.region("xyz", c=1 - p.c), core, p.partner("c"), 0))
            ticks[1].append(functools.partial(
                self.take, cond, lambda: self.region("xyz"), [core], [0], False))
            for i, dim in enumerate(dims):
                rest = left.replace(dim, "")
                last = i == 2
                mine = functools.partial(self.region, rest)
                if dim == "z":
                    bufs = [line.at[t - 1] if rest else line.at[t - 1, 0] for t in (1, 2, 3)]
                    for t in (1, 2, 3):
                        to = (p.z + t) % 4
                        ticks[i + 1].append(functools.partial(
                            self.push, cond, functools.partial(self.region, rest, z=to),
                            bufs[t - 1], p.device(z=to), 2 + t))
                    ticks[i + 2].append(functools.partial(
                        self.take, cond, mine, bufs, [3, 4, 5], last))
                else:
                    buf = first if i == 0 else (second if i == 1 else second.at[0])
                    number = 1 if i == 0 else 2
                    own = p.x if dim == "x" else p.y
                    ticks[i + 1].append(functools.partial(
                        self.push, cond, functools.partial(self.region, rest, **{dim: 1 - own}),
                        buf, p.partner(dim), number))
                    ticks[i + 2].append(functools.partial(
                        self.take, cond, mine, [buf], [number], last))
                left = rest
        return ticks

    def tick(self, i):
        for f in self.ticks[i]:
            f()

    def finish(self):
        for cond, end in self.sent:
            guarded(cond, end)


SCATTER_SEMS = 6
GATHER_SEMS = 9


def scatter_bufs(count, rows, cols, dtype=jnp.bfloat16):
    return [pltpu.VMEM((count, 2, 2, 4, rows, cols), dtype), pltpu.VMEM((count, 2, 4, rows, cols), dtype),
            pltpu.VMEM((count, 4, rows, cols), dtype), pltpu.VMEM((count, 3, 2, rows, cols), dtype),
            pltpu.SemaphoreType.DMA((count, SCATTER_SEMS)), pltpu.SemaphoreType.DMA((count, SCATTER_SEMS))]


D, FF, CH = 1024, 4096, 512
DELAY = (0, 1, 4, 6, 8)
TILE = 256


def dot_nn(a, b):
    return lax.dot_general(a, b, (((1,), (0,)), ((), ())), preferred_element_type=jnp.float32)


def dot_nt(a, b):
    return lax.dot_general(a, b, (((1,), (1,)), ((), ())), preferred_element_type=jnp.float32)


def dot_tn(a, b):
    return lax.dot_general(a, b, (((0,), (0,)), ((), ())), preferred_element_type=jnp.float32)


def norm_stats(rows_in):
    mean = jnp.mean(rows_in, axis=-1, keepdims=True)
    centered = rows_in - mean
    var = jnp.mean(centered * centered, axis=-1, keepdims=True)
    rstd = lax.rsqrt(var + 1e-05)
    return centered * rstd, rstd


def gelu_both(v):
    phi = 0.5 + 0.5 * lax.erf(v * 0.7071067811865476)
    slope = phi + v * (jnp.exp(-0.5 * v * v) * 0.3989422804014327)
    return (v * phi).astype(jnp.bfloat16), slope


def mlp_kernel(comm, after_hbm, cot_hbm, mask_ref, vec_ref, fcb_ref, wfc_hbm, wdn_hbm,
               out_ref, gafter_hbm, gdown_hbm, gfc_ref, small_ref, gfcb_ref,
               after, gm, n2, n2t, gelu, gp, fin, gn2, wfc, wdn, stage, slots, lsem, wsem, ssem, *rest):
    place = Place()
    if comm:
        greet(place)
    load_after = pltpu.make_async_copy(after_hbm, after, lsem.at[0])
    load_cot = pltpu.make_async_copy(cot_hbm, gm, lsem.at[1])
    load_after.start()
    load_cot.start()

    def fetch_fc(j):
        return pltpu.make_async_copy(wfc_hbm.at[:, pl.ds(j * CH, CH)], wfc.at[j % 2], wsem.at[j % 2, 0])

    def fetch_down(i):
        j = i % (FF // CH)
        return pltpu.make_async_copy(wdn_hbm.at[pl.ds(j * CH, CH), :], wdn.at[i % 2], wsem.at[i % 2, 1])

    fetch_fc(0).start()
    fetch_down(0).start()
    load_after.wait()
    load_cot.wait()

    @pl.loop(0, D // 128)
    def _(i):
        rows = pl.ds(pl.multiple_of(i * 128, 128), 128)
        xhat, _ = norm_stats(after[rows, :])
        v = (xhat * vec_ref[1:2, :] + vec_ref[6:7, :]).astype(jnp.bfloat16)
        n2[rows, :] = v
        n2t[:, rows] = v.T
        g = gm[rows, :].astype(jnp.float32) * mask_ref[rows, :]
        gm[rows, :] = g.astype(jnp.bfloat16)
        fin[rows, :] = jnp.zeros((128, D), jnp.float32)
        gn2[rows, :] = jnp.zeros((128, D), jnp.float32)

    n = FF // CH

    def store(j):
        return pltpu.make_async_copy(stage.at[j % 2], gdown_hbm.at[pl.ds(j * CH, CH), :], ssem.at[j % 2])

    pieces = []
    if comm:
        bufs = rest
        for j in range(n):
            def put(value, j=j):
                gfc_ref[:, pl.ds(j * CH, CH)] = value

            pieces.append(Scatter(place, slots.at[j], [b.at[j] for b in bufs[:4]],
                                  GATHER_ORDER[j % 6], bufs[4].at[j], bufs[5].at[j], put))

    def advance(step, first, last):
        if comm:
            for now in range(first, last):
                @pl.when(step == now)
                def _(now=now):
                    for stage_no in (4, 3, 2, 1, 0):
                        j = now - DELAY[stage_no]
                        if 0 <= j < n:
                            pieces[j].tick(stage_no)
                            if stage_no == 4:
                                pieces[j].finish()

    @pl.loop(0, n)
    def _(j):
        s = j % 2
        fetch_fc(j).wait()
        fetch_down(j).wait()
        fetch_down(j + 1).start()

        @pl.when(j + 1 < n)
        def _():
            fetch_fc(j + 1).start()

        cols = pl.ds(pl.multiple_of(j * CH, CH), CH)
        pre = dot_nn(n2[...], wfc[s]) + fcb_ref[:, cols]
        act, slope = gelu_both(pre)
        grad = (dot_nt(gm[...], wdn[s]) * slope).astype(jnp.bfloat16)
        gelu[:, cols] = act
        gp[...] = grad
        gfcb_ref[:, cols] = jnp.sum(grad.astype(jnp.float32), axis=0, keepdims=True)
        gn2[...] += dot_nt(gp[...], wfc[s])
        slots[j] = dot_nn(n2t[...], gp[...]).astype(jnp.bfloat16).reshape(2, 2, 4, 2, 32, CH)
        advance(j, 0, n)

    @pl.loop(0, n)
    def _(j):
        s = j % 2
        fetch_down(j + n).wait()

        @pl.when(j + 1 < n)
        def _():
            fetch_down(j + n + 1).start()

        @pl.when(j >= 2)
        def _():
            store(j - 2).wait()

        cols = pl.ds(pl.multiple_of(j * CH, CH), CH)
        fin[...] += dot_nn(gelu[:, cols], wdn[s])
        stage[s] = dot_tn(gelu[:, cols], gm[...]).astype(jnp.bfloat16)
        store(j).start()
        advance(j + n, n, 2 * n)

    store(n - 2).wait()
    store(n - 1).wait()

    def norm_step(i, sums):
        rows = pl.ds(pl.multiple_of(i * 128, 128), 128)
        xhat, rstd = norm_stats(after[rows, :])
        keep = mask_ref[rows, :]
        out_ref[rows, :] = ((after[rows, :] + fin[rows, :] + vec_ref[7:8, :]) * keep).astype(jnp.bfloat16)
        g = gn2[rows, :]
        y = g * vec_ref[1:2, :]
        m1 = jnp.mean(y, axis=-1, keepdims=True)
        m2 = jnp.mean(y * xhat, axis=-1, keepdims=True)
        gmf = gm[rows, :].astype(jnp.float32)
        ga = gmf + rstd * (y - m1 - xhat * m2)
        fin[rows, :] = ga
        gattn = ga.astype(jnp.bfloat16).astype(jnp.float32)
        return tuple(s + jnp.sum(v, axis=0, keepdims=True)
                     for s, v in zip(sums, (g * xhat, g, gmf, gattn)))

    def half(h):
        return pltpu.make_async_copy(fin.at[pl.ds(h * 512, 512), :], gafter_hbm.at[pl.ds(h * 512, 512), :], lsem.at[h])

    zero = jnp.zeros((1, D), jnp.float32)
    sums = lax.fori_loop(0, D // 256, norm_step, (zero,) * 4)
    half(0).start()
    sums = lax.fori_loop(D // 256, D // 128, norm_step, sums)
    half(1).start()
    for i in range(4):
        small_ref[i:i + 1, :] = sums[i]
    half(0).wait()
    half(1).wait()


def mlp(comm, after, cot, mask, vecs, fcb, wfc, wdn):
    n = FF // CH
    any_ = pl.BlockSpec(memory_space=pl.ANY)
    vmem = pl.BlockSpec(memory_space=pltpu.VMEM)
    return pl.pallas_call(
        functools.partial(mlp_kernel, comm),
        out_shape=[jax.ShapeDtypeStruct((D, D), jnp.bfloat16), jax.ShapeDtypeStruct((D, D), jnp.float32),
                   jax.ShapeDtypeStruct((FF, D), jnp.bfloat16), jax.ShapeDtypeStruct((32, FF), jnp.float32),
                   jax.ShapeDtypeStruct((8, D), jnp.float32), jax.ShapeDtypeStruct((1, FF), jnp.float32)],
        in_specs=[any_, any_, vmem, vmem, vmem, any_, any_],
        out_specs=[vmem, any_, any_, vmem, vmem, vmem],
        scratch_shapes=[pltpu.VMEM((D, D), jnp.float32), pltpu.VMEM((D, D), jnp.bfloat16),
                        pltpu.VMEM((D, D), jnp.bfloat16), pltpu.VMEM((D, D), jnp.bfloat16),
                        pltpu.VMEM((D, FF), jnp.bfloat16), pltpu.VMEM((D, CH), jnp.bfloat16),
                        pltpu.VMEM((D, D), jnp.float32), pltpu.VMEM((D, D), jnp.float32),
                        pltpu.VMEM((2, D, CH), jnp.bfloat16), pltpu.VMEM((2, CH, D), jnp.bfloat16),
                        pltpu.VMEM((2, CH, D), jnp.bfloat16),
                        pltpu.VMEM((n, 2, 2, 4, 2, 32, CH), jnp.bfloat16),
                        pltpu.SemaphoreType.DMA((2,)), pltpu.SemaphoreType.DMA((2, 2)), pltpu.SemaphoreType.DMA((2,))]
        + (scatter_bufs(n, 32, CH) if comm else []),
        compiler_params=pltpu.CompilerParams(vmem_limit_bytes=60 << 20,
            **(dict(collective_id=2, has_side_effects=True) if comm else {})),
    )(after, cot, mask, vecs, fcb, wfc, wdn)


HEADS = 16
BLOCK = 128


def layer_norm(rows_in, gain_vec, shift_vec):
    row_mean = jnp.mean(rows_in, axis=-1, keepdims=True)
    centered = rows_in - row_mean
    row_var = jnp.mean(centered * centered, axis=-1, keepdims=True)
    return centered * lax.rsqrt(row_var + 1e-05) * gain_vec + shift_vec


def outer_sum(first, second):
    return lax.dot_general(
        first, second, (((0,), (0,)), ((), ())), preferred_element_type=jnp.float32
    )


def times_transposed(first, second):
    return lax.dot_general(
        first, second, (((1,), (1,)), ((), ())), preferred_element_type=jnp.float32
    )


def masked_scores(queries_h, keys_h):
    scores = (
        jnp.einsum("bqhd,bkhd->bhqk", queries_h, keys_h, preferred_element_type=jnp.float32) * 0.125
    )
    causal = lax.broadcasted_iota(jnp.int32, scores.shape, 2) >= lax.broadcasted_iota(
        jnp.int32, scores.shape, 3
    )
    return jnp.where(causal, scores, -1e30)


def plain_body(
    tokens,
    condition,
    valid_mask,
    w_qkv,
    w_out,
    w_fc,
    w_down,
    norm_gains,
    biases,
    fc_bias,
    cotangent,
):
    window_count, span_rows, model_width = tokens.shape
    row_total = window_count * span_rows
    head_size = model_width // HEADS
    head_shape = (row_total // BLOCK, BLOCK, HEADS, head_size)
    keep_rows = valid_mask.reshape(row_total, 1).astype(jnp.float32)
    hidden = tokens.reshape(row_total, model_width).astype(jnp.float32) + condition.reshape(
        row_total, model_width
    ).astype(jnp.float32)
    full_qkv, full_out, full_gains, full_biases = (
        lax.all_gather(w_qkv, ("win", "seq"), axis=0, tiled=True),
        lax.all_gather(w_out, ("win", "seq"), axis=0, tiled=True),
        lax.all_gather(norm_gains, ("win", "seq"), axis=1, tiled=True),
        lax.all_gather(biases, ("win", "seq"), axis=1, tiled=True),
    )
    gain_f = full_gains.astype(jnp.float32)
    bias_f = full_biases.astype(jnp.float32)
    normed_f, norm_back_one = jax.vjp(layer_norm, hidden, gain_f[0], bias_f[0])
    normed = normed_f.astype(jnp.bfloat16)
    projected = jnp.dot(normed, full_qkv, preferred_element_type=jnp.float32)
    queries = (projected[:, :model_width] + bias_f[1]).astype(jnp.bfloat16).reshape(head_shape)
    key_rows = projected[:, model_width : 2 * model_width].astype(jnp.bfloat16).reshape(head_shape)
    values = (projected[:, 2 * model_width :] + bias_f[2]).astype(jnp.bfloat16).reshape(head_shape)
    scores = masked_scores(queries, key_rows)
    row_max = jnp.max(scores, axis=-1, keepdims=True)
    log_total = row_max + jnp.log(jnp.sum(jnp.exp(scores - row_max), axis=-1, keepdims=True))
    probs = jnp.exp(scores - log_total).astype(jnp.bfloat16)
    mixed = jnp.einsum("bhqk,bkhd->bqhd", probs, values, preferred_element_type=jnp.float32)
    mixed = mixed.reshape(row_total, model_width).astype(jnp.bfloat16)
    after_attn = hidden + jnp.dot(mixed, full_out, preferred_element_type=jnp.float32) + bias_f[3]
    full_fc, full_down, full_fc_bias = (
        lax.all_gather(w_fc, ("win", "seq"), axis=0, tiled=True),
        lax.all_gather(w_down, ("win", "seq"), axis=0, tiled=True),
        lax.all_gather(fc_bias, ("win", "seq"), axis=0, tiled=True),
    )
    normed_two_f, norm_back_two = jax.vjp(layer_norm, after_attn, gain_f[1], bias_f[4])
    normed_two = normed_two_f.astype(jnp.bfloat16)
    pre_gelu = jnp.dot(
        normed_two, full_fc, preferred_element_type=jnp.float32
    ) + full_fc_bias.astype(jnp.float32)
    gelu_f, gelu_back = jax.vjp(partial(jax.nn.gelu, approximate=False), pre_gelu)
    gelu_out = gelu_f.astype(jnp.bfloat16)
    final_rows = (
        after_attn + jnp.dot(gelu_out, full_down, preferred_element_type=jnp.float32) + bias_f[5]
    )
    output = (final_rows * keep_rows).astype(jnp.bfloat16).reshape(tokens.shape)
    back_fc, back_down = (
        lax.all_gather(w_fc, ("win", "seq"), axis=0, tiled=True),
        lax.all_gather(w_down, ("win", "seq"), axis=0, tiled=True),
    )
    grad_final = cotangent.reshape(row_total, model_width).astype(jnp.float32) * keep_rows
    grad_mlp = grad_final.astype(jnp.bfloat16)
    grad_down_local = outer_sum(gelu_out, grad_mlp)
    grad_down_bias = jnp.sum(grad_mlp.astype(jnp.float32), axis=0)
    grad_gelu = times_transposed(grad_mlp, back_down)
    grad_pre = gelu_back(grad_gelu)[0].astype(jnp.bfloat16)
    grad_fc_local = outer_sum(normed_two, grad_pre)
    grad_fc_bias_local = jnp.sum(grad_pre.astype(jnp.float32), axis=0)
    grad_w_fc, grad_w_down, grad_fc_bias = (
        lax.psum_scatter(grad_fc_local, ("win", "seq"), scatter_dimension=0, tiled=True),
        lax.psum_scatter(grad_down_local, ("win", "seq"), scatter_dimension=0, tiled=True),
        lax.psum_scatter(grad_fc_bias_local, ("win", "seq"), scatter_dimension=0, tiled=True),
    )
    grad_normed_two = times_transposed(grad_pre, back_fc)
    grad_after_norm, grad_gain_two, grad_shift_two = norm_back_two(grad_normed_two)
    grad_after = grad_final + grad_after_norm
    back_qkv, back_out = (
        lax.all_gather(w_qkv, ("win", "seq"), axis=0, tiled=True),
        lax.all_gather(w_out, ("win", "seq"), axis=0, tiled=True),
    )
    grad_attn = grad_after.astype(jnp.bfloat16)
    grad_out_local = outer_sum(mixed, grad_attn)
    grad_out_bias = jnp.sum(grad_attn.astype(jnp.float32), axis=0)
    grad_mixed = times_transposed(grad_attn, back_out).astype(jnp.bfloat16).reshape(head_shape)
    probs_full = jnp.exp(masked_scores(queries, key_rows) - log_total)
    grad_probs = jnp.einsum(
        "bqhd,bkhd->bhqk", grad_mixed, values, preferred_element_type=jnp.float32
    )
    grad_values = jnp.einsum(
        "bhqk,bqhd->bkhd", probs, grad_mixed, preferred_element_type=jnp.float32
    )
    grad_values = grad_values.reshape(row_total, model_width).astype(jnp.bfloat16)
    grad_scores = probs_full * (
        grad_probs - jnp.sum(probs_full * grad_probs, axis=-1, keepdims=True)
    )
    grad_scores = grad_scores.astype(jnp.bfloat16)
    grad_queries = (
        jnp.einsum("bhqk,bkhd->bqhd", grad_scores, key_rows, preferred_element_type=jnp.float32)
        * 0.125
    )
    grad_keys = (
        jnp.einsum("bhqk,bqhd->bkhd", grad_scores, queries, preferred_element_type=jnp.float32)
        * 0.125
    )
    grad_queries = grad_queries.reshape(row_total, model_width).astype(jnp.bfloat16)
    grad_keys = grad_keys.reshape(row_total, model_width).astype(jnp.bfloat16)
    grad_query_bias = jnp.sum(grad_queries.astype(jnp.float32), axis=0)
    grad_value_bias = jnp.sum(grad_values.astype(jnp.float32), axis=0)
    grad_projected = jnp.concatenate([grad_queries, grad_keys, grad_values], axis=1)
    grad_qkv_local = outer_sum(normed, grad_projected)
    grad_normed = times_transposed(grad_projected, back_qkv)
    grad_hidden_norm, grad_gain_one, grad_shift_one = norm_back_one(grad_normed)
    grad_input = (grad_after + grad_hidden_norm).astype(jnp.bfloat16).reshape(tokens.shape)
    gains_local = jnp.stack([grad_gain_one, grad_gain_two])
    biases_local = jnp.stack(
        [
            grad_shift_one,
            grad_query_bias,
            grad_value_bias,
            grad_out_bias,
            grad_shift_two,
            grad_down_bias,
        ]
    )
    grad_w_qkv, grad_w_out, grad_gains, grad_biases = (
        lax.psum_scatter(grad_qkv_local, ("win", "seq"), scatter_dimension=0, tiled=True),
        lax.psum_scatter(grad_out_local, ("win", "seq"), scatter_dimension=0, tiled=True),
        lax.psum_scatter(gains_local, ("win", "seq"), scatter_dimension=1, tiled=True),
        lax.psum_scatter(biases_local, ("win", "seq"), scatter_dimension=1, tiled=True),
    )
    return (
        output,
        grad_input,
        grad_w_qkv,
        grad_w_out,
        grad_w_fc,
        grad_w_down,
        grad_gains,
        grad_biases,
        grad_fc_bias,
    )


GATHER_ORDER = (2, 0, 2, 2, 1, 2)


def pack_small(gains, biases, fc_bias, rows, dtype):
    devices = fc_bias.shape[0] // 128
    eight = jnp.concatenate([gains, biases], axis=0)
    eight = eight.reshape(8, devices, 32).transpose(1, 0, 2).reshape(devices, 2, 128)
    packed = jnp.concatenate([eight, fc_bias.reshape(devices, 1, 128)], axis=1)
    return jnp.pad(packed, ((0, 0), (0, rows - 3), (0, 0))).astype(dtype)


def unpack_small(packed):
    devices = packed.shape[0]
    eight = packed[:, :2].reshape(devices, 8, 32).transpose(1, 0, 2).reshape(8, devices * 32)
    return eight[:2], eight[2:], packed[:, 2].reshape(devices * 128)


def gather_all(w_qkv, w_out, w_fc, w_down, norm_gains, biases, fc_bias):
    small = pack_small(norm_gains, biases, fc_bias, 16, jnp.bfloat16)[0]
    shards = (small, w_qkv, w_out, w_fc, w_down)
    cuts = [(0, (0, 16), (0, 128))]
    cuts += [(1, (0, 32), (i * 512, 512)) for i in range(6)]
    cuts += [(2, (0, 32), (i * 512, 512)) for i in range(2)]
    cuts += [(3, (0, 32), (i * 512, 512)) for i in range(8)]
    cuts += [(4, (i * 16, 16), (0, 1024)) for i in range(8)]
    count = len(cuts)

    def kernel(*refs):
        ins, fulls, (send, recv, local) = refs[:5], refs[5:10], refs[10:]
        place = Place()
        greet(place)
        own = [
            pltpu.make_async_copy(s, f.at[place.y, place.x, place.z, place.c], local.at[i])
            for i, (s, f) in enumerate(zip(ins, fulls))
        ]
        for c in own:
            c.start()
        for c in own:
            c.wait()

        def make(k):
            n, (r0, r), (c0, w) = cuts[k]
            view = lambda y, x, z, c: fulls[n].at[y, x, z, c, pl.ds(r0, r), pl.ds(c0, w)]
            return Gather(place, view, GATHER_ORDER[k % 6], send.at[k], recv.at[k], 1)

        run_ticks([make(k) for k in range(count)], [(k + 2) // 3 for k in range(count)])

    fulls = pl.pallas_call(
        kernel,
        out_shape=[jax.ShapeDtypeStruct((2, 2, 4, 2) + s.shape, s.dtype) for s in shards],
        in_specs=[pl.BlockSpec(memory_space=pl.ANY)] * 5,
        out_specs=[pl.BlockSpec(memory_space=pl.ANY)] * 5,
        scratch_shapes=[
            pltpu.SemaphoreType.DMA((count, GATHER_SEMS)),
            pltpu.SemaphoreType.DMA((count, GATHER_SEMS)),
            pltpu.SemaphoreType.DMA((5,)),
        ],
        compiler_params=pltpu.CompilerParams(collective_id=0, has_side_effects=True),
    )(*shards)
    mats = [f.reshape(-1, f.shape[-1]) for f in fulls[1:]]
    return (*mats, *unpack_small(fulls[0].reshape(32, 16, 128)))


def scatter_all(g_qkv, g_out, g_down, gains, biases, fc_bias):
    small = pack_small(gains, biases, fc_bias, 8, jnp.float32)
    full = [g.astype(jnp.bfloat16) for g in (g_qkv, g_out, g_down)]
    shapes = [(g.shape[0] // 32, g.shape[1]) for g in full]
    cuts = [
        (n, (r0, 32), (c0, 512))
        for n, (rows, cols) in enumerate(shapes)
        for r0 in range(0, rows, 32)
        for c0 in range(0, cols, 512)
    ]
    count, depth = len(cuts), 16

    def kernel(*refs):
        ins, outs, (slots, own, load_sem), rest = refs[:4], refs[4:8], refs[8:11], refs[11:]
        big, little = rest[:6], rest[6:]
        place = Place()
        greet(place)

        def make(k):
            n, (r0, r), (c0, w) = cuts[k]

            def put(value):
                outs[n + 1][pl.ds(r0, r), pl.ds(c0, w)] = value

            return Scatter(place, slots.at[k % depth], [b.at[k] for b in big[:4]],
                           GATHER_ORDER[k % 6], big[4].at[k], big[5].at[k], put)

        def put_small(value):
            outs[0][...] = value

        def load(k):
            n, (r0, r), (c0, w) = cuts[k]
            return pltpu.make_async_copy(
                ins[n + 1].at[:, :, :, :, pl.ds(r0, r), pl.ds(c0, w)],
                slots.at[k % depth], load_sem.at[k % depth])

        small_load = pltpu.make_async_copy(ins[0], own, load_sem.at[depth])
        small_load.start()
        pieces = [Scatter(place, own, [b.at[0] for b in little[:4]], 2,
                          little[4].at[0], little[5].at[0], put_small)]
        pieces += [make(k) for k in range(count)]
        loads = [small_load] + [load(k) for k in range(count)]
        groups = [[0, 1, 2, 3]] + [list(range(i, min(i + 3, count + 1))) for i in range(4, count + 1, 3)]
        for k in groups[0][1:]:
            loads[k].start()
        for now in range(len(groups) + 4):
            if now + 1 < len(groups):
                for k in groups[now + 1]:
                    loads[k].start()
            for age in range(4, -1, -1):
                if 0 <= now - age < len(groups):
                    for k in groups[now - age]:
                        if age == 0:
                            loads[k].wait()
                        pieces[k].tick(age)
                        if age == 4:
                            pieces[k].finish()

    out = pl.pallas_call(
        kernel,
        out_shape=[jax.ShapeDtypeStruct(s, jnp.float32) for s in [(8, 128)] + shapes],
        in_specs=[pl.BlockSpec(memory_space=pl.ANY)] * 4,
        out_specs=[pl.BlockSpec(memory_space=pltpu.VMEM)] * 4,
        scratch_shapes=[pltpu.VMEM((depth, 2, 2, 4, 2, 32, 512), jnp.bfloat16),
                        pltpu.VMEM((2, 2, 4, 2, 8, 128), jnp.float32),
                        pltpu.SemaphoreType.DMA((depth + 1,))]
        + scatter_bufs(count, 32, 512) + scatter_bufs(1, 8, 128, jnp.float32),
        compiler_params=pltpu.CompilerParams(
            collective_id=1, has_side_effects=True, vmem_limit_bytes=60 << 20),
    )(small.reshape(2, 2, 4, 2, 8, 128),
      *[g.reshape((2, 2, 4, 2) + s) for g, s in zip(full, shapes)])
    return (*out[1:], *unpack_small(out[0][None]))


def body(
    tokens,
    condition,
    valid_mask,
    w_qkv,
    w_out,
    w_fc,
    w_down,
    norm_gains,
    biases,
    fc_bias,
    cotangent,
):
    window_count, span_rows, model_width = tokens.shape
    row_total = window_count * span_rows
    head_size = model_width // HEADS
    head_shape = (row_total // BLOCK, BLOCK, HEADS, head_size)
    keep_rows = valid_mask.reshape(row_total, 1).astype(jnp.float32)
    hidden = tokens.reshape(row_total, model_width).astype(jnp.float32) + condition.reshape(
        row_total, model_width
    ).astype(jnp.float32)
    full_qkv, full_out, full_fc, full_down, full_gains, full_biases, full_fc_bias = gather_all(
        w_qkv, w_out, w_fc, w_down, norm_gains, biases, fc_bias
    )
    gain_f = full_gains.astype(jnp.float32)
    bias_f = full_biases.astype(jnp.float32)
    normed_f, norm_back_one = jax.vjp(layer_norm, hidden, gain_f[0], bias_f[0])
    normed = normed_f.astype(jnp.bfloat16)
    projected = jnp.dot(normed, full_qkv, preferred_element_type=jnp.float32)
    queries = (projected[:, :model_width] + bias_f[1]).astype(jnp.bfloat16).reshape(head_shape)
    key_rows = projected[:, model_width : 2 * model_width].astype(jnp.bfloat16).reshape(head_shape)
    values = (projected[:, 2 * model_width :] + bias_f[2]).astype(jnp.bfloat16).reshape(head_shape)
    scores = masked_scores(queries, key_rows)
    row_max = jnp.max(scores, axis=-1, keepdims=True)
    log_total = row_max + jnp.log(jnp.sum(jnp.exp(scores - row_max), axis=-1, keepdims=True))
    probs = jnp.exp(scores - log_total).astype(jnp.bfloat16)
    mixed = jnp.einsum("bhqk,bkhd->bqhd", probs, values, preferred_element_type=jnp.float32)
    mixed = mixed.reshape(row_total, model_width).astype(jnp.bfloat16)
    after_attn = hidden + jnp.dot(mixed, full_out, preferred_element_type=jnp.float32) + bias_f[3]
    vecs = jnp.concatenate([gain_f, bias_f], axis=0)
    output, grad_after, grad_down_local, grad_w_fc, two_sums, grad_fc_bias_local = mlp(
        True,
        after_attn,
        cotangent.reshape(row_total, model_width),
        keep_rows,
        vecs,
        full_fc_bias.astype(jnp.float32).reshape(1, -1),
        full_fc,
        full_down,
    )
    output = output.reshape(tokens.shape)
    grad_fc_bias_local = grad_fc_bias_local.reshape(-1)
    back_qkv, back_out = full_qkv, full_out
    grad_attn = grad_after.astype(jnp.bfloat16)
    grad_out_local = outer_sum(mixed, grad_attn)
    grad_mixed = times_transposed(grad_attn, back_out).astype(jnp.bfloat16).reshape(head_shape)
    probs_full = jnp.exp(masked_scores(queries, key_rows) - log_total)
    grad_probs = jnp.einsum(
        "bqhd,bkhd->bhqk", grad_mixed, values, preferred_element_type=jnp.float32
    )
    grad_values = jnp.einsum(
        "bhqk,bqhd->bkhd", probs, grad_mixed, preferred_element_type=jnp.float32
    )
    grad_values = grad_values.reshape(row_total, model_width).astype(jnp.bfloat16)
    grad_scores = probs_full * (
        grad_probs - jnp.sum(probs_full * grad_probs, axis=-1, keepdims=True)
    )
    grad_scores = grad_scores.astype(jnp.bfloat16)
    grad_queries = (
        jnp.einsum("bhqk,bkhd->bqhd", grad_scores, key_rows, preferred_element_type=jnp.float32)
        * 0.125
    )
    grad_keys = (
        jnp.einsum("bhqk,bqhd->bkhd", grad_scores, queries, preferred_element_type=jnp.float32)
        * 0.125
    )
    grad_queries = grad_queries.reshape(row_total, model_width).astype(jnp.bfloat16)
    grad_keys = grad_keys.reshape(row_total, model_width).astype(jnp.bfloat16)
    grad_query_bias = jnp.sum(grad_queries.astype(jnp.float32), axis=0)
    grad_value_bias = jnp.sum(grad_values.astype(jnp.float32), axis=0)
    grad_projected = jnp.concatenate([grad_queries, grad_keys, grad_values], axis=1)
    grad_qkv_local = outer_sum(normed, grad_projected)
    grad_normed = times_transposed(grad_projected, back_qkv)
    grad_hidden_norm, grad_gain_one, grad_shift_one = norm_back_one(grad_normed)
    grad_input = (grad_after + grad_hidden_norm).astype(jnp.bfloat16).reshape(tokens.shape)
    gains_local = jnp.stack([grad_gain_one, two_sums[0]])
    biases_local = jnp.stack(
        [
            grad_shift_one,
            grad_query_bias,
            grad_value_bias,
            two_sums[3],
            two_sums[1],
            two_sums[2],
        ]
    )
    grad_w_qkv, grad_w_out, grad_w_down, grad_gains, grad_biases, grad_fc_bias = scatter_all(
        grad_qkv_local, grad_out_local, grad_down_local,
        gains_local, biases_local, grad_fc_bias_local,
    )
    return (
        output,
        grad_input,
        grad_w_qkv,
        grad_w_out,
        grad_w_fc,
        grad_w_down,
        grad_gains,
        grad_biases,
        grad_fc_bias,
    )


def solution(mesh):
    fast = mesh.shape["win"] == 4 and mesh.shape["seq"] == 8
    return jax.shard_map(
        body if fast else plain_body,
        mesh=mesh,
        in_specs=(
            P("win", "seq", None),
            P("win", "seq", None),
            P("win", "seq"),
            P(("win", "seq"), None),
            P(("win", "seq"), None),
            P(("win", "seq"), None),
            P(("win", "seq"), None),
            P(None, ("win", "seq")),
            P(None, ("win", "seq")),
            P(("win", "seq")),
            P("win", "seq", None),
        ),
        out_specs=(
            P("win", "seq", None),
            P("win", "seq", None),
            P(("win", "seq"), None),
            P(("win", "seq"), None),
            P(("win", "seq"), None),
            P(("win", "seq"), None),
            P(None, ("win", "seq")),
            P(None, ("win", "seq")),
            P(("win", "seq")),
        ),
        check_vma=False,
    )
```

```python
import functools
from functools import partial

import jax
import jax.numpy as jnp
from jax import lax
from jax.experimental import pallas as pl
from jax.experimental.pallas import tpu as pltpu
from jax.sharding import PartitionSpec as P

MESH = pl.DeviceIdType.MESH
ALL = slice(None)


class Place:
    def __init__(self):
        win, seq = lax.axis_index("win"), lax.axis_index("seq")
        self.y, self.x = win // 2, win % 2
        self.z, self.c = seq // 2, seq % 2

    def device(self, y=None, x=None, z=None, c=None):
        y = self.y if y is None else y
        x = self.x if x is None else x
        z = self.z if z is None else z
        c = self.c if c is None else c
        return (y * 2 + x, z * 2 + c)

    def partner(self, dim):
        if dim == "x":
            return self.device(x=1 - self.x)
        if dim == "y":
            return self.device(y=1 - self.y)
        return self.device(c=1 - self.c)


def greet(place):
    barrier = pltpu.get_barrier_semaphore()
    others = [place.partner(dim) for dim in "xyc"]
    others += [place.device(z=(place.z + t) % 4) for t in (1, 2, 3)]
    for device in others:
        pl.semaphore_signal(barrier, inc=1, device_id=device, device_id_type=MESH)
    pl.semaphore_wait(barrier, 6)


def guarded(cond, thunk):
    if cond is None:
        thunk()
    else:
        pl.when(cond)(thunk)


class Gather:
    def __init__(self, place, view, order, send, recv, slack=0):
        self.p, self.view, self.send, self.recv = place, view, send, recv
        self.order, self.sent = order, []
        self.ticks = self.plan(slack)

    def region(self, got, **at):
        p = self.p
        pick = lambda d, own: at[d] if d in at else (ALL if d in got else own)
        return self.view(pick("y", p.y), pick("x", p.x), pick("z", p.z), at.get("c", p.c))

    def copy(self, region, device, number):
        return pltpu.make_async_remote_copy(
            region, region, self.send.at[number], self.recv.at[number],
            device_id=device, device_id_type=MESH)

    def push(self, cond, make, device, number):
        def go():
            self.copy(make(), device, number).start()
        guarded(cond, go)

        def end():
            self.copy(make(), device, number).wait_send()
        self.sent.append((cond, end))

    def take(self, cond, make, number):
        def go():
            self.copy(make(), self.p.device(c=1 - self.p.c), number).wait_recv()
        guarded(cond, go)

    def both(self, cond, other):
        return other if cond is None else jnp.logical_and(cond, other)

    def line_push(self, got, cond):
        for t in (1, 2, 3):
            self.push(cond, lambda: self.region(got), self.p.device(z=(self.p.z + t) % 4), 1 + t)

    def line_take(self, got, cond):
        for t in (1, 2, 3):
            self.take(cond, lambda t=t: self.region(got, z=(self.p.z + 4 - t) % 4), 1 + t)

    def plan(self, slack):
        out = []
        p = self.p
        orders = {0: (("xzy", None),), 1: (("yzx", None),),
                  2: (("zxy", p.c == 0), ("zyx", p.c == 1))}[self.order]
        lists = []
        for order, cond in orders:
            ticks = [[]]
            got = ""
            ex = 0
            for dim in order:
                if dim == "z":
                    ticks[-1].append(functools.partial(self.line_push, got, cond))
                    ticks.append([])
                    ticks[-1].append(functools.partial(self.line_take, got, cond))
                else:
                    ticks[-1].append(functools.partial(
                        self.push, cond, functools.partial(self.region, got), p.partner(dim), ex))
                    if ex == 1:
                        ticks.extend([] for _ in range(slack))
                    ticks.append([])
                    own = p.x if dim == "x" else p.y
                    ticks[-1].append(functools.partial(
                        self.take, cond, functools.partial(self.region, got, **{dim: 1 - own}), ex))
                    ex += 1
                got += dim
            ticks[-1].append(functools.partial(self.push, cond, functools.partial(self.region, "xyz"),
                                               p.partner("c"), 8))
            ticks.append([])
            ticks[-1].append(functools.partial(self.take, cond,
                                               functools.partial(self.region, "xyz", c=1 - p.c), 8))
            lists.append(ticks)
        n = max(len(t) for t in lists)
        for i in range(n):
            thunks = [f for t in lists if i < len(t) for f in t[i]]
            out.append(thunks)
        return out

    def tick(self, i):
        for f in self.ticks[i]:
            f()

    def finish(self):
        for cond, end in self.sent:
            guarded(cond, end)


def run_ticks(pieces, starts, between=None):
    last = max(s + len(p.ticks) for p, s in zip(pieces, starts))
    for now in range(last):
        for p, s in zip(pieces, starts):
            if 0 <= now - s < len(p.ticks):
                p.tick(now - s)
        if between and now in between:
            between[now]()
    for p in pieces:
        p.finish()


class Scatter:
    def __init__(self, place, slot, bufs, order, send, recv, put):
        self.p, self.slot, self.bufs, self.put = place, slot, bufs, put
        self.send, self.recv, self.sent = send, recv, []
        self.ticks = self.plan(order)

    def region(self, left, **at):
        p = self.p
        pick = lambda d, own: at[d] if d in at else (ALL if d in left else own)
        return self.slot.at[pick("y", p.y), pick("x", p.x), pick("z", p.z), at.get("c", p.c)]

    def push(self, cond, make, buf, device, number):
        def copy():
            return pltpu.make_async_remote_copy(
                make(), buf, self.send.at[number], self.recv.at[number],
                device_id=device, device_id_type=MESH)
        guarded(cond, lambda: copy().start())
        self.sent.append((cond, lambda: copy().wait_send()))

    def take(self, cond, makes, bufs, numbers, last):
        def go():
            for buf, number in zip(bufs, numbers):
                pltpu.make_async_remote_copy(
                    buf, buf, self.send.at[number], self.recv.at[number],
                    device_id=self.p.partner("c"), device_id_type=MESH).wait_recv()
            region = makes()
            shape = region.shape
            outer = [()]
            while len(shape) - len(outer[0]) > 3:
                outer = [o + (i,) for o in outer for i in range(shape[len(o)])]
            for o in outer:
                many = last or len(bufs) > 1
                total = region[o + (Ellipsis,)]
                total = total.astype(jnp.float32) if many else total
                for buf in bufs:
                    total = total + buf[o + (Ellipsis,)].astype(total.dtype)
                if last:
                    self.put(total)
                else:
                    region[o + (Ellipsis,)] = total.astype(region.dtype)
        guarded(cond, go)

    def plan(self, order):
        p = self.p
        core, first, second, line = self.bufs
        variants = {0: (("yzx", None),), 1: (("xzy", None),),
                    2: (("yxz", p.c == 0), ("xyz", p.c == 1))}[order]
        ticks = [[] for _ in range(5)]
        for dims, cond in variants:
            left = "xyz"
            ticks[0].append(functools.partial(
                self.push, cond, lambda: self.region("xyz", c=1 - p.c), core, p.partner("c"), 0))
            ticks[1].append(functools.partial(
                self.take, cond, lambda: self.region("xyz"), [core], [0], False))
            for i, dim in enumerate(dims):
                rest = left.replace(dim, "")
                last = i == 2
                mine = functools.partial(self.region, rest)
                if dim == "z":
                    bufs = [line.at[t - 1] if rest else line.at[t - 1, 0] for t in (1, 2, 3)]
                    for t in (1, 2, 3):
                        to = (p.z + t) % 4
                        ticks[i + 1].append(functools.partial(
                            self.push, cond, functools.partial(self.region, rest, z=to),
                            bufs[t - 1], p.device(z=to), 2 + t))
                    ticks[i + 2].append(functools.partial(
                        self.take, cond, mine, bufs, [3, 4, 5], last))
                else:
                    buf = first if i == 0 else (second if i == 1 else second.at[0])
                    number = 1 if i == 0 else 2
                    own = p.x if dim == "x" else p.y
                    ticks[i + 1].append(functools.partial(
                        self.push, cond, functools.partial(self.region, rest, **{dim: 1 - own}),
                        buf, p.partner(dim), number))
                    ticks[i + 2].append(functools.partial(
                        self.take, cond, mine, [buf], [number], last))
                left = rest
        return ticks

    def tick(self, i):
        for f in self.ticks[i]:
            f()

    def finish(self):
        for cond, end in self.sent:
            guarded(cond, end)


SCATTER_SEMS = 6
GATHER_SEMS = 9


def scatter_bufs(count, rows, cols, dtype=jnp.bfloat16):
    return [pltpu.VMEM((count, 2, 2, 4, rows, cols), dtype), pltpu.VMEM((count, 2, 4, rows, cols), dtype),
            pltpu.VMEM((count, 4, rows, cols), dtype), pltpu.VMEM((count, 3, 2, rows, cols), dtype),
            pltpu.SemaphoreType.DMA((count, SCATTER_SEMS)), pltpu.SemaphoreType.DMA((count, SCATTER_SEMS))]


D, FF, CH = 1024, 4096, 512
DELAY = (0, 1, 4, 6, 8)
TILE = 256


def dot_nn(a, b):
    return lax.dot_general(a, b, (((1,), (0,)), ((), ())), preferred_element_type=jnp.float32)


def dot_nt(a, b):
    return lax.dot_general(a, b, (((1,), (1,)), ((), ())), preferred_element_type=jnp.float32)


def dot_tn(a, b):
    return lax.dot_general(a, b, (((0,), (0,)), ((), ())), preferred_element_type=jnp.float32)


def norm_stats(rows_in):
    mean = jnp.mean(rows_in, axis=-1, keepdims=True)
    centered = rows_in - mean
    var = jnp.mean(centered * centered, axis=-1, keepdims=True)
    rstd = lax.rsqrt(var + 1e-05)
    return centered * rstd, rstd


def gelu_both(v):
    phi = 0.5 + 0.5 * lax.erf(v * 0.7071067811865476)
    slope = phi + v * (jnp.exp(-0.5 * v * v) * 0.3989422804014327)
    return (v * phi).astype(jnp.bfloat16), slope


def mlp_kernel(comm, after_hbm, cot_hbm, mask_ref, vec_ref, fcb_ref, wfc_hbm, wdn_hbm,
               out_ref, gafter_hbm, gdown_hbm, gfc_ref, small_ref, gfcb_ref,
               after, gm, n2, n2t, gelu, gp, fin, gn2, wfc, wdn, stage, slots, lsem, wsem, ssem, *rest):
    place = Place()
    if comm:
        greet(place)
    load_after = pltpu.make_async_copy(after_hbm, after, lsem.at[0])
    load_cot = pltpu.make_async_copy(cot_hbm, gm, lsem.at[1])
    load_after.start()
    load_cot.start()

    def fetch_fc(j):
        return pltpu.make_async_copy(wfc_hbm.at[:, pl.ds(j * CH, CH)], wfc.at[j % 2], wsem.at[j % 2, 0])

    def fetch_down(i):
        j = i % (FF // CH)
        return pltpu.make_async_copy(wdn_hbm.at[pl.ds(j * CH, CH), :], wdn.at[i % 2], wsem.at[i % 2, 1])

    fetch_fc(0).start()
    fetch_down(0).start()
    load_after.wait()
    load_cot.wait()

    @pl.loop(0, D // 128)
    def _(i):
        rows = pl.ds(pl.multiple_of(i * 128, 128), 128)
        xhat, _ = norm_stats(after[rows, :])
        v = (xhat * vec_ref[1:2, :] + vec_ref[6:7, :]).astype(jnp.bfloat16)
        n2[rows, :] = v
        n2t[:, rows] = v.T
        g = gm[rows, :].astype(jnp.float32) * mask_ref[rows, :]
        gm[rows, :] = g.astype(jnp.bfloat16)
        fin[rows, :] = jnp.zeros((128, D), jnp.float32)
        gn2[rows, :] = jnp.zeros((128, D), jnp.float32)

    n = FF // CH

    def store(j):
        return pltpu.make_async_copy(stage.at[j % 2], gdown_hbm.at[pl.ds(j * CH, CH), :], ssem.at[j % 2])

    pieces = []
    if comm:
        bufs = rest
        for j in range(n):
            def put(value, j=j):
                gfc_ref[:, pl.ds(j * CH, CH)] = value

            pieces.append(Scatter(place, slots.at[j], [b.at[j] for b in bufs[:4]],
                                  GATHER_ORDER[j % 6], bufs[4].at[j], bufs[5].at[j], put))

    def advance(step, first, last):
        if comm:
            for now in range(first, last):
                @pl.when(step == now)
                def _(now=now):
                    for stage_no in (4, 3, 2, 1, 0):
                        j = now - DELAY[stage_no]
                        if 0 <= j < n:
                            pieces[j].tick(stage_no)
                            if stage_no == 4:
                                pieces[j].finish()

    @pl.loop(0, n)
    def _(j):
        s = j % 2
        fetch_fc(j).wait()
        fetch_down(j).wait()
        fetch_down(j + 1).start()

        @pl.when(j + 1 < n)
        def _():
            fetch_fc(j + 1).start()

        cols = pl.ds(pl.multiple_of(j * CH, CH), CH)
        pre = dot_nn(n2[...], wfc[s]) + fcb_ref[:, cols]
        act, slope = gelu_both(pre)
        grad = (dot_nt(gm[...], wdn[s]) * slope).astype(jnp.bfloat16)
        gelu[:, cols] = act
        gp[...] = grad
        gfcb_ref[:, cols] = jnp.sum(grad.astype(jnp.float32), axis=0, keepdims=True)
        gn2[...] += dot_nt(gp[...], wfc[s])
        slots[j] = dot_nn(n2t[...], gp[...]).astype(jnp.bfloat16).reshape(2, 2, 4, 2, 32, CH)
        advance(j, 0, n)

    @pl.loop(0, n)
    def _(j):
        s = j % 2
        fetch_down(j + n).wait()

        @pl.when(j + 1 < n)
        def _():
            fetch_down(j + n + 1).start()

        @pl.when(j >= 2)
        def _():
            store(j - 2).wait()

        cols = pl.ds(pl.multiple_of(j * CH, CH), CH)
        fin[...] += dot_nn(gelu[:, cols], wdn[s])
        stage[s] = dot_tn(gelu[:, cols], gm[...]).astype(jnp.bfloat16)
        store(j).start()
        advance(j + n, n, 2 * n)

    store(n - 2).wait()
    store(n - 1).wait()

    def norm_step(i, sums):
        rows = pl.ds(pl.multiple_of(i * 128, 128), 128)
        xhat, rstd = norm_stats(after[rows, :])
        keep = mask_ref[rows, :]
        out_ref[rows, :] = ((after[rows, :] + fin[rows, :] + vec_ref[7:8, :]) * keep).astype(jnp.bfloat16)
        g = gn2[rows, :]
        y = g * vec_ref[1:2, :]
        m1 = jnp.mean(y, axis=-1, keepdims=True)
        m2 = jnp.mean(y * xhat, axis=-1, keepdims=True)
        gmf = gm[rows, :].astype(jnp.float32)
        ga = gmf + rstd * (y - m1 - xhat * m2)
        fin[rows, :] = ga
        gattn = ga.astype(jnp.bfloat16).astype(jnp.float32)
        return tuple(s + jnp.sum(v, axis=0, keepdims=True)
                     for s, v in zip(sums, (g * xhat, g, gmf, gattn)))

    def half(h):
        return pltpu.make_async_copy(fin.at[pl.ds(h * 512, 512), :], gafter_hbm.at[pl.ds(h * 512, 512), :], lsem.at[h])

    zero = jnp.zeros((1, D), jnp.float32)
    sums = lax.fori_loop(0, D // 256, norm_step, (zero,) * 4)
    half(0).start()
    sums = lax.fori_loop(D // 256, D // 128, norm_step, sums)
    half(1).start()
    for i in range(4):
        small_ref[i:i + 1, :] = sums[i]
    half(0).wait()
    half(1).wait()


def mlp(comm, after, cot, mask, vecs, fcb, wfc, wdn):
    n = FF // CH
    any_ = pl.BlockSpec(memory_space=pl.ANY)
    vmem = pl.BlockSpec(memory_space=pltpu.VMEM)
    return pl.pallas_call(
        functools.partial(mlp_kernel, comm),
        out_shape=[jax.ShapeDtypeStruct((D, D), jnp.bfloat16), jax.ShapeDtypeStruct((D, D), jnp.float32),
                   jax.ShapeDtypeStruct((FF, D), jnp.bfloat16), jax.ShapeDtypeStruct((32, FF), jnp.float32),
                   jax.ShapeDtypeStruct((8, D), jnp.float32), jax.ShapeDtypeStruct((1, FF), jnp.float32)],
        in_specs=[any_, any_, vmem, vmem, vmem, any_, any_],
        out_specs=[vmem, any_, any_, vmem, vmem, vmem],
        scratch_shapes=[pltpu.VMEM((D, D), jnp.float32), pltpu.VMEM((D, D), jnp.bfloat16),
                        pltpu.VMEM((D, D), jnp.bfloat16), pltpu.VMEM((D, D), jnp.bfloat16),
                        pltpu.VMEM((D, FF), jnp.bfloat16), pltpu.VMEM((D, CH), jnp.bfloat16),
                        pltpu.VMEM((D, D), jnp.float32), pltpu.VMEM((D, D), jnp.float32),
                        pltpu.VMEM((2, D, CH), jnp.bfloat16), pltpu.VMEM((2, CH, D), jnp.bfloat16),
                        pltpu.VMEM((2, CH, D), jnp.bfloat16),
                        pltpu.VMEM((n, 2, 2, 4, 2, 32, CH), jnp.bfloat16),
                        pltpu.SemaphoreType.DMA((2,)), pltpu.SemaphoreType.DMA((2, 2)), pltpu.SemaphoreType.DMA((2,))]
        + (scatter_bufs(n, 32, CH) if comm else []),
        compiler_params=pltpu.CompilerParams(vmem_limit_bytes=60 << 20,
            **(dict(collective_id=2, has_side_effects=True) if comm else {})),
    )(after, cot, mask, vecs, fcb, wfc, wdn)


HEADS = 16
BLOCK = 128


def layer_norm(rows_in, gain_vec, shift_vec):
    row_mean = jnp.mean(rows_in, axis=-1, keepdims=True)
    centered = rows_in - row_mean
    row_var = jnp.mean(centered * centered, axis=-1, keepdims=True)
    return centered * lax.rsqrt(row_var + 1e-05) * gain_vec + shift_vec


def outer_sum(first, second):
    return lax.dot_general(
        first, second, (((0,), (0,)), ((), ())), preferred_element_type=jnp.float32
    )


def times_transposed(first, second):
    return lax.dot_general(
        first, second, (((1,), (1,)), ((), ())), preferred_element_type=jnp.float32
    )


def masked_scores(queries_h, keys_h):
    scores = (
        jnp.einsum("bqhd,bkhd->bhqk", queries_h, keys_h, preferred_element_type=jnp.float32) * 0.125
    )
    causal = lax.broadcasted_iota(jnp.int32, scores.shape, 2) >= lax.broadcasted_iota(
        jnp.int32, scores.shape, 3
    )
    return jnp.where(causal, scores, -1e30)


def lane_low(shape):
    return lax.broadcasted_iota(jnp.int32, shape, len(shape) - 1) < 64


def stack_heads(pair):
    low = lane_low(pair.shape)
    zero = jnp.zeros_like(pair)
    return jnp.concatenate([jnp.where(low, pair, zero), jnp.where(low, zero, pair)], axis=0)


def merge_heads(stacked):
    half = stacked.shape[0] // 2
    return jnp.where(lane_low((half, stacked.shape[1])), stacked[:half], stacked[half:])


def softmax_pair(query2, key2):
    scores = dot_nt(query2, key2) * 0.125
    row = lax.broadcasted_iota(jnp.int32, scores.shape, 0) % BLOCK
    col = lax.broadcasted_iota(jnp.int32, scores.shape, 1)
    scores = jnp.where(row >= col, scores, -1e30)
    top = jnp.max(scores, axis=-1, keepdims=True)
    raised = jnp.exp(scores - top)
    return raised * (1.0 / jnp.sum(raised, axis=-1, keepdims=True))


GATHER_CUTS = ([(0, (0, 16), (0, 128))]
               + [(1, (0, 32), (i * 512, 512)) for i in range(6)]
               + [(2, (0, 32), (i * 512, 512)) for i in range(2)]
               + [(3, (0, 32), (i * 512, 512)) for i in range(8)]
               + [(4, (i * 16, 16), (0, 1024)) for i in range(8)])


def gather_kernel(small, wqkv_s, wout_s, wfc_s, wdn_s, tok_hbm, cond_hbm,
                  small_f, wqkv_f, wout_f, wfc_f, wdn_f, qkv_hbm, mixed_hbm, after_hbm, vec_ref, fcb_ref,
                  tok, cond, hidden, normed, wqkv, wout, qkv, mixed, smallv,
                  send, recv, own_sem, lsem, wsem, osem):
    ins = (small, wqkv_s, wout_s, wfc_s, wdn_s)
    fulls = (small_f, wqkv_f, wout_f, wfc_f, wdn_f)
    place = Place()
    greet(place)
    own = [pltpu.make_async_copy(s, f.at[place.y, place.x, place.z, place.c], own_sem.at[i])
           for i, (s, f) in enumerate(zip(ins, fulls))]
    loads = [pltpu.make_async_copy(tok_hbm, tok, lsem.at[0]), pltpu.make_async_copy(cond_hbm, cond, lsem.at[1])]
    for c in own + loads:
        c.start()
    for c in own:
        c.wait()

    def make(k):
        n, (r0, r), (c0, w) = GATHER_CUTS[k]
        view = lambda y, x, z, c: fulls[n].at[y, x, z, c, pl.ds(r0, r), pl.ds(c0, w)]
        return Gather(place, view, GATHER_ORDER[k % 6], send.at[k], recv.at[k], 1)

    load_small = pltpu.make_async_copy(small_f, smallv, lsem.at[2])
    load_qkv = pltpu.make_async_copy(wqkv_f, wqkv, wsem.at[0])
    load_out = pltpu.make_async_copy(wout_f, wout, wsem.at[1])
    store_qkv = pltpu.make_async_copy(qkv, qkv_hbm, osem.at[0])
    store_mixed = pltpu.make_async_copy(mixed, mixed_hbm, osem.at[1])
    store_after = pltpu.make_async_copy(hidden, after_hbm, osem.at[2])

    def add_hidden():
        for c in loads:
            c.wait()

        @pl.loop(0, D // 128)
        def _(i):
            rows = pl.ds(pl.multiple_of(i * 128, 128), 128)
            hidden[rows, :] = tok[rows, :].astype(jnp.float32) + cond[rows, :].astype(jnp.float32)

    def first_norm():
        load_small.start()
        load_small.wait()
        for g in range(8):
            win, z0 = g // 2, (g % 2) * 2
            total = None
            for i in range(4):
                y, x, z, c = win // 2, win % 2, z0 + i // 2, i % 2
                one = smallv[y, x, z, c].astype(jnp.float32)
                device = g * 4 + i
                fcb_ref[:, device * 128:(device + 1) * 128] = one[8:9]
                total = one[:8] if total is None else total + one[:8]
            vec_ref[:, g * 128:(g + 1) * 128] = total

        @pl.loop(0, D // 128)
        def _(i):
            rows = pl.ds(pl.multiple_of(i * 128, 128), 128)
            xhat, _ = norm_stats(hidden[rows, :])
            normed[rows, :] = (xhat * vec_ref[0:1, :] + vec_ref[2:3, :]).astype(jnp.bfloat16)

    def project(first, last):
        for i in range(first, last):
            cols = slice(i * 512, (i + 1) * 512)
            weight = wqkv[:, :, :, :, :, cols].reshape(D, 512)
            part = dot_nn(normed[...], weight)
            if i < 2:
                part = part + vec_ref[3:4, cols]
            if i >= 4:
                part = part + vec_ref[4:5, i * 512 - 2048:i * 512 - 1536]
            qkv[:, cols] = part.astype(jnp.bfloat16)

    def attend(first, last):
        @pl.loop(first, last)
        def _(b):
            rows = pl.ds(pl.multiple_of(b * BLOCK, BLOCK), BLOCK)
            for pair in range(8):
                q2 = stack_heads(qkv[rows, pair * 128:(pair + 1) * 128])
                k2 = qkv[rows, 1024 + pair * 128:1024 + (pair + 1) * 128]
                v2 = qkv[rows, 2048 + pair * 128:2048 + (pair + 1) * 128]
                probs = softmax_pair(q2, k2).astype(jnp.bfloat16)
                mixed[rows, pair * 128:(pair + 1) * 128] = merge_heads(dot_nn(probs, v2)).astype(jnp.bfloat16)

    def output_projection():
        load_out.wait()
        for i in range(2):
            cols = slice(i * 512, (i + 1) * 512)
            part = dot_nn(mixed[...], wout[:, :, :, :, :, cols].reshape(D, 512))
            hidden[:, cols] += part + vec_ref[5:6, cols]
        store_after.start()

    def step8():
        load_qkv.wait()
        project(0, 6)
        store_qkv.start()

    def step7():
        load_qkv.start()

    def step9():
        load_out.start()
        attend(0, 4)

    def step10():
        attend(4, 8)
        store_mixed.start()

    between = {0: add_hidden, 5: first_norm, 7: step7, 8: step8, 9: step9, 10: step10, 11: output_projection}
    run_ticks([make(k) for k in range(len(GATHER_CUTS))], [(k + 2) // 3 for k in range(len(GATHER_CUTS))], between)
    store_qkv.wait()
    store_mixed.wait()
    store_after.wait()


def gather_and_attend(shards, tok, cond):
    any_ = pl.BlockSpec(memory_space=pl.ANY)
    vmem = pl.BlockSpec(memory_space=pltpu.VMEM)
    count = len(GATHER_CUTS)
    bf, f32 = jnp.bfloat16, jnp.float32
    dma = pltpu.SemaphoreType.DMA
    return pl.pallas_call(
        gather_kernel,
        out_shape=[jax.ShapeDtypeStruct((2, 2, 4, 2) + s.shape, s.dtype) for s in shards]
        + [jax.ShapeDtypeStruct((D, 3 * D), bf), jax.ShapeDtypeStruct((D, D), bf), jax.ShapeDtypeStruct((D, D), f32),
           jax.ShapeDtypeStruct((8, D), f32), jax.ShapeDtypeStruct((1, FF), f32)],
        in_specs=[any_] * 7,
        out_specs=[any_] * 8 + [vmem] * 2,
        scratch_shapes=[pltpu.VMEM((D, D), bf), pltpu.VMEM((D, D), bf), pltpu.VMEM((D, D), f32), pltpu.VMEM((D, D), bf),
                        pltpu.VMEM((2, 2, 4, 2, 32, 3 * D), bf), pltpu.VMEM((2, 2, 4, 2, 32, D), bf),
                        pltpu.VMEM((D, 3 * D), bf), pltpu.VMEM((D, D), bf), pltpu.VMEM((2, 2, 4, 2, 16, 128), bf),
                        dma((count, GATHER_SEMS)), dma((count, GATHER_SEMS)), dma((5,)), dma((3,)), dma((2,)), dma((3,))],
        compiler_params=pltpu.CompilerParams(collective_id=0, has_side_effects=True, vmem_limit_bytes=60 << 20),
    )(*shards, tok, cond)


def own_small(gains, biases, fc_bias):
    seq = lax.axis_index("seq")
    eight = jnp.concatenate([gains, biases], axis=0)
    placed = jnp.where(jnp.arange(4)[None, :, None] == seq % 4, eight[:, None, :], 0).reshape(8, 128)
    return jnp.concatenate([placed, fc_bias.reshape(1, 128), jnp.zeros((7, 128), fc_bias.dtype)], axis=0)


DOWN_CUTS = [(r0, c0) for r0 in range(0, 128, 32) for c0 in (0, 512)]
OFFSETS = (0, 1, 3, 4, 6)
DOWN_START = (0, 0, 1, 2, 3, 4, 5, 6)


def backward_kernel(gafter_hbm, qkv_hbm, mixed_hbm, tok_hbm, cond_hbm, wqkv_hbm, wout_hbm, gdown_hbm, vec_ref,
                    sums_ref, fcb_ref,
                    gin_hbm, gqkv_ref, gout_ref, gdown_ref, small_ref,
                    gafter, gattn, mixed, qkv, gqkv, tok, cond, normed, slots, own, lsem, dsem,
                    *rest):
    big, little = rest[:6], rest[6:]
    place = Place()
    greet(place)
    loads = [pltpu.make_async_copy(s, d, lsem.at[i]) for i, (s, d) in enumerate((
        (gafter_hbm, gafter), (mixed_hbm, mixed), (wout_hbm, normed), (tok_hbm, tok), (cond_hbm, cond), (qkv_hbm, qkv)))]
    down_loads = [pltpu.make_async_copy(gdown_hbm.at[:, :, :, :, pl.ds(r0, 32), pl.ds(c0, 512)], slots.at[i], dsem.at[i])
                  for i, (r0, c0) in enumerate(DOWN_CUTS)]
    for c in down_loads[:2] + loads + down_loads[2:]:
        c.start()
    load_wqkv = pltpu.make_async_copy(wqkv_hbm, qkv, lsem.at[6])

    def piece(k, slot, put):
        return Scatter(place, slots.at[slot], [b.at[k] for b in big[:4]], GATHER_ORDER[k % 6],
                       big[4].at[k], big[5].at[k], put)

    def putter(ref, r0, c0):
        def put(value):
            ref[pl.ds(r0, 32), pl.ds(c0, 512)] = value
        return put

    agenda = []
    for i, (r0, c0) in enumerate(DOWN_CUTS):
        agenda.append((piece(i, i, putter(gdown_ref, r0, c0)), [DOWN_START[i] + o for o in OFFSETS]))
    for i in range(2):
        agenda.append((piece(8 + i, 8 + i, putter(gout_ref, 0, i * 512)), [7 + i + o for o in OFFSETS]))
    for i, ready in enumerate((7, 8, 9, 14, 15, 16)):
        col = (i % 3) * 1024 + (i // 3) * 512
        start = ready + (2, 2, 2, 0, 0, 0)[i]
        agenda.append((piece(10 + i, i, putter(gqkv_ref, 0, col)), [start + o for o in LATE[i]]))

    def put_small(value):
        small_ref[...] = value

    agenda.append((Scatter(place, own, [b.at[0] for b in little[:4]], 2, little[4].at[0], little[5].at[0], put_small),
                   [SMALL_START + o for o in range(5)]))
    last_step = max(steps[-1] for _, steps in agenda)

    def grad_w_out():
        for c in loads[:2]:
            c.wait()

        @pl.loop(0, 8)
        def _(i):
            rows = pl.ds(pl.multiple_of(i * 128, 128), 128)
            gattn[rows, :] = gafter[rows, :].astype(jnp.bfloat16)

        for i in range(2):
            part = dot_tn(mixed[...], gattn[:, i * 512:(i + 1) * 512])
            slots[8 + i] = part.astype(jnp.bfloat16).reshape(2, 2, 4, 2, 32, 512)

    def grad_mixed():
        for c in loads[2:]:
            c.wait()
        for i in range(2):
            cols = slice(i * 512, (i + 1) * 512)
            mixed[:, cols] = dot_nt(gattn[...], normed[cols, :]).astype(jnp.bfloat16)

        @pl.loop(0, 8)
        def _(i):
            rows = pl.ds(pl.multiple_of(i * 128, 128), 128)
            xhat, _ = norm_stats(tok[rows, :].astype(jnp.float32) + cond[rows, :].astype(jnp.float32))
            normed[rows, :] = (xhat * vec_ref[0:1, :] + vec_ref[2:3, :]).astype(jnp.bfloat16)

    def attention_back(half, first, last):
        @pl.loop(first, last)
        def _(b):
            rows = pl.ds(pl.multiple_of(b * BLOCK, BLOCK), BLOCK)
            for pair in range(half * 4, half * 4 + 4):
                c0 = pair * 128
                q2 = stack_heads(qkv[rows, c0:c0 + 128])
                k2 = qkv[rows, 1024 + c0:1024 + c0 + 128]
                v2 = qkv[rows, 2048 + c0:2048 + c0 + 128]
                g2 = stack_heads(mixed[rows, c0:c0 + 128])
                p32 = softmax_pair(q2, k2)
                gprobs = dot_nt(g2, v2)
                gvalue = dot_tn(p32.astype(jnp.bfloat16), g2)
                spread = jnp.sum(p32 * gprobs, axis=-1, keepdims=True)
                gscores = (p32 * (gprobs - spread)).astype(jnp.bfloat16)
                gquery = merge_heads(dot_nn(gscores, k2)) * 0.125
                gkey = dot_tn(gscores, q2) * 0.125
                gqkv[rows, c0:c0 + 128] = gquery.astype(jnp.bfloat16)
                gqkv[rows, 1024 + c0:1024 + c0 + 128] = gkey.astype(jnp.bfloat16)
                gqkv[rows, 2048 + c0:2048 + c0 + 128] = gvalue.astype(jnp.bfloat16)

    def grad_w_qkv(i):
        col = (i % 3) * 1024 + (i // 3) * 512
        part = dot_tn(normed[...], gqkv[:, col:col + 512])
        slots[i] = part.astype(jnp.bfloat16).reshape(2, 2, 4, 2, 32, 512)

    zero = jnp.zeros((1, D), jnp.float32)
    totals = [zero] * 4

    def input_back(h):
        if h == 0:
            load_wqkv.wait()
        rows512 = pl.ds(h * 512, 512)
        gnormed = dot_nt(gqkv[rows512, :], qkv[...])
        gafter2 = gnormed

        xhat, rstd = norm_stats(tok[rows512, :].astype(jnp.float32) + cond[rows512, :].astype(jnp.float32))
        y = gafter2 * vec_ref[0:1, :]
        m1 = jnp.mean(y, axis=-1, keepdims=True)
        m2 = jnp.mean(y * xhat, axis=-1, keepdims=True)
        normed[rows512, :] = (gafter[rows512, :] + rstd * (y - m1 - xhat * m2)).astype(jnp.bfloat16)
        add = (jnp.sum(gafter2 * xhat, axis=0, keepdims=True), jnp.sum(gafter2, axis=0, keepdims=True),
               jnp.sum(gqkv[rows512, :D].astype(jnp.float32), axis=0, keepdims=True),
               jnp.sum(gqkv[rows512, 2 * D:].astype(jnp.float32), axis=0, keepdims=True))
        for i in range(4):
            totals[i] = totals[i] + add[i]
        pltpu.make_async_copy(normed.at[rows512, :], gin_hbm.at[rows512, :], dsem.at[h]).start()

    def fill_small():
        gain1, shift1, qbias, vbias = totals
        eight = jnp.concatenate([gain1, sums_ref[0:1], shift1, qbias, vbias, sums_ref[3:4], sums_ref[1:2], sums_ref[2:3]],
                                axis=0)
        for device in range(32):
            g = device // 4
            w, s = device // 8, device % 8
            at = (w // 2, w % 2, s // 2, s % 2)
            own[at + (slice(0, 8),)] = eight[:, g * 128:(g + 1) * 128]
            own[at + (slice(8, 16),)] = jnp.broadcast_to(fcb_ref[:, device * 128:(device + 1) * 128], (8, 128))

    work = {1: [grad_w_out], 2: [grad_mixed]}
    for i in range(4):
        work[3 + i] = [functools.partial(attention_back, 0, 2 * i, 2 * i + 2)]
        work[10 + i] = [functools.partial(attention_back, 1, 2 * i, 2 * i + 2)]
    work[13].append(load_wqkv.start)
    for i, ready in enumerate((7, 8, 9, 14, 15, 16)):
        work[ready] = [functools.partial(grad_w_qkv, i)]
    work[17] = [functools.partial(input_back, 0)]
    work[18] = [functools.partial(input_back, 1), fill_small]
    waited = set()
    for step in range(last_step + 1):
        for f in work.get(step, ()):
            f()
        for stage_no in (4, 3, 2, 1, 0):
            for number, (p, steps) in enumerate(agenda):
                if steps[stage_no] == step:
                    if stage_no == 0 and number < 8:
                        down_loads[number].wait()
                    p.tick(stage_no)
                    if stage_no == 4:
                        p.finish()
    for h in range(2):
        rows512 = pl.ds(h * 512, 512)
        pltpu.make_async_copy(normed.at[rows512, :], gin_hbm.at[rows512, :], dsem.at[h]).wait()


LATE = ((0, 1, 3, 4, 6), (0, 1, 3, 4, 6), (0, 1, 3, 4, 6), (0, 1, 3, 4, 5), (0, 1, 3, 4, 5), (0, 1, 3, 4, 5))
SMALL_START = 18


def backward(gafter, qkv, mixed, tok, cond, wqkv, wout, gdown, vecs, sums, fcb):
    any_ = pl.BlockSpec(memory_space=pl.ANY)
    vmem = pl.BlockSpec(memory_space=pltpu.VMEM)
    bf, f32 = jnp.bfloat16, jnp.float32
    dma = pltpu.SemaphoreType.DMA
    return pl.pallas_call(
        backward_kernel,
        out_shape=[jax.ShapeDtypeStruct((D, D), bf), jax.ShapeDtypeStruct((32, 3 * D), f32),
                   jax.ShapeDtypeStruct((32, D), f32), jax.ShapeDtypeStruct((128, D), f32),
                   jax.ShapeDtypeStruct((16, 128), f32)],
        in_specs=[any_] * 8 + [vmem] * 3,
        out_specs=[any_] + [vmem] * 4,
        scratch_shapes=[pltpu.VMEM((D, D), f32), pltpu.VMEM((D, D), bf), pltpu.VMEM((D, D), bf),
                        pltpu.VMEM((D, 3 * D), bf), pltpu.VMEM((D, 3 * D), bf), pltpu.VMEM((D, D), bf),
                        pltpu.VMEM((D, D), bf), pltpu.VMEM((D, D), bf),
                        pltpu.VMEM((10, 2, 2, 4, 2, 32, 512), bf), pltpu.VMEM((2, 2, 4, 2, 16, 128), f32),
                        dma((7,)), dma((8,))]
        + scatter_bufs(16, 32, 512) + scatter_bufs(1, 16, 128, f32),
        compiler_params=pltpu.CompilerParams(collective_id=1, has_side_effects=True, vmem_limit_bytes=63 << 20),
    )(gafter, qkv, mixed, tok, cond, wqkv, wout, gdown, vecs, sums, fcb)


def own_sums(small):
    seq = lax.axis_index("seq")
    mine = lax.dynamic_slice(small, (0, (seq % 4) * 32), (8, 32))
    return mine[:2], mine[2:], small[8]


def plain_body(
    tokens,
    condition,
    valid_mask,
    w_qkv,
    w_out,
    w_fc,
    w_down,
    norm_gains,
    biases,
    fc_bias,
    cotangent,
):
    window_count, span_rows, model_width = tokens.shape
    row_total = window_count * span_rows
    head_size = model_width // HEADS
    head_shape = (row_total // BLOCK, BLOCK, HEADS, head_size)
    keep_rows = valid_mask.reshape(row_total, 1).astype(jnp.float32)
    hidden = tokens.reshape(row_total, model_width).astype(jnp.float32) + condition.reshape(
        row_total, model_width
    ).astype(jnp.float32)
    full_qkv, full_out, full_gains, full_biases = (
        lax.all_gather(w_qkv, ("win", "seq"), axis=0, tiled=True),
        lax.all_gather(w_out, ("win", "seq"), axis=0, tiled=True),
        lax.all_gather(norm_gains, ("win", "seq"), axis=1, tiled=True),
        lax.all_gather(biases, ("win", "seq"), axis=1, tiled=True),
    )
    gain_f = full_gains.astype(jnp.float32)
    bias_f = full_biases.astype(jnp.float32)
    normed_f, norm_back_one = jax.vjp(layer_norm, hidden, gain_f[0], bias_f[0])
    normed = normed_f.astype(jnp.bfloat16)
    projected = jnp.dot(normed, full_qkv, preferred_element_type=jnp.float32)
    queries = (projected[:, :model_width] + bias_f[1]).astype(jnp.bfloat16).reshape(head_shape)
    key_rows = projected[:, model_width : 2 * model_width].astype(jnp.bfloat16).reshape(head_shape)
    values = (projected[:, 2 * model_width :] + bias_f[2]).astype(jnp.bfloat16).reshape(head_shape)
    scores = masked_scores(queries, key_rows)
    row_max = jnp.max(scores, axis=-1, keepdims=True)
    log_total = row_max + jnp.log(jnp.sum(jnp.exp(scores - row_max), axis=-1, keepdims=True))
    probs = jnp.exp(scores - log_total).astype(jnp.bfloat16)
    mixed = jnp.einsum("bhqk,bkhd->bqhd", probs, values, preferred_element_type=jnp.float32)
    mixed = mixed.reshape(row_total, model_width).astype(jnp.bfloat16)
    after_attn = hidden + jnp.dot(mixed, full_out, preferred_element_type=jnp.float32) + bias_f[3]
    full_fc, full_down, full_fc_bias = (
        lax.all_gather(w_fc, ("win", "seq"), axis=0, tiled=True),
        lax.all_gather(w_down, ("win", "seq"), axis=0, tiled=True),
        lax.all_gather(fc_bias, ("win", "seq"), axis=0, tiled=True),
    )
    normed_two_f, norm_back_two = jax.vjp(layer_norm, after_attn, gain_f[1], bias_f[4])
    normed_two = normed_two_f.astype(jnp.bfloat16)
    pre_gelu = jnp.dot(
        normed_two, full_fc, preferred_element_type=jnp.float32
    ) + full_fc_bias.astype(jnp.float32)
    gelu_f, gelu_back = jax.vjp(partial(jax.nn.gelu, approximate=False), pre_gelu)
    gelu_out = gelu_f.astype(jnp.bfloat16)
    final_rows = (
        after_attn + jnp.dot(gelu_out, full_down, preferred_element_type=jnp.float32) + bias_f[5]
    )
    output = (final_rows * keep_rows).astype(jnp.bfloat16).reshape(tokens.shape)
    back_fc, back_down = (
        lax.all_gather(w_fc, ("win", "seq"), axis=0, tiled=True),
        lax.all_gather(w_down, ("win", "seq"), axis=0, tiled=True),
    )
    grad_final = cotangent.reshape(row_total, model_width).astype(jnp.float32) * keep_rows
    grad_mlp = grad_final.astype(jnp.bfloat16)
    grad_down_local = outer_sum(gelu_out, grad_mlp)
    grad_down_bias = jnp.sum(grad_mlp.astype(jnp.float32), axis=0)
    grad_gelu = times_transposed(grad_mlp, back_down)
    grad_pre = gelu_back(grad_gelu)[0].astype(jnp.bfloat16)
    grad_fc_local = outer_sum(normed_two, grad_pre)
    grad_fc_bias_local = jnp.sum(grad_pre.astype(jnp.float32), axis=0)
    grad_w_fc, grad_w_down, grad_fc_bias = (
        lax.psum_scatter(grad_fc_local, ("win", "seq"), scatter_dimension=0, tiled=True),
        lax.psum_scatter(grad_down_local, ("win", "seq"), scatter_dimension=0, tiled=True),
        lax.psum_scatter(grad_fc_bias_local, ("win", "seq"), scatter_dimension=0, tiled=True),
    )
    grad_normed_two = times_transposed(grad_pre, back_fc)
    grad_after_norm, grad_gain_two, grad_shift_two = norm_back_two(grad_normed_two)
    grad_after = grad_final + grad_after_norm
    back_qkv, back_out = (
        lax.all_gather(w_qkv, ("win", "seq"), axis=0, tiled=True),
        lax.all_gather(w_out, ("win", "seq"), axis=0, tiled=True),
    )
    grad_attn = grad_after.astype(jnp.bfloat16)
    grad_out_local = outer_sum(mixed, grad_attn)
    grad_out_bias = jnp.sum(grad_attn.astype(jnp.float32), axis=0)
    grad_mixed = times_transposed(grad_attn, back_out).astype(jnp.bfloat16).reshape(head_shape)
    probs_full = jnp.exp(masked_scores(queries, key_rows) - log_total)
    grad_probs = jnp.einsum(
        "bqhd,bkhd->bhqk", grad_mixed, values, preferred_element_type=jnp.float32
    )
    grad_values = jnp.einsum(
        "bhqk,bqhd->bkhd", probs, grad_mixed, preferred_element_type=jnp.float32
    )
    grad_values = grad_values.reshape(row_total, model_width).astype(jnp.bfloat16)
    grad_scores = probs_full * (
        grad_probs - jnp.sum(probs_full * grad_probs, axis=-1, keepdims=True)
    )
    grad_scores = grad_scores.astype(jnp.bfloat16)
    grad_queries = (
        jnp.einsum("bhqk,bkhd->bqhd", grad_scores, key_rows, preferred_element_type=jnp.float32)
        * 0.125
    )
    grad_keys = (
        jnp.einsum("bhqk,bqhd->bkhd", grad_scores, queries, preferred_element_type=jnp.float32)
        * 0.125
    )
    grad_queries = grad_queries.reshape(row_total, model_width).astype(jnp.bfloat16)
    grad_keys = grad_keys.reshape(row_total, model_width).astype(jnp.bfloat16)
    grad_query_bias = jnp.sum(grad_queries.astype(jnp.float32), axis=0)
    grad_value_bias = jnp.sum(grad_values.astype(jnp.float32), axis=0)
    grad_projected = jnp.concatenate([grad_queries, grad_keys, grad_values], axis=1)
    grad_qkv_local = outer_sum(normed, grad_projected)
    grad_normed = times_transposed(grad_projected, back_qkv)
    grad_hidden_norm, grad_gain_one, grad_shift_one = norm_back_one(grad_normed)
    grad_input = (grad_after + grad_hidden_norm).astype(jnp.bfloat16).reshape(tokens.shape)
    gains_local = jnp.stack([grad_gain_one, grad_gain_two])
    biases_local = jnp.stack(
        [
            grad_shift_one,
            grad_query_bias,
            grad_value_bias,
            grad_out_bias,
            grad_shift_two,
            grad_down_bias,
        ]
    )
    grad_w_qkv, grad_w_out, grad_gains, grad_biases = (
        lax.psum_scatter(grad_qkv_local, ("win", "seq"), scatter_dimension=0, tiled=True),
        lax.psum_scatter(grad_out_local, ("win", "seq"), scatter_dimension=0, tiled=True),
        lax.psum_scatter(gains_local, ("win", "seq"), scatter_dimension=1, tiled=True),
        lax.psum_scatter(biases_local, ("win", "seq"), scatter_dimension=1, tiled=True),
    )
    return (
        output,
        grad_input,
        grad_w_qkv,
        grad_w_out,
        grad_w_fc,
        grad_w_down,
        grad_gains,
        grad_biases,
        grad_fc_bias,
    )


GATHER_ORDER = (2, 0, 2, 2, 1, 2)


def body(
    tokens,
    condition,
    valid_mask,
    w_qkv,
    w_out,
    w_fc,
    w_down,
    norm_gains,
    biases,
    fc_bias,
    cotangent,
):
    tok, cond, cot = (a.reshape(D, D) for a in (tokens, condition, cotangent))
    keep_rows = valid_mask.reshape(D, 1).astype(jnp.float32)
    shards = (own_small(norm_gains, biases, fc_bias), w_qkv, w_out, w_fc, w_down)
    _, full_qkv, full_out, full_fc, full_down, qkv, mixed, after, vecs, full_fc_bias = gather_and_attend(
        shards, tok, cond
    )
    output, grad_after, grad_down_local, grad_w_fc, two_sums, fc_bias_sums = mlp(
        True, after, cot, keep_rows, vecs, full_fc_bias, full_fc.reshape(D, FF), full_down.reshape(FF, D)
    )
    grad_input, grad_w_qkv, grad_w_out, grad_w_down, small = backward(
        grad_after,
        qkv,
        mixed,
        tok,
        cond,
        full_qkv.reshape(D, 3 * D),
        full_out.reshape(D, D),
        grad_down_local.reshape(2, 2, 4, 2, 128, D),
        vecs,
        two_sums,
        fc_bias_sums,
    )
    grad_gains, grad_biases, grad_fc_bias = own_sums(small)
    return (
        output.reshape(tokens.shape),
        grad_input.reshape(tokens.shape),
        grad_w_qkv,
        grad_w_out,
        grad_w_fc,
        grad_w_down,
        grad_gains,
        grad_biases,
        grad_fc_bias,
    )


def solution(mesh):
    fast = mesh.shape["win"] == 4 and mesh.shape["seq"] == 8
    return jax.shard_map(
        body if fast else plain_body,
        mesh=mesh,
        in_specs=(
            P("win", "seq", None),
            P("win", "seq", None),
            P("win", "seq"),
            P(("win", "seq"), None),
            P(("win", "seq"), None),
            P(("win", "seq"), None),
            P(("win", "seq"), None),
            P(None, ("win", "seq")),
            P(None, ("win", "seq")),
            P(("win", "seq")),
            P("win", "seq", None),
        ),
        out_specs=(
            P("win", "seq", None),
            P("win", "seq", None),
            P(("win", "seq"), None),
            P(("win", "seq"), None),
            P(("win", "seq"), None),
            P(("win", "seq"), None),
            P(None, ("win", "seq")),
            P(None, ("win", "seq")),
            P(("win", "seq")),
        ),
        check_vma=False,
    )
```

```python
import functools
from functools import partial

import jax
import jax.numpy as jnp
from jax import lax
from jax.experimental import pallas as pl
from jax.experimental.pallas import tpu as pltpu
from jax.sharding import PartitionSpec as P

MESH = pl.DeviceIdType.MESH
ALL = slice(None)


class Place:
    def __init__(self):
        win, seq = lax.axis_index("win"), lax.axis_index("seq")
        self.y, self.x = win // 2, win % 2
        self.z, self.c = seq // 2, seq % 2

    def device(self, y=None, x=None, z=None, c=None):
        y = self.y if y is None else y
        x = self.x if x is None else x
        z = self.z if z is None else z
        c = self.c if c is None else c
        return (y * 2 + x, z * 2 + c)

    def partner(self, dim):
        if dim == "x":
            return self.device(x=1 - self.x)
        if dim == "y":
            return self.device(y=1 - self.y)
        return self.device(c=1 - self.c)


def greet(place):
    barrier = pltpu.get_barrier_semaphore()
    others = [place.partner(dim) for dim in "xyc"]
    others += [place.device(z=(place.z + t) % 4) for t in (1, 2, 3)]
    for device in others:
        pl.semaphore_signal(barrier, inc=1, device_id=device, device_id_type=MESH)
    pl.semaphore_wait(barrier, 6)


def guarded(cond, thunk):
    if cond is None:
        thunk()
    else:
        pl.when(cond)(thunk)


class Gather:
    def __init__(self, place, view, order, send, recv, slack=0):
        self.p, self.view, self.send, self.recv = place, view, send, recv
        self.order, self.sent = order, []
        self.ticks = self.plan(slack)

    def region(self, got, **at):
        p = self.p
        pick = lambda d, own: at[d] if d in at else (ALL if d in got else own)
        return self.view(pick("y", p.y), pick("x", p.x), pick("z", p.z), at.get("c", p.c))

    def copy(self, region, device, number):
        return pltpu.make_async_remote_copy(
            region, region, self.send.at[number], self.recv.at[number],
            device_id=device, device_id_type=MESH)

    def push(self, cond, make, device, number):
        def go():
            self.copy(make(), device, number).start()
        guarded(cond, go)

        def end():
            self.copy(make(), device, number).wait_send()
        self.sent.append((cond, end))

    def take(self, cond, make, number):
        def go():
            self.copy(make(), self.p.device(c=1 - self.p.c), number).wait_recv()
        guarded(cond, go)

    def both(self, cond, other):
        return other if cond is None else jnp.logical_and(cond, other)

    def line_push(self, got, cond):
        for t in (1, 2, 3):
            self.push(cond, lambda: self.region(got), self.p.device(z=(self.p.z + t) % 4), 1 + t)

    def line_take(self, got, cond):
        for t in (1, 2, 3):
            self.take(cond, lambda t=t: self.region(got, z=(self.p.z + 4 - t) % 4), 1 + t)

    def plan(self, slack):
        out = []
        p = self.p
        orders = {0: (("xzy", None),), 1: (("yzx", None),),
                  2: (("zxy", p.c == 0), ("zyx", p.c == 1))}[self.order]
        lists = []
        for order, cond in orders:
            ticks = [[]]
            got = ""
            ex = 0
            for dim in order:
                if dim == "z":
                    ticks[-1].append(functools.partial(self.line_push, got, cond))
                    ticks.append([])
                    ticks[-1].append(functools.partial(self.line_take, got, cond))
                else:
                    ticks[-1].append(functools.partial(
                        self.push, cond, functools.partial(self.region, got), p.partner(dim), ex))
                    if ex == 1:
                        ticks.extend([] for _ in range(slack))
                    ticks.append([])
                    own = p.x if dim == "x" else p.y
                    ticks[-1].append(functools.partial(
                        self.take, cond, functools.partial(self.region, got, **{dim: 1 - own}), ex))
                    ex += 1
                got += dim
            ticks[-1].append(functools.partial(self.push, cond, functools.partial(self.region, "xyz"),
                                               p.partner("c"), 8))
            ticks.append([])
            ticks[-1].append(functools.partial(self.take, cond,
                                               functools.partial(self.region, "xyz", c=1 - p.c), 8))
            lists.append(ticks)
        n = max(len(t) for t in lists)
        for i in range(n):
            thunks = [f for t in lists if i < len(t) for f in t[i]]
            out.append(thunks)
        return out

    def tick(self, i):
        for f in self.ticks[i]:
            f()

    def finish(self):
        for cond, end in self.sent:
            guarded(cond, end)


def run_ticks(pieces, starts, between=None):
    last = max(s + len(p.ticks) for p, s in zip(pieces, starts))
    for now in range(last):
        for p, s in zip(pieces, starts):
            if 0 <= now - s < len(p.ticks):
                p.tick(now - s)
        if between and now in between:
            between[now]()
    for p in pieces:
        p.finish()


class Scatter:
    def __init__(self, place, slot, bufs, order, send, recv, put):
        self.p, self.slot, self.bufs, self.put = place, slot, bufs, put
        self.send, self.recv, self.sent = send, recv, []
        self.ticks = self.plan(order)

    def region(self, left, **at):
        p = self.p
        pick = lambda d, own: at[d] if d in at else (ALL if d in left else own)
        return self.slot.at[pick("y", p.y), pick("x", p.x), pick("z", p.z), at.get("c", p.c)]

    def push(self, cond, make, buf, device, number):
        def copy():
            return pltpu.make_async_remote_copy(
                make(), buf, self.send.at[number], self.recv.at[number],
                device_id=device, device_id_type=MESH)
        guarded(cond, lambda: copy().start())
        self.sent.append((cond, lambda: copy().wait_send()))

    def take(self, cond, makes, bufs, numbers, last):
        def go():
            for buf, number in zip(bufs, numbers):
                pltpu.make_async_remote_copy(
                    buf, buf, self.send.at[number], self.recv.at[number],
                    device_id=self.p.partner("c"), device_id_type=MESH).wait_recv()
            region = makes()
            shape = region.shape
            outer = [()]
            while len(shape) - len(outer[0]) > 3:
                outer = [o + (i,) for o in outer for i in range(shape[len(o)])]
            for o in outer:
                many = last or len(bufs) > 1
                total = region[o + (Ellipsis,)]
                total = total.astype(jnp.float32) if many else total
                for buf in bufs:
                    total = total + buf[o + (Ellipsis,)].astype(total.dtype)
                if last:
                    self.put(total)
                else:
                    region[o + (Ellipsis,)] = total.astype(region.dtype)
        guarded(cond, go)

    def plan(self, order):
        p = self.p
        core, first, second, line = self.bufs
        variants = {0: (("yzx", None),), 1: (("xzy", None),),
                    2: (("yxz", p.c == 0), ("xyz", p.c == 1))}[order]
        ticks = [[] for _ in range(5)]
        for dims, cond in variants:
            left = "xyz"
            ticks[0].append(functools.partial(
                self.push, cond, lambda: self.region("xyz", c=1 - p.c), core, p.partner("c"), 0))
            ticks[1].append(functools.partial(
                self.take, cond, lambda: self.region("xyz"), [core], [0], False))
            for i, dim in enumerate(dims):
                rest = left.replace(dim, "")
                last = i == 2
                mine = functools.partial(self.region, rest)
                if dim == "z":
                    bufs = [line.at[t - 1] if rest else line.at[t - 1, 0] for t in (1, 2, 3)]
                    for t in (1, 2, 3):
                        to = (p.z + t) % 4
                        ticks[i + 1].append(functools.partial(
                            self.push, cond, functools.partial(self.region, rest, z=to),
                            bufs[t - 1], p.device(z=to), 2 + t))
                    ticks[i + 2].append(functools.partial(
                        self.take, cond, mine, bufs, [3, 4, 5], last))
                else:
                    buf = first if i == 0 else (second if i == 1 else second.at[0])
                    number = 1 if i == 0 else 2
                    own = p.x if dim == "x" else p.y
                    ticks[i + 1].append(functools.partial(
                        self.push, cond, functools.partial(self.region, rest, **{dim: 1 - own}),
                        buf, p.partner(dim), number))
                    ticks[i + 2].append(functools.partial(
                        self.take, cond, mine, [buf], [number], last))
                left = rest
        return ticks

    def tick(self, i):
        for f in self.ticks[i]:
            f()

    def finish(self):
        for cond, end in self.sent:
            guarded(cond, end)


SCATTER_SEMS = 6
GATHER_SEMS = 9


def scatter_bufs(count, rows, cols, dtype=jnp.bfloat16, cores=None):
    return [pltpu.VMEM((cores or count, 2, 2, 4, rows, cols), dtype), pltpu.VMEM((count, 2, 4, rows, cols), dtype),
            pltpu.VMEM((count, 4, rows, cols), dtype), pltpu.VMEM((count, 3, 2, rows, cols), dtype),
            pltpu.SemaphoreType.DMA((count, SCATTER_SEMS)), pltpu.SemaphoreType.DMA((count, SCATTER_SEMS))]


D, FF, CH = 1024, 4096, 512
DELAY = (0, 1, 4, 6, 8)
TILE = 256


def dot_nn(a, b):
    return lax.dot_general(a, b, (((1,), (0,)), ((), ())), preferred_element_type=jnp.float32)


def dot_nt(a, b):
    return lax.dot_general(a, b, (((1,), (1,)), ((), ())), preferred_element_type=jnp.float32)


def dot_tn(a, b):
    return lax.dot_general(a, b, (((0,), (0,)), ((), ())), preferred_element_type=jnp.float32)


def norm_stats(rows_in):
    mean = jnp.mean(rows_in, axis=-1, keepdims=True)
    centered = rows_in - mean
    var = jnp.mean(centered * centered, axis=-1, keepdims=True)
    rstd = lax.rsqrt(var + 1e-05)
    return centered * rstd, rstd


def gelu_both(v):
    phi = 0.5 + 0.5 * lax.erf(v * 0.7071067811865476)
    slope = phi + v * (jnp.exp(-0.5 * v * v) * 0.3989422804014327)
    return (v * phi).astype(jnp.bfloat16), slope


def mlp_kernel(comm, after_hbm, cot_hbm, mask_ref, vec_ref, fcb_ref, wfc_hbm, wdn_hbm,
               out_ref, gafter_hbm, gdown_hbm, gfc_ref, small_ref, gfcb_ref,
               after, gm, n2, n2t, gelu, gp, fin, gn2, wfc, wdn, stage, slots, lsem, wsem, ssem, *rest):
    place = Place()
    if comm:
        greet(place)
    load_after = pltpu.make_async_copy(after_hbm, after, lsem.at[0])
    load_cot = pltpu.make_async_copy(cot_hbm, gm, lsem.at[1])
    load_after.start()
    load_cot.start()

    def fetch_fc(j):
        return pltpu.make_async_copy(wfc_hbm.at[:, pl.ds(j * CH, CH)], wfc.at[j % 2], wsem.at[j % 2, 0])

    def fetch_down(i):
        j = i % (FF // CH)
        return pltpu.make_async_copy(wdn_hbm.at[pl.ds(j * CH, CH), :], wdn.at[i % 2], wsem.at[i % 2, 1])

    fetch_fc(0).start()
    fetch_down(0).start()
    load_after.wait()
    load_cot.wait()

    @pl.loop(0, D // 128)
    def _(i):
        rows = pl.ds(pl.multiple_of(i * 128, 128), 128)
        xhat, _ = norm_stats(after[rows, :])
        v = (xhat * vec_ref[1:2, :] + vec_ref[6:7, :]).astype(jnp.bfloat16)
        n2[rows, :] = v
        n2t[:, rows] = v.T
        g = gm[rows, :].astype(jnp.float32) * mask_ref[rows, :]
        gm[rows, :] = g.astype(jnp.bfloat16)
        fin[rows, :] = jnp.zeros((128, D), jnp.float32)
        gn2[rows, :] = jnp.zeros((128, D), jnp.float32)

    n = FF // CH

    def store(j):
        return pltpu.make_async_copy(stage.at[j % 2], gdown_hbm.at[pl.ds(j * CH, CH), :], ssem.at[j % 2])

    pieces = []
    if comm:
        bufs = rest
        for j in range(n):
            def put(value, j=j):
                gfc_ref[:, pl.ds(j * CH, CH)] = value

            pieces.append(Scatter(place, slots.at[j], [b.at[j] for b in bufs[:4]],
                                  GATHER_ORDER[j % 6], bufs[4].at[j], bufs[5].at[j], put))

    def advance(step, first, last):
        if comm:
            for now in range(first, last):
                @pl.when(step == now)
                def _(now=now):
                    for stage_no in (4, 3, 2, 1, 0):
                        j = now - DELAY[stage_no]
                        if 0 <= j < n:
                            pieces[j].tick(stage_no)
                            if stage_no == 4:
                                pieces[j].finish()

    @pl.loop(0, n)
    def _(j):
        s = j % 2
        fetch_fc(j).wait()
        fetch_down(j).wait()
        fetch_down(j + 1).start()

        @pl.when(j + 1 < n)
        def _():
            fetch_fc(j + 1).start()

        cols = pl.ds(pl.multiple_of(j * CH, CH), CH)
        pre = dot_nn(n2[...], wfc[s]) + fcb_ref[:, cols]
        act, slope = gelu_both(pre)
        grad = (dot_nt(gm[...], wdn[s]) * slope).astype(jnp.bfloat16)
        gelu[:, cols] = act
        gp[...] = grad
        gfcb_ref[:, cols] = jnp.sum(grad.astype(jnp.float32), axis=0, keepdims=True)
        gn2[...] += dot_nt(gp[...], wfc[s])
        slots[j] = dot_nn(n2t[...], gp[...]).astype(jnp.bfloat16).reshape(2, 2, 4, 2, 32, CH)
        advance(j, 0, n)

    @pl.loop(0, n)
    def _(j):
        s = j % 2
        fetch_down(j + n).wait()

        @pl.when(j + 1 < n)
        def _():
            fetch_down(j + n + 1).start()

        @pl.when(j >= 2)
        def _():
            store(j - 2).wait()

        cols = pl.ds(pl.multiple_of(j * CH, CH), CH)
        fin[...] += dot_nn(gelu[:, cols], wdn[s])
        stage[s] = dot_tn(gelu[:, cols], gm[...]).astype(jnp.bfloat16)
        store(j).start()
        advance(j + n, n, 2 * n)

    store(n - 2).wait()
    store(n - 1).wait()

    def norm_step(i, sums):
        rows = pl.ds(pl.multiple_of(i * 128, 128), 128)
        xhat, rstd = norm_stats(after[rows, :])
        keep = mask_ref[rows, :]
        out_ref[rows, :] = ((after[rows, :] + fin[rows, :] + vec_ref[7:8, :]) * keep).astype(jnp.bfloat16)
        g = gn2[rows, :]
        y = g * vec_ref[1:2, :]
        m1 = jnp.mean(y, axis=-1, keepdims=True)
        m2 = jnp.mean(y * xhat, axis=-1, keepdims=True)
        gmf = gm[rows, :].astype(jnp.float32)
        ga = gmf + rstd * (y - m1 - xhat * m2)
        fin[rows, :] = ga
        gattn = ga.astype(jnp.bfloat16).astype(jnp.float32)
        return tuple(s + jnp.sum(v, axis=0, keepdims=True)
                     for s, v in zip(sums, (g * xhat, g, gmf, gattn)))

    def half(h):
        return pltpu.make_async_copy(fin.at[pl.ds(h * 512, 512), :], gafter_hbm.at[pl.ds(h * 512, 512), :], lsem.at[h])

    zero = jnp.zeros((1, D), jnp.float32)
    sums = lax.fori_loop(0, D // 256, norm_step, (zero,) * 4)
    half(0).start()
    sums = lax.fori_loop(D // 256, D // 128, norm_step, sums)
    half(1).start()
    for i in range(4):
        small_ref[i:i + 1, :] = sums[i]
    half(0).wait()
    half(1).wait()


def mlp(comm, after, cot, mask, vecs, fcb, wfc, wdn):
    n = FF // CH
    any_ = pl.BlockSpec(memory_space=pl.ANY)
    vmem = pl.BlockSpec(memory_space=pltpu.VMEM)
    return pl.pallas_call(
        functools.partial(mlp_kernel, comm),
        out_shape=[jax.ShapeDtypeStruct((D, D), jnp.bfloat16), jax.ShapeDtypeStruct((D, D), jnp.float32),
                   jax.ShapeDtypeStruct((FF, D), jnp.bfloat16), jax.ShapeDtypeStruct((32, FF), jnp.float32),
                   jax.ShapeDtypeStruct((8, D), jnp.float32), jax.ShapeDtypeStruct((1, FF), jnp.float32)],
        in_specs=[any_, any_, vmem, vmem, vmem, any_, any_],
        out_specs=[vmem, any_, any_, vmem, vmem, vmem],
        scratch_shapes=[pltpu.VMEM((D, D), jnp.float32), pltpu.VMEM((D, D), jnp.bfloat16),
                        pltpu.VMEM((D, D), jnp.bfloat16), pltpu.VMEM((D, D), jnp.bfloat16),
                        pltpu.VMEM((D, FF), jnp.bfloat16), pltpu.VMEM((D, CH), jnp.bfloat16),
                        pltpu.VMEM((D, D), jnp.float32), pltpu.VMEM((D, D), jnp.float32),
                        pltpu.VMEM((2, D, CH), jnp.bfloat16), pltpu.VMEM((2, CH, D), jnp.bfloat16),
                        pltpu.VMEM((2, CH, D), jnp.bfloat16),
                        pltpu.VMEM((n, 2, 2, 4, 2, 32, CH), jnp.bfloat16),
                        pltpu.SemaphoreType.DMA((2,)), pltpu.SemaphoreType.DMA((2, 2)), pltpu.SemaphoreType.DMA((2,))]
        + (scatter_bufs(n, 32, CH) if comm else []),
        compiler_params=pltpu.CompilerParams(vmem_limit_bytes=60 << 20,
            **(dict(collective_id=2, has_side_effects=True) if comm else {})),
    )(after, cot, mask, vecs, fcb, wfc, wdn)


HEADS = 16
BLOCK = 128


def layer_norm(rows_in, gain_vec, shift_vec):
    row_mean = jnp.mean(rows_in, axis=-1, keepdims=True)
    centered = rows_in - row_mean
    row_var = jnp.mean(centered * centered, axis=-1, keepdims=True)
    return centered * lax.rsqrt(row_var + 1e-05) * gain_vec + shift_vec


def outer_sum(first, second):
    return lax.dot_general(
        first, second, (((0,), (0,)), ((), ())), preferred_element_type=jnp.float32
    )


def times_transposed(first, second):
    return lax.dot_general(
        first, second, (((1,), (1,)), ((), ())), preferred_element_type=jnp.float32
    )


def masked_scores(queries_h, keys_h):
    scores = (
        jnp.einsum("bqhd,bkhd->bhqk", queries_h, keys_h, preferred_element_type=jnp.float32) * 0.125
    )
    causal = lax.broadcasted_iota(jnp.int32, scores.shape, 2) >= lax.broadcasted_iota(
        jnp.int32, scores.shape, 3
    )
    return jnp.where(causal, scores, -1e30)


def lane_low(shape):
    return lax.broadcasted_iota(jnp.int32, shape, len(shape) - 1) < 64


def stack_heads(pair):
    low = lane_low(pair.shape)
    zero = jnp.zeros_like(pair)
    return jnp.concatenate([jnp.where(low, pair, zero), jnp.where(low, zero, pair)], axis=0)


def merge_heads(stacked):
    half = stacked.shape[0] // 2
    return jnp.where(lane_low((half, stacked.shape[1])), stacked[:half], stacked[half:])


def softmax_keys(key2, query2):
    scores = dot_nt(key2, query2)
    key = lax.broadcasted_iota(jnp.int32, scores.shape, 0)
    query = lax.broadcasted_iota(jnp.int32, scores.shape, 1) % BLOCK
    scores = jnp.where(key <= query, scores, -1e30)
    top = jnp.max(scores, axis=0, keepdims=True)
    raised = jnp.exp((scores - top) * 0.125)
    return raised * (1.0 / jnp.sum(raised, axis=0, keepdims=True))


GATHER_CUTS = ([(0, (0, 16), (0, 128))]
               + [(1, (0, 32), (i * 512, 512)) for i in range(6)]
               + [(2, (0, 32), (i * 512, 512)) for i in range(2)]
               + [(3, (0, 32), (i * 512, 512)) for i in range(8)]
               + [(4, (i * 16, 16), (0, 1024)) for i in range(8)])


def gather_kernel(small, wqkv_s, wout_s, wfc_s, wdn_s, tok_hbm, cond_hbm,
                  small_f, wqkv_f, wout_f, wfc_f, wdn_f, qkv_hbm, mixed_hbm, after_hbm, vec_ref, fcb_ref,
                  tok, cond, hidden, normed, wqkv, wout, qkv, mixed, smallv,
                  send, recv, own_sem, lsem, wsem, osem):
    ins = (small, wqkv_s, wout_s, wfc_s, wdn_s)
    fulls = (small_f, wqkv_f, wout_f, wfc_f, wdn_f)
    place = Place()
    greet(place)
    own = [pltpu.make_async_copy(s, f.at[place.y, place.x, place.z, place.c], own_sem.at[i])
           for i, (s, f) in enumerate(zip(ins, fulls))]
    loads = [pltpu.make_async_copy(tok_hbm, tok, lsem.at[0]), pltpu.make_async_copy(cond_hbm, cond, lsem.at[1])]
    for c in own + loads:
        c.start()
    for c in own:
        c.wait()

    def make(k):
        n, (r0, r), (c0, w) = GATHER_CUTS[k]
        view = lambda y, x, z, c: fulls[n].at[y, x, z, c, pl.ds(r0, r), pl.ds(c0, w)]
        return Gather(place, view, GATHER_ORDER[k % 6], send.at[k], recv.at[k], 1)

    load_small = pltpu.make_async_copy(small_f, smallv, lsem.at[2])
    load_qkv = pltpu.make_async_copy(wqkv_f, wqkv, wsem.at[0])
    load_out = pltpu.make_async_copy(wout_f, wout, wsem.at[1])
    store_qkv = pltpu.make_async_copy(qkv, qkv_hbm, osem.at[0])
    store_mixed = pltpu.make_async_copy(mixed, mixed_hbm, osem.at[1])
    store_after = pltpu.make_async_copy(hidden, after_hbm, osem.at[2])

    def add_hidden():
        for c in loads:
            c.wait()

        @pl.loop(0, D // 128)
        def _(i):
            rows = pl.ds(pl.multiple_of(i * 128, 128), 128)
            hidden[rows, :] = tok[rows, :].astype(jnp.float32) + cond[rows, :].astype(jnp.float32)

    def first_norm():
        load_small.start()
        load_small.wait()
        for g in range(8):
            win, z0 = g // 2, (g % 2) * 2
            total = None
            for i in range(4):
                y, x, z, c = win // 2, win % 2, z0 + i // 2, i % 2
                one = smallv[y, x, z, c].astype(jnp.float32)
                device = g * 4 + i
                fcb_ref[:, device * 128:(device + 1) * 128] = one[8:9]
                total = one[:8] if total is None else total + one[:8]
            vec_ref[:, g * 128:(g + 1) * 128] = total

        @pl.loop(0, D // 128)
        def _(i):
            rows = pl.ds(pl.multiple_of(i * 128, 128), 128)
            xhat, _ = norm_stats(hidden[rows, :])
            normed[rows, :] = (xhat * vec_ref[0:1, :] + vec_ref[2:3, :]).astype(jnp.bfloat16)

    def project(first, last):
        for i in range(first, last):
            cols = slice(i * 512, (i + 1) * 512)
            weight = wqkv[:, :, :, :, :, cols].reshape(D, 512)
            part = dot_nn(normed[...], weight)
            if i < 2:
                part = part + vec_ref[3:4, cols]
            if i >= 4:
                part = part + vec_ref[4:5, i * 512 - 2048:i * 512 - 1536]
            qkv[:, cols] = part.astype(jnp.bfloat16)

    def attend(first, last):
        @pl.loop(first, last)
        def _(b):
            rows = pl.ds(pl.multiple_of(b * BLOCK, BLOCK), BLOCK)
            starts = range(0, D, 128)
            queries = [stack_heads(qkv[rows, c:c + 128]) for c in starts]
            keys = [qkv[rows, D + c:D + c + 128] for c in starts]
            values = [qkv[rows, 2 * D + c:2 * D + c + 128] for c in starts]
            probs = [softmax_keys(k, q).astype(jnp.bfloat16) for k, q in zip(keys, queries)]
            outs = [merge_heads(dot_tn(p, v)) for p, v in zip(probs, values)]
            for c, out in zip(starts, outs):
                mixed[rows, c:c + 128] = out.astype(jnp.bfloat16)

    def output_projection():
        load_out.wait()
        for i in range(2):
            cols = slice(i * 512, (i + 1) * 512)
            part = dot_nn(mixed[...], wout[:, :, :, :, :, cols].reshape(D, 512))
            hidden[:, cols] += part + vec_ref[5:6, cols]
        store_after.start()

    def step8():
        load_qkv.wait()
        project(0, 6)
        store_qkv.start()

    def step7():
        load_qkv.start()

    def step9():
        load_out.start()
        attend(0, 4)

    def step10():
        attend(4, 8)
        store_mixed.start()

    between = {0: add_hidden, 5: first_norm, 7: step7, 8: step8, 9: step9, 10: step10, 11: output_projection}
    run_ticks([make(k) for k in range(len(GATHER_CUTS))], [(k + 2) // 3 for k in range(len(GATHER_CUTS))], between)
    store_qkv.wait()
    store_mixed.wait()
    store_after.wait()


def gather_and_attend(shards, tok, cond):
    any_ = pl.BlockSpec(memory_space=pl.ANY)
    vmem = pl.BlockSpec(memory_space=pltpu.VMEM)
    count = len(GATHER_CUTS)
    bf, f32 = jnp.bfloat16, jnp.float32
    dma = pltpu.SemaphoreType.DMA
    return pl.pallas_call(
        gather_kernel,
        out_shape=[jax.ShapeDtypeStruct((2, 2, 4, 2) + s.shape, s.dtype) for s in shards]
        + [jax.ShapeDtypeStruct((D, 3 * D), bf), jax.ShapeDtypeStruct((D, D), bf), jax.ShapeDtypeStruct((D, D), f32),
           jax.ShapeDtypeStruct((8, D), f32), jax.ShapeDtypeStruct((1, FF), f32)],
        in_specs=[any_] * 7,
        out_specs=[any_] * 8 + [vmem] * 2,
        scratch_shapes=[pltpu.VMEM((D, D), bf), pltpu.VMEM((D, D), bf), pltpu.VMEM((D, D), f32), pltpu.VMEM((D, D), bf),
                        pltpu.VMEM((2, 2, 4, 2, 32, 3 * D), bf), pltpu.VMEM((2, 2, 4, 2, 32, D), bf),
                        pltpu.VMEM((D, 3 * D), bf), pltpu.VMEM((D, D), bf), pltpu.VMEM((2, 2, 4, 2, 16, 128), bf),
                        dma((count, GATHER_SEMS)), dma((count, GATHER_SEMS)), dma((5,)), dma((3,)), dma((2,)), dma((3,))],
        compiler_params=pltpu.CompilerParams(collective_id=0, has_side_effects=True, vmem_limit_bytes=60 << 20),
    )(*shards, tok, cond)


def own_small(gains, biases, fc_bias):
    seq = lax.axis_index("seq")
    eight = jnp.concatenate([gains, biases], axis=0)
    placed = jnp.where(jnp.arange(4)[None, :, None] == seq % 4, eight[:, None, :], 0).reshape(8, 128)
    return jnp.concatenate([placed, fc_bias.reshape(1, 128), jnp.zeros((7, 128), fc_bias.dtype)], axis=0)


DOWN_CUTS = [(r0, c0) for r0 in range(0, 128, 32) for c0 in (0, 512)]


def backward_kernel(gafter_hbm, qkv_hbm, mixed_hbm, tok_hbm, cond_hbm, wqkv_hbm, wout_hbm, gdown_hbm, vec_ref,
                    sums_ref, fcb_ref,
                    gin_hbm, gqkv_ref, gout_ref, gdown_ref, small_ref,
                    gafter, gattn, mixed, qkv, gqkv, tok, cond, normed, slots, own, lsem, dsem,
                    *rest):
    big, little, credit = rest[:6], rest[6:12], rest[12]
    place = Place()
    greet(place)
    loads = [pltpu.make_async_copy(s, d, lsem.at[i]) for i, (s, d) in enumerate((
        (gafter_hbm, gafter), (mixed_hbm, mixed), (wout_hbm, normed), (tok_hbm, tok), (cond_hbm, cond), (qkv_hbm, qkv)))]
    down_loads = [pltpu.make_async_copy(gdown_hbm.at[:, :, :, :, pl.ds(r0, 32), pl.ds(c0, 512)], slots.at[i], dsem.at[i])
                  for i, (r0, c0) in enumerate(DOWN_CUTS)]
    for c in down_loads[:2] + loads + down_loads[2:]:
        c.start()
    load_wqkv = pltpu.make_async_copy(wqkv_hbm, qkv, lsem.at[6])

    def piece(k, slot, put):
        return Scatter(place, slots.at[slot], [big[0].at[k % 8]] + [b.at[k] for b in big[1:4]], GATHER_ORDER[k % 6],
                       big[4].at[k], big[5].at[k], put)

    def putter(ref, r0, c0):
        def put(value):
            ref[pl.ds(r0, 32), pl.ds(c0, 512)] = value
        return put

    agenda = []
    for i, (r0, c0) in enumerate(DOWN_CUTS):
        agenda.append((piece(i, i, putter(gdown_ref, r0, c0)), DOWN_STEPS[i]))
    for i in range(2):
        agenda.append((piece(8 + i, 8 + i, putter(gout_ref, 0, i * 512)), OUT_STEPS[i]))
    for i in range(6):
        col = (i % 3) * 1024 + (i // 3) * 512
        agenda.append((piece(10 + i, QKV_SLOT[i], putter(gqkv_ref, 0, col)), QKV_STEPS[i // 3]))

    def put_small(value):
        small_ref[...] = value

    agenda.append((Scatter(place, own, [b.at[0] for b in little[:4]], 2, little[4].at[0], little[5].at[0], put_small),
                   SMALL_STEPS))
    last_step = max(steps[-1] for _, steps in agenda)

    def grad_w_out():
        for c in loads[:2]:
            c.wait()

        @pl.loop(0, 8)
        def _(i):
            rows = pl.ds(pl.multiple_of(i * 128, 128), 128)
            gattn[rows, :] = gafter[rows, :].astype(jnp.bfloat16)

        for i in range(2):
            part = dot_tn(mixed[...], gattn[:, i * 512:(i + 1) * 512])
            slots[8 + i] = part.astype(jnp.bfloat16).reshape(2, 2, 4, 2, 32, 512)

    def grad_mixed():
        for c in loads[2:]:
            c.wait()
        for i in range(2):
            cols = slice(i * 512, (i + 1) * 512)
            mixed[:, cols] = dot_nt(gattn[...], normed[cols, :]).astype(jnp.bfloat16)

        @pl.loop(0, 8)
        def _(i):
            rows = pl.ds(pl.multiple_of(i * 128, 128), 128)
            xhat, _ = norm_stats(tok[rows, :].astype(jnp.float32) + cond[rows, :].astype(jnp.float32))
            normed[rows, :] = (xhat * vec_ref[0:1, :] + vec_ref[2:3, :]).astype(jnp.bfloat16)

    def attention_back(half, first, last):
        @pl.loop(first, last)
        def _(b):
            rows = pl.ds(pl.multiple_of(b * BLOCK, BLOCK), BLOCK)
            starts = range(half * 512, half * 512 + 512, 128)
            queries = [stack_heads(qkv[rows, c:c + 128]) for c in starts]
            keys = [qkv[rows, D + c:D + c + 128] for c in starts]
            values = [qkv[rows, 2 * D + c:2 * D + c + 128] for c in starts]
            grads = [stack_heads(mixed[rows, c:c + 128]) for c in starts]
            probs = [softmax_keys(k, q) for k, q in zip(keys, queries)]
            gprobs = [dot_nt(v, g) for v, g in zip(values, grads)]
            gvalues = [dot_nn(p.astype(jnp.bfloat16), g) for p, g in zip(probs, grads)]
            gscores = [(p * (g - jnp.sum(p * g, axis=0, keepdims=True))).astype(jnp.bfloat16)
                       for p, g in zip(probs, gprobs)]
            gkeys = [dot_nn(s, q) * 0.125 for s, q in zip(gscores, queries)]
            gqueries = [merge_heads(dot_tn(s, k)) * 0.125 for s, k in zip(gscores, keys)]
            for c, gq, gk, gv in zip(starts, gqueries, gkeys, gvalues):
                gqkv[rows, c:c + 128] = gq.astype(jnp.bfloat16)
                gqkv[rows, D + c:D + c + 128] = gk.astype(jnp.bfloat16)
                gqkv[rows, 2 * D + c:2 * D + c + 128] = gv.astype(jnp.bfloat16)

    def grad_w_qkv(i):
        col = (i % 3) * 1024 + (i // 3) * 512
        part = dot_tn(normed[...], gqkv[:, col:col + 512])
        slots[QKV_SLOT[i]] = part.astype(jnp.bfloat16).reshape(2, 2, 4, 2, 32, 512)

    zero = jnp.zeros((1, D), jnp.float32)
    totals = [zero] * 4

    def input_back(h):
        if h == 0:
            load_wqkv.wait()
        rows512 = pl.ds(h * 512, 512)
        gnormed = dot_nt(gqkv[rows512, :], qkv[...])
        gafter2 = gnormed

        xhat, rstd = norm_stats(tok[rows512, :].astype(jnp.float32) + cond[rows512, :].astype(jnp.float32))
        y = gafter2 * vec_ref[0:1, :]
        m1 = jnp.mean(y, axis=-1, keepdims=True)
        m2 = jnp.mean(y * xhat, axis=-1, keepdims=True)
        normed[rows512, :] = (gafter[rows512, :] + rstd * (y - m1 - xhat * m2)).astype(jnp.bfloat16)
        add = (jnp.sum(gafter2 * xhat, axis=0, keepdims=True), jnp.sum(gafter2, axis=0, keepdims=True),
               jnp.sum(gqkv[rows512, :D].astype(jnp.float32), axis=0, keepdims=True),
               jnp.sum(gqkv[rows512, 2 * D:].astype(jnp.float32), axis=0, keepdims=True))
        for i in range(4):
            totals[i] = totals[i] + add[i]
        pltpu.make_async_copy(normed.at[rows512, :], gin_hbm.at[rows512, :], dsem.at[h]).start()

    def fill_small():
        gain1, shift1, qbias, vbias = totals
        eight = jnp.concatenate([gain1, sums_ref[0:1], shift1, qbias, vbias, sums_ref[3:4], sums_ref[1:2], sums_ref[2:3]],
                                axis=0)
        for device in range(32):
            g = device // 4
            w, s = device // 8, device % 8
            at = (w // 2, w % 2, s // 2, s % 2)
            own[at + (slice(0, 8),)] = eight[:, g * 128:(g + 1) * 128]
            own[at + (slice(8, 16),)] = jnp.broadcast_to(fcb_ref[:, device * 128:(device + 1) * 128], (8, 128))

    work = {0: [grad_w_out], 1: [grad_mixed], 2: [functools.partial(attention_back, 0, 0, 8)],
            3: [functools.partial(grad_w_qkv, i) for i in range(3)],
            4: [functools.partial(attention_back, 1, 0, 8), load_wqkv.start],
            5: [functools.partial(grad_w_qkv, i) for i in range(3, 6)],
            6: [functools.partial(input_back, 0)], 7: [functools.partial(input_back, 1), fill_small]}
    for step in range(last_step + 1):
        for f in work.get(step, ()):
            f()
        for stage_no in (4, 3, 2, 1, 0):
            for number, (p, steps) in enumerate(agenda):
                if steps[stage_no] == step:
                    if stage_no == 0 and number < 8:
                        down_loads[number].wait()
                    if stage_no == 0 and 8 <= number < 16:
                        pl.semaphore_wait(credit.at[number - 8], 1)
                    p.tick(stage_no)
                    if stage_no == 1 and number < 8:
                        pl.semaphore_signal(credit.at[number], inc=1, device_id=place.partner("c"), device_id_type=MESH)
                    if stage_no == 4:
                        p.finish()
    for h in range(2):
        rows512 = pl.ds(h * 512, 512)
        pltpu.make_async_copy(normed.at[rows512, :], gin_hbm.at[rows512, :], dsem.at[h]).wait()


DOWN_STEPS = [[s + o for o in range(5)] for s in (0, 0, 0, 1, 1, 1, 2, 2)]
OUT_STEPS = ((2, 3, 4, 5, 6), (3, 4, 5, 6, 7))
QKV_STEPS = ((3, 4, 6, 7, 8), (5, 6, 8, 9, 10))
QKV_SLOT = (10, 11, 12, 0, 1, 2)
SMALL_STEPS = (7, 8, 9, 10, 11)


def backward(gafter, qkv, mixed, tok, cond, wqkv, wout, gdown, vecs, sums, fcb):
    any_ = pl.BlockSpec(memory_space=pl.ANY)
    vmem = pl.BlockSpec(memory_space=pltpu.VMEM)
    bf, f32 = jnp.bfloat16, jnp.float32
    dma = pltpu.SemaphoreType.DMA
    return pl.pallas_call(
        backward_kernel,
        out_shape=[jax.ShapeDtypeStruct((D, D), bf), jax.ShapeDtypeStruct((32, 3 * D), f32),
                   jax.ShapeDtypeStruct((32, D), f32), jax.ShapeDtypeStruct((128, D), f32),
                   jax.ShapeDtypeStruct((16, 128), f32)],
        in_specs=[any_] * 8 + [vmem] * 3,
        out_specs=[any_] + [vmem] * 4,
        scratch_shapes=[pltpu.VMEM((D, D), f32), pltpu.VMEM((D, D), bf), pltpu.VMEM((D, D), bf),
                        pltpu.VMEM((D, 3 * D), bf), pltpu.VMEM((D, 3 * D), bf), pltpu.VMEM((D, D), bf),
                        pltpu.VMEM((D, D), bf), pltpu.VMEM((D, D), bf),
                        pltpu.VMEM((13, 2, 2, 4, 2, 32, 512), bf), pltpu.VMEM((2, 2, 4, 2, 16, 128), f32),
                        dma((7,)), dma((8,))]
        + scatter_bufs(16, 32, 512, cores=8) + scatter_bufs(1, 16, 128, f32)
        + [pltpu.SemaphoreType.REGULAR((8,))],
        compiler_params=pltpu.CompilerParams(collective_id=1, has_side_effects=True, vmem_limit_bytes=63 << 20),
    )(gafter, qkv, mixed, tok, cond, wqkv, wout, gdown, vecs, sums, fcb)


def own_sums(small):
    seq = lax.axis_index("seq")
    mine = lax.dynamic_slice(small, (0, (seq % 4) * 32), (8, 32))
    return mine[:2], mine[2:], small[8]


def plain_body(
    tokens,
    condition,
    valid_mask,
    w_qkv,
    w_out,
    w_fc,
    w_down,
    norm_gains,
    biases,
    fc_bias,
    cotangent,
):
    window_count, span_rows, model_width = tokens.shape
    row_total = window_count * span_rows
    head_size = model_width // HEADS
    head_shape = (row_total // BLOCK, BLOCK, HEADS, head_size)
    keep_rows = valid_mask.reshape(row_total, 1).astype(jnp.float32)
    hidden = tokens.reshape(row_total, model_width).astype(jnp.float32) + condition.reshape(
        row_total, model_width
    ).astype(jnp.float32)
    full_qkv, full_out, full_gains, full_biases = (
        lax.all_gather(w_qkv, ("win", "seq"), axis=0, tiled=True),
        lax.all_gather(w_out, ("win", "seq"), axis=0, tiled=True),
        lax.all_gather(norm_gains, ("win", "seq"), axis=1, tiled=True),
        lax.all_gather(biases, ("win", "seq"), axis=1, tiled=True),
    )
    gain_f = full_gains.astype(jnp.float32)
    bias_f = full_biases.astype(jnp.float32)
    normed_f, norm_back_one = jax.vjp(layer_norm, hidden, gain_f[0], bias_f[0])
    normed = normed_f.astype(jnp.bfloat16)
    projected = jnp.dot(normed, full_qkv, preferred_element_type=jnp.float32)
    queries = (projected[:, :model_width] + bias_f[1]).astype(jnp.bfloat16).reshape(head_shape)
    key_rows = projected[:, model_width : 2 * model_width].astype(jnp.bfloat16).reshape(head_shape)
    values = (projected[:, 2 * model_width :] + bias_f[2]).astype(jnp.bfloat16).reshape(head_shape)
    scores = masked_scores(queries, key_rows)
    row_max = jnp.max(scores, axis=-1, keepdims=True)
    log_total = row_max + jnp.log(jnp.sum(jnp.exp(scores - row_max), axis=-1, keepdims=True))
    probs = jnp.exp(scores - log_total).astype(jnp.bfloat16)
    mixed = jnp.einsum("bhqk,bkhd->bqhd", probs, values, preferred_element_type=jnp.float32)
    mixed = mixed.reshape(row_total, model_width).astype(jnp.bfloat16)
    after_attn = hidden + jnp.dot(mixed, full_out, preferred_element_type=jnp.float32) + bias_f[3]
    full_fc, full_down, full_fc_bias = (
        lax.all_gather(w_fc, ("win", "seq"), axis=0, tiled=True),
        lax.all_gather(w_down, ("win", "seq"), axis=0, tiled=True),
        lax.all_gather(fc_bias, ("win", "seq"), axis=0, tiled=True),
    )
    normed_two_f, norm_back_two = jax.vjp(layer_norm, after_attn, gain_f[1], bias_f[4])
    normed_two = normed_two_f.astype(jnp.bfloat16)
    pre_gelu = jnp.dot(
        normed_two, full_fc, preferred_element_type=jnp.float32
    ) + full_fc_bias.astype(jnp.float32)
    gelu_f, gelu_back = jax.vjp(partial(jax.nn.gelu, approximate=False), pre_gelu)
    gelu_out = gelu_f.astype(jnp.bfloat16)
    final_rows = (
        after_attn + jnp.dot(gelu_out, full_down, preferred_element_type=jnp.float32) + bias_f[5]
    )
    output = (final_rows * keep_rows).astype(jnp.bfloat16).reshape(tokens.shape)
    back_fc, back_down = (
        lax.all_gather(w_fc, ("win", "seq"), axis=0, tiled=True),
        lax.all_gather(w_down, ("win", "seq"), axis=0, tiled=True),
    )
    grad_final = cotangent.reshape(row_total, model_width).astype(jnp.float32) * keep_rows
    grad_mlp = grad_final.astype(jnp.bfloat16)
    grad_down_local = outer_sum(gelu_out, grad_mlp)
    grad_down_bias = jnp.sum(grad_mlp.astype(jnp.float32), axis=0)
    grad_gelu = times_transposed(grad_mlp, back_down)
    grad_pre = gelu_back(grad_gelu)[0].astype(jnp.bfloat16)
    grad_fc_local = outer_sum(normed_two, grad_pre)
    grad_fc_bias_local = jnp.sum(grad_pre.astype(jnp.float32), axis=0)
    grad_w_fc, grad_w_down, grad_fc_bias = (
        lax.psum_scatter(grad_fc_local, ("win", "seq"), scatter_dimension=0, tiled=True),
        lax.psum_scatter(grad_down_local, ("win", "seq"), scatter_dimension=0, tiled=True),
        lax.psum_scatter(grad_fc_bias_local, ("win", "seq"), scatter_dimension=0, tiled=True),
    )
    grad_normed_two = times_transposed(grad_pre, back_fc)
    grad_after_norm, grad_gain_two, grad_shift_two = norm_back_two(grad_normed_two)
    grad_after = grad_final + grad_after_norm
    back_qkv, back_out = (
        lax.all_gather(w_qkv, ("win", "seq"), axis=0, tiled=True),
        lax.all_gather(w_out, ("win", "seq"), axis=0, tiled=True),
    )
    grad_attn = grad_after.astype(jnp.bfloat16)
    grad_out_local = outer_sum(mixed, grad_attn)
    grad_out_bias = jnp.sum(grad_attn.astype(jnp.float32), axis=0)
    grad_mixed = times_transposed(grad_attn, back_out).astype(jnp.bfloat16).reshape(head_shape)
    probs_full = jnp.exp(masked_scores(queries, key_rows) - log_total)
    grad_probs = jnp.einsum(
        "bqhd,bkhd->bhqk", grad_mixed, values, preferred_element_type=jnp.float32
    )
    grad_values = jnp.einsum(
        "bhqk,bqhd->bkhd", probs, grad_mixed, preferred_element_type=jnp.float32
    )
    grad_values = grad_values.reshape(row_total, model_width).astype(jnp.bfloat16)
    grad_scores = probs_full * (
        grad_probs - jnp.sum(probs_full * grad_probs, axis=-1, keepdims=True)
    )
    grad_scores = grad_scores.astype(jnp.bfloat16)
    grad_queries = (
        jnp.einsum("bhqk,bkhd->bqhd", grad_scores, key_rows, preferred_element_type=jnp.float32)
        * 0.125
    )
    grad_keys = (
        jnp.einsum("bhqk,bqhd->bkhd", grad_scores, queries, preferred_element_type=jnp.float32)
        * 0.125
    )
    grad_queries = grad_queries.reshape(row_total, model_width).astype(jnp.bfloat16)
    grad_keys = grad_keys.reshape(row_total, model_width).astype(jnp.bfloat16)
    grad_query_bias = jnp.sum(grad_queries.astype(jnp.float32), axis=0)
    grad_value_bias = jnp.sum(grad_values.astype(jnp.float32), axis=0)
    grad_projected = jnp.concatenate([grad_queries, grad_keys, grad_values], axis=1)
    grad_qkv_local = outer_sum(normed, grad_projected)
    grad_normed = times_transposed(grad_projected, back_qkv)
    grad_hidden_norm, grad_gain_one, grad_shift_one = norm_back_one(grad_normed)
    grad_input = (grad_after + grad_hidden_norm).astype(jnp.bfloat16).reshape(tokens.shape)
    gains_local = jnp.stack([grad_gain_one, grad_gain_two])
    biases_local = jnp.stack(
        [
            grad_shift_one,
            grad_query_bias,
            grad_value_bias,
            grad_out_bias,
            grad_shift_two,
            grad_down_bias,
        ]
    )
    grad_w_qkv, grad_w_out, grad_gains, grad_biases = (
        lax.psum_scatter(grad_qkv_local, ("win", "seq"), scatter_dimension=0, tiled=True),
        lax.psum_scatter(grad_out_local, ("win", "seq"), scatter_dimension=0, tiled=True),
        lax.psum_scatter(gains_local, ("win", "seq"), scatter_dimension=1, tiled=True),
        lax.psum_scatter(biases_local, ("win", "seq"), scatter_dimension=1, tiled=True),
    )
    return (
        output,
        grad_input,
        grad_w_qkv,
        grad_w_out,
        grad_w_fc,
        grad_w_down,
        grad_gains,
        grad_biases,
        grad_fc_bias,
    )


GATHER_ORDER = (2, 0, 2, 2, 1, 2)


def body(
    tokens,
    condition,
    valid_mask,
    w_qkv,
    w_out,
    w_fc,
    w_down,
    norm_gains,
    biases,
    fc_bias,
    cotangent,
):
    tok, cond, cot = (a.reshape(D, D) for a in (tokens, condition, cotangent))
    keep_rows = valid_mask.reshape(D, 1).astype(jnp.float32)
    shards = (own_small(norm_gains, biases, fc_bias), w_qkv, w_out, w_fc, w_down)
    _, full_qkv, full_out, full_fc, full_down, qkv, mixed, after, vecs, full_fc_bias = gather_and_attend(
        shards, tok, cond
    )
    output, grad_after, grad_down_local, grad_w_fc, two_sums, fc_bias_sums = mlp(
        True, after, cot, keep_rows, vecs, full_fc_bias, full_fc.reshape(D, FF), full_down.reshape(FF, D)
    )
    grad_input, grad_w_qkv, grad_w_out, grad_w_down, small = backward(
        grad_after,
        qkv,
        mixed,
        tok,
        cond,
        full_qkv.reshape(D, 3 * D),
        full_out.reshape(D, D),
        grad_down_local.reshape(2, 2, 4, 2, 128, D),
        vecs,
        two_sums,
        fc_bias_sums,
    )
    grad_gains, grad_biases, grad_fc_bias = own_sums(small)
    return (
        output.reshape(tokens.shape),
        grad_input.reshape(tokens.shape),
        grad_w_qkv,
        grad_w_out,
        grad_w_fc,
        grad_w_down,
        grad_gains,
        grad_biases,
        grad_fc_bias,
    )


def solution(mesh):
    fast = mesh.shape["win"] == 4 and mesh.shape["seq"] == 8
    return jax.shard_map(
        body if fast else plain_body,
        mesh=mesh,
        in_specs=(
            P("win", "seq", None),
            P("win", "seq", None),
            P("win", "seq"),
            P(("win", "seq"), None),
            P(("win", "seq"), None),
            P(("win", "seq"), None),
            P(("win", "seq"), None),
            P(None, ("win", "seq")),
            P(None, ("win", "seq")),
            P(("win", "seq")),
            P("win", "seq", None),
        ),
        out_specs=(
            P("win", "seq", None),
            P("win", "seq", None),
            P(("win", "seq"), None),
            P(("win", "seq"), None),
            P(("win", "seq"), None),
            P(("win", "seq"), None),
            P(None, ("win", "seq")),
            P(None, ("win", "seq")),
            P(("win", "seq")),
        ),
        check_vma=False,
    )
```

```python
import functools
from functools import partial

import jax
import jax.numpy as jnp
from jax import lax
from jax.experimental import pallas as pl
from jax.experimental.pallas import tpu as pltpu
from jax.sharding import PartitionSpec as P

MESH = pl.DeviceIdType.MESH
ALL = slice(None)


class Place:
    def __init__(self):
        win, seq = lax.axis_index("win"), lax.axis_index("seq")
        self.y, self.x = win // 2, win % 2
        self.z, self.c = seq // 2, seq % 2

    def device(self, y=None, x=None, z=None, c=None):
        y = self.y if y is None else y
        x = self.x if x is None else x
        z = self.z if z is None else z
        c = self.c if c is None else c
        return (y * 2 + x, z * 2 + c)

    def partner(self, dim):
        if dim == "x":
            return self.device(x=1 - self.x)
        if dim == "y":
            return self.device(y=1 - self.y)
        return self.device(c=1 - self.c)


def greet(place):
    barrier = pltpu.get_barrier_semaphore()
    others = [place.partner(dim) for dim in "xyc"]
    others += [place.device(z=(place.z + t) % 4) for t in (1, 2, 3)]
    for device in others:
        pl.semaphore_signal(barrier, inc=1, device_id=device, device_id_type=MESH)
    pl.semaphore_wait(barrier, 6)


def guarded(cond, thunk):
    if cond is None:
        thunk()
    else:
        pl.when(cond)(thunk)


class Gather:
    def __init__(self, place, view, order, send, recv, slack=0):
        self.p, self.view, self.send, self.recv = place, view, send, recv
        self.order, self.sent = order, []
        self.ticks = self.plan(slack)

    def region(self, got, **at):
        p = self.p
        pick = lambda d, own: at[d] if d in at else (ALL if d in got else own)
        return self.view(pick("y", p.y), pick("x", p.x), pick("z", p.z), at.get("c", p.c))

    def copy(self, region, device, number):
        return pltpu.make_async_remote_copy(
            region, region, self.send.at[number], self.recv.at[number],
            device_id=device, device_id_type=MESH)

    def push(self, cond, make, device, number):
        def go():
            self.copy(make(), device, number).start()
        guarded(cond, go)

        def end():
            self.copy(make(), device, number).wait_send()
        self.sent.append((cond, end))

    def take(self, cond, make, number):
        def go():
            self.copy(make(), self.p.device(c=1 - self.p.c), number).wait_recv()
        guarded(cond, go)

    def both(self, cond, other):
        return other if cond is None else jnp.logical_and(cond, other)

    def line(self, got, tick, cond):
        z = self.p.z
        if tick > 0:
            self.take(self.both(cond, z >= tick), lambda: self.region(got, z=z - tick), 1 + tick)
            self.take(self.both(cond, z + tick <= 3), lambda: self.region(got, z=z + tick), 4 + tick)
        if tick < 3:
            self.push(self.both(cond, jnp.logical_and(z >= tick, z < 3)),
                      lambda: self.region(got, z=z - tick), self.p.device(z=z + 1), 2 + tick)
            self.push(self.both(cond, jnp.logical_and(z + tick <= 3, z > 0)),
                      lambda: self.region(got, z=z + tick), self.p.device(z=z - 1), 5 + tick)

    def plan(self, slack):
        out = []
        p = self.p
        orders = {0: (("xzy", None),), 1: (("yzx", None),),
                  2: (("zxy", p.c == 0), ("zyx", p.c == 1))}[self.order]
        lists = []
        for order, cond in orders:
            ticks = [[]]
            got = ""
            ex = 0
            for dim in order:
                if dim == "z":
                    for t in range(4):
                        ticks[-1].append(functools.partial(self.line, got, t, cond))
                        if t < 3:
                            ticks.append([])
                else:
                    ticks[-1].append(functools.partial(
                        self.push, cond, functools.partial(self.region, got), p.partner(dim), ex))
                    if ex == 1:
                        ticks.extend([] for _ in range(slack))
                    ticks.append([])
                    own = p.x if dim == "x" else p.y
                    ticks[-1].append(functools.partial(
                        self.take, cond, functools.partial(self.region, got, **{dim: 1 - own}), ex))
                    ex += 1
                got += dim
            ticks[-1].append(functools.partial(self.push, cond, functools.partial(self.region, "xyz"),
                                               p.partner("c"), 8))
            ticks.append([])
            ticks[-1].append(functools.partial(self.take, cond,
                                               functools.partial(self.region, "xyz", c=1 - p.c), 8))
            lists.append(ticks)
        n = max(len(t) for t in lists)
        for i in range(n):
            thunks = [f for t in lists if i < len(t) for f in t[i]]
            out.append(thunks)
        return out

    def tick(self, i):
        for f in self.ticks[i]:
            f()

    def finish(self):
        for cond, end in self.sent:
            guarded(cond, end)


def run_ticks(pieces, starts, between=None):
    last = max(s + len(p.ticks) for p, s in zip(pieces, starts))
    for now in range(last):
        for p, s in zip(pieces, starts):
            if 0 <= now - s < len(p.ticks):
                p.tick(now - s)
        if between and now in between:
            between[now]()
    for p in pieces:
        p.finish()


class Scatter:
    def __init__(self, place, slot, bufs, order, send, recv, put):
        self.p, self.slot, self.bufs, self.put = place, slot, bufs, put
        self.send, self.recv, self.sent = send, recv, []
        self.ticks = self.plan(order)

    def region(self, left, **at):
        p = self.p
        pick = lambda d, own: at[d] if d in at else (ALL if d in left else own)
        return self.slot.at[pick("y", p.y), pick("x", p.x), pick("z", p.z), at.get("c", p.c)]

    def push(self, cond, make, buf, device, number):
        def copy():
            return pltpu.make_async_remote_copy(
                make(), buf, self.send.at[number], self.recv.at[number],
                device_id=device, device_id_type=MESH)
        guarded(cond, lambda: copy().start())
        self.sent.append((cond, lambda: copy().wait_send()))

    def take(self, cond, makes, bufs, numbers, last):
        def go():
            for buf, number in zip(bufs, numbers):
                pltpu.make_async_remote_copy(
                    buf, buf, self.send.at[number], self.recv.at[number],
                    device_id=self.p.partner("c"), device_id_type=MESH).wait_recv()
            region = makes()
            shape = region.shape
            outer = [()]
            while len(shape) - len(outer[0]) > 3:
                outer = [o + (i,) for o in outer for i in range(shape[len(o)])]
            for o in outer:
                many = last or len(bufs) > 1
                total = region[o + (Ellipsis,)]
                total = total.astype(jnp.float32) if many else total
                for buf in bufs:
                    total = total + buf[o + (Ellipsis,)].astype(total.dtype)
                if last:
                    self.put(total)
                else:
                    region[o + (Ellipsis,)] = total.astype(region.dtype)
        guarded(cond, go)

    def plan(self, order):
        p = self.p
        core, first, second, line = self.bufs
        variants = {0: (("yzx", None),), 1: (("xzy", None),),
                    2: (("yxz", p.c == 0), ("xyz", p.c == 1))}[order]
        ticks = [[] for _ in range(5)]
        for dims, cond in variants:
            left = "xyz"
            ticks[0].append(functools.partial(
                self.push, cond, lambda: self.region("xyz", c=1 - p.c), core, p.partner("c"), 0))
            ticks[1].append(functools.partial(
                self.take, cond, lambda: self.region("xyz"), [core], [0], False))
            for i, dim in enumerate(dims):
                rest = left.replace(dim, "")
                last = i == 2
                mine = functools.partial(self.region, rest)
                if dim == "z":
                    bufs = [line.at[t - 1] if rest else line.at[t - 1, 0] for t in (1, 2, 3)]
                    for t in (1, 2, 3):
                        to = (p.z + t) % 4
                        ticks[i + 1].append(functools.partial(
                            self.push, cond, functools.partial(self.region, rest, z=to),
                            bufs[t - 1], p.device(z=to), 2 + t))
                    ticks[i + 2].append(functools.partial(
                        self.take, cond, mine, bufs, [3, 4, 5], last))
                else:
                    buf = first if i == 0 else (second if i == 1 else second.at[0])
                    number = 1 if i == 0 else 2
                    own = p.x if dim == "x" else p.y
                    ticks[i + 1].append(functools.partial(
                        self.push, cond, functools.partial(self.region, rest, **{dim: 1 - own}),
                        buf, p.partner(dim), number))
                    ticks[i + 2].append(functools.partial(
                        self.take, cond, mine, [buf], [number], last))
                left = rest
        return ticks

    def tick(self, i):
        for f in self.ticks[i]:
            f()

    def finish(self):
        for cond, end in self.sent:
            guarded(cond, end)


SCATTER_SEMS = 6
GATHER_SEMS = 9


def scatter_bufs(count, rows, cols, dtype=jnp.bfloat16, cores=None):
    return [pltpu.VMEM((cores or count, 2, 2, 4, rows, cols), dtype), pltpu.VMEM((count, 2, 4, rows, cols), dtype),
            pltpu.VMEM((count, 4, rows, cols), dtype), pltpu.VMEM((count, 3, 2, rows, cols), dtype),
            pltpu.SemaphoreType.DMA((count, SCATTER_SEMS)), pltpu.SemaphoreType.DMA((count, SCATTER_SEMS))]


D, FF, CH = 1024, 4096, 512
DELAY = (0, 1, 4, 6, 8)
TILE = 256


def dot_nn(a, b):
    return lax.dot_general(a, b, (((1,), (0,)), ((), ())), preferred_element_type=jnp.float32)


def dot_nt(a, b):
    return lax.dot_general(a, b, (((1,), (1,)), ((), ())), preferred_element_type=jnp.float32)


def dot_tn(a, b):
    return lax.dot_general(a, b, (((0,), (0,)), ((), ())), preferred_element_type=jnp.float32)


def norm_stats(rows_in):
    mean = jnp.mean(rows_in, axis=-1, keepdims=True)
    centered = rows_in - mean
    var = jnp.mean(centered * centered, axis=-1, keepdims=True)
    rstd = lax.rsqrt(var + 1e-05)
    return centered * rstd, rstd


def gelu_both(v):
    phi = 0.5 + 0.5 * lax.erf(v * 0.7071067811865476)
    slope = phi + v * (jnp.exp(-0.5 * v * v) * 0.3989422804014327)
    return (v * phi).astype(jnp.bfloat16), slope


def mlp_kernel(comm, after_hbm, n2_hbm, gm_hbm, mask_ref, vec_ref, fcb_ref, wfc_hbm, wdn_hbm,
               out_ref, gafter_hbm, gdown_hbm, gfc_ref, small_ref, gfcb_ref,
               after, gm, n2, gelu, gp, fin, gn2, wfc, wdn, stage, slots, lsem, wsem, ssem, *rest):
    place = Place()
    if comm:
        greet(place)
    load_after = pltpu.make_async_copy(after_hbm, after, lsem.at[0])
    load_gm = pltpu.make_async_copy(gm_hbm, gm, lsem.at[1])
    load_n2 = pltpu.make_async_copy(n2_hbm, n2, lsem.at[2])
    load_n2.start()

    def fetch_fc(j):
        return pltpu.make_async_copy(wfc_hbm.at[:, pl.ds(j * CH, CH)], wfc.at[j % 2], wsem.at[j % 2, 0])

    def fetch_down(i):
        j = i % (FF // CH)
        return pltpu.make_async_copy(wdn_hbm.at[pl.ds(j * CH, CH), :], wdn.at[i % 2], wsem.at[i % 2, 1])

    fetch_fc(0).start()
    fetch_down(0).start()
    load_gm.start()
    load_after.start()

    @pl.loop(0, D // 128)
    def _(i):
        rows = pl.ds(pl.multiple_of(i * 128, 128), 128)
        fin[rows, :] = jnp.zeros((128, D), jnp.float32)
        gn2[rows, :] = jnp.zeros((128, D), jnp.float32)

    load_n2.wait()
    load_gm.wait()
    n = FF // CH

    def store(j):
        return pltpu.make_async_copy(stage.at[j % 2], gdown_hbm.at[pl.ds(j * CH, CH), :], ssem.at[j % 2])

    pieces = []
    if comm:
        bufs = rest
        for j in range(n):
            def put(value, j=j):
                gfc_ref[:, pl.ds(j * CH, CH)] = value

            pieces.append(Scatter(place, slots.at[j], [b.at[j] for b in bufs[:4]],
                                  GATHER_ORDER[j % 6], bufs[4].at[j], bufs[5].at[j], put))

    def advance(step, first, last):
        if comm:
            for now in range(first, last):
                @pl.when(step == now)
                def _(now=now):
                    for stage_no in (4, 3, 2, 1, 0):
                        j = now - DELAY[stage_no]
                        if 0 <= j < n:
                            pieces[j].tick(stage_no)
                            if stage_no == 4:
                                pieces[j].finish()

    @pl.loop(0, n)
    def _(j):
        s = j % 2
        fetch_fc(j).wait()
        fetch_down(j).wait()
        fetch_down(j + 1).start()

        @pl.when(j + 1 < n)
        def _():
            fetch_fc(j + 1).start()

        cols = pl.ds(pl.multiple_of(j * CH, CH), CH)
        pre = dot_nn(n2[...], wfc[s]) + fcb_ref[:, cols]
        act, slope = gelu_both(pre)
        grad = (dot_nt(gm[...], wdn[s]) * slope).astype(jnp.bfloat16)
        gelu[:, cols] = act
        gp[...] = grad
        gfcb_ref[:, cols] = jnp.sum(grad.astype(jnp.float32), axis=0, keepdims=True)
        gn2[...] += dot_nt(gp[...], wfc[s])
        slots[j] = dot_tn(n2[...], gp[...]).astype(jnp.bfloat16).reshape(2, 2, 4, 2, 32, CH)
        advance(j, 0, n)

    @pl.loop(0, n)
    def _(j):
        s = j % 2
        fetch_down(j + n).wait()

        @pl.when(j + 1 < n)
        def _():
            fetch_down(j + n + 1).start()

        @pl.when(j >= 2)
        def _():
            store(j - 2).wait()

        cols = pl.ds(pl.multiple_of(j * CH, CH), CH)
        fin[...] += dot_nn(gelu[:, cols], wdn[s])
        stage[s] = dot_tn(gelu[:, cols], gm[...]).astype(jnp.bfloat16)
        store(j).start()
        advance(j + n, n, 2 * n)

    store(n - 2).wait()
    store(n - 1).wait()

    def norm_step(i, sums):
        rows = pl.ds(pl.multiple_of(i * 128, 128), 128)
        xhat, rstd = norm_stats(after[rows, :])
        keep = mask_ref[rows, :]
        out_ref[rows, :] = ((after[rows, :] + fin[rows, :] + vec_ref[7:8, :]) * keep).astype(jnp.bfloat16)
        g = gn2[rows, :]
        y = g * vec_ref[1:2, :]
        m1 = jnp.mean(y, axis=-1, keepdims=True)
        m2 = jnp.mean(y * xhat, axis=-1, keepdims=True)
        gmf = gm[rows, :].astype(jnp.float32)
        ga = gmf + rstd * (y - m1 - xhat * m2)
        fin[rows, :] = ga
        gattn = ga.astype(jnp.bfloat16).astype(jnp.float32)
        return tuple(s + jnp.sum(v, axis=0, keepdims=True)
                     for s, v in zip(sums, (g * xhat, g, gmf, gattn)))

    def half(h):
        return pltpu.make_async_copy(fin.at[pl.ds(h * 512, 512), :], gafter_hbm.at[pl.ds(h * 512, 512), :], lsem.at[h])

    zero = jnp.zeros((1, D), jnp.float32)
    load_after.wait()
    sums = lax.fori_loop(0, D // 256, norm_step, (zero,) * 4)
    half(0).start()
    sums = lax.fori_loop(D // 256, D // 128, norm_step, sums)
    half(1).start()
    for i in range(4):
        small_ref[i:i + 1, :] = sums[i]
    half(0).wait()
    half(1).wait()


def mlp(comm, after, n2, gm, mask, vecs, fcb, wfc, wdn):
    n = FF // CH
    any_ = pl.BlockSpec(memory_space=pl.ANY)
    vmem = pl.BlockSpec(memory_space=pltpu.VMEM)
    return pl.pallas_call(
        functools.partial(mlp_kernel, comm),
        out_shape=[jax.ShapeDtypeStruct((D, D), jnp.bfloat16), jax.ShapeDtypeStruct((D, D), jnp.float32),
                   jax.ShapeDtypeStruct((FF, D), jnp.bfloat16), jax.ShapeDtypeStruct((32, FF), jnp.float32),
                   jax.ShapeDtypeStruct((8, D), jnp.float32), jax.ShapeDtypeStruct((1, FF), jnp.float32)],
        in_specs=[any_, any_, any_, vmem, vmem, vmem, any_, any_],
        out_specs=[vmem, any_, any_, vmem, vmem, vmem],
        scratch_shapes=[pltpu.VMEM((D, D), jnp.float32), pltpu.VMEM((D, D), jnp.bfloat16),
                        pltpu.VMEM((D, D), jnp.bfloat16),
                        pltpu.VMEM((D, FF), jnp.bfloat16), pltpu.VMEM((D, CH), jnp.bfloat16),
                        pltpu.VMEM((D, D), jnp.float32), pltpu.VMEM((D, D), jnp.float32),
                        pltpu.VMEM((2, D, CH), jnp.bfloat16), pltpu.VMEM((2, CH, D), jnp.bfloat16),
                        pltpu.VMEM((2, CH, D), jnp.bfloat16),
                        pltpu.VMEM((n, 2, 2, 4, 2, 32, CH), jnp.bfloat16),
                        pltpu.SemaphoreType.DMA((3,)), pltpu.SemaphoreType.DMA((2, 2)), pltpu.SemaphoreType.DMA((2,))]
        + (scatter_bufs(n, 32, CH) if comm else []),
        compiler_params=pltpu.CompilerParams(vmem_limit_bytes=60 << 20,
            **(dict(collective_id=2, has_side_effects=True) if comm else {})),
    )(after, n2, gm, mask, vecs, fcb, wfc, wdn)


HEADS = 16
BLOCK = 128


def layer_norm(rows_in, gain_vec, shift_vec):
    row_mean = jnp.mean(rows_in, axis=-1, keepdims=True)
    centered = rows_in - row_mean
    row_var = jnp.mean(centered * centered, axis=-1, keepdims=True)
    return centered * lax.rsqrt(row_var + 1e-05) * gain_vec + shift_vec


def outer_sum(first, second):
    return lax.dot_general(
        first, second, (((0,), (0,)), ((), ())), preferred_element_type=jnp.float32
    )


def times_transposed(first, second):
    return lax.dot_general(
        first, second, (((1,), (1,)), ((), ())), preferred_element_type=jnp.float32
    )


def masked_scores(queries_h, keys_h):
    scores = (
        jnp.einsum("bqhd,bkhd->bhqk", queries_h, keys_h, preferred_element_type=jnp.float32) * 0.125
    )
    causal = lax.broadcasted_iota(jnp.int32, scores.shape, 2) >= lax.broadcasted_iota(
        jnp.int32, scores.shape, 3
    )
    return jnp.where(causal, scores, -1e30)


def lane_low(shape):
    return lax.broadcasted_iota(jnp.int32, shape, len(shape) - 1) < 64


def stack_heads(pair):
    low = lane_low(pair.shape)
    zero = jnp.zeros_like(pair)
    return jnp.concatenate([jnp.where(low, pair, zero), jnp.where(low, zero, pair)], axis=0)


def merge_heads(stacked):
    half = stacked.shape[0] // 2
    return jnp.where(lane_low((half, stacked.shape[1])), stacked[:half], stacked[half:])


def softmax_keys(key2, query2):
    scores = dot_nt(key2, query2)
    key = lax.broadcasted_iota(jnp.int32, scores.shape, 0)
    query = lax.broadcasted_iota(jnp.int32, scores.shape, 1) % BLOCK
    scores = jnp.where(key <= query, scores, -1e30)
    top = jnp.max(scores, axis=0, keepdims=True)
    raised = jnp.exp((scores - top) * 0.125)
    return raised * (1.0 / jnp.sum(raised, axis=0, keepdims=True))


GATHER_CUTS = ([(0, (0, 16), (0, 128))]
               + [(1, (0, 32), (i * 512, 512)) for i in range(6)]
               + [(2, (0, 32), (i * 512, 512)) for i in range(2)]
               + [(3, (0, 32), (i * 512, 512)) for i in range(8)]
               + [(4, (i * 16, 16), (0, 1024)) for i in range(8)])


def gather_kernel(small, wqkv_s, wout_s, wfc_s, wdn_s, tok_hbm, cond_hbm, cot_hbm, mask_ref,
                  small_f, wqkv_f, wout_f, wfc_f, wdn_f, qkv_hbm, mixed_hbm, after_hbm, n2_hbm, gm_hbm, vec_ref, fcb_ref,
                  tok, cond, hidden, normed, wqkv, wout, qkv, mixed, smallv,
                  send, recv, own_sem, lsem, wsem, osem):
    ins = (small, wqkv_s, wout_s, wfc_s, wdn_s)
    fulls = (small_f, wqkv_f, wout_f, wfc_f, wdn_f)
    place = Place()
    greet(place)
    own = [pltpu.make_async_copy(s, f.at[place.y, place.x, place.z, place.c], own_sem.at[i])
           for i, (s, f) in enumerate(zip(ins, fulls))]
    loads = [pltpu.make_async_copy(tok_hbm, tok, lsem.at[0]), pltpu.make_async_copy(cond_hbm, cond, lsem.at[1])]
    for c in own + loads:
        c.start()
    for c in own:
        c.wait()

    def make(k):
        n, (r0, r), (c0, w) = GATHER_CUTS[k]
        view = lambda y, x, z, c: fulls[n].at[y, x, z, c, pl.ds(r0, r), pl.ds(c0, w)]
        return Gather(place, view, k % 3, send.at[k], recv.at[k], 1)

    load_small = pltpu.make_async_copy(small_f, smallv, lsem.at[2])
    load_qkv = pltpu.make_async_copy(wqkv_f, wqkv, wsem.at[0])
    load_out = pltpu.make_async_copy(wout_f, wout, wsem.at[1])
    store_qkv = pltpu.make_async_copy(qkv, qkv_hbm, osem.at[0])
    store_mixed = pltpu.make_async_copy(mixed, mixed_hbm, osem.at[1])
    store_after = pltpu.make_async_copy(hidden, after_hbm, osem.at[2])

    def add_hidden():
        for c in loads:
            c.wait()

        @pl.loop(0, D // 128)
        def _(i):
            rows = pl.ds(pl.multiple_of(i * 128, 128), 128)
            hidden[rows, :] = tok[rows, :].astype(jnp.float32) + cond[rows, :].astype(jnp.float32)

    def first_norm():
        load_small.start()
        load_small.wait()
        for g in range(8):
            win, z0 = g // 2, (g % 2) * 2
            total = None
            for i in range(4):
                y, x, z, c = win // 2, win % 2, z0 + i // 2, i % 2
                one = smallv[y, x, z, c].astype(jnp.float32)
                device = g * 4 + i
                fcb_ref[:, device * 128:(device + 1) * 128] = one[8:9]
                total = one[:8] if total is None else total + one[:8]
            vec_ref[:, g * 128:(g + 1) * 128] = total

        @pl.loop(0, D // 128)
        def _(i):
            rows = pl.ds(pl.multiple_of(i * 128, 128), 128)
            xhat, _ = norm_stats(hidden[rows, :])
            normed[rows, :] = (xhat * vec_ref[0:1, :] + vec_ref[2:3, :]).astype(jnp.bfloat16)

    def project(first, last):
        for i in range(first, last):
            cols = slice(i * 512, (i + 1) * 512)
            weight = wqkv[:, :, :, :, :, cols].reshape(D, 512)
            part = dot_nn(normed[...], weight)
            if i < 2:
                part = part + vec_ref[3:4, cols]
            if i >= 4:
                part = part + vec_ref[4:5, i * 512 - 2048:i * 512 - 1536]
            qkv[:, cols] = part.astype(jnp.bfloat16)

    def attend(first, last):
        @pl.loop(first, last)
        def _(b):
            rows = pl.ds(pl.multiple_of(b * BLOCK, BLOCK), BLOCK)
            starts = range(0, D, 128)
            queries = [stack_heads(qkv[rows, c:c + 128]) for c in starts]
            keys = [qkv[rows, D + c:D + c + 128] for c in starts]
            values = [qkv[rows, 2 * D + c:2 * D + c + 128] for c in starts]
            probs = [softmax_keys(k, q).astype(jnp.bfloat16) for k, q in zip(keys, queries)]
            outs = [merge_heads(dot_tn(p, v)) for p, v in zip(probs, values)]
            for c, out in zip(starts, outs):
                mixed[rows, c:c + 128] = out.astype(jnp.bfloat16)

    def output_projection():
        load_out.wait()
        for i in range(2):
            cols = slice(i * 512, (i + 1) * 512)
            part = dot_nn(mixed[...], wout[:, :, :, :, :, cols].reshape(D, 512))
            hidden[:, cols] += part + vec_ref[5:6, cols]
        store_after.start()

    store_n2 = pltpu.make_async_copy(tok, n2_hbm, osem.at[3])
    store_gm = pltpu.make_async_copy(cond, gm_hbm, osem.at[4])
    load_cot = pltpu.make_async_copy(cot_hbm, cond, lsem.at[3])

    def mask_cotangent():
        load_cot.wait()

        @pl.loop(0, D // 128)
        def _(i):
            rows = pl.ds(pl.multiple_of(i * 128, 128), 128)
            cond[rows, :] = (cond[rows, :].astype(jnp.float32) * mask_ref[rows, :]).astype(jnp.bfloat16)

        store_gm.start()

    def second_norm():
        @pl.loop(0, D // 128)
        def _(i):
            rows = pl.ds(pl.multiple_of(i * 128, 128), 128)
            xhat, _ = norm_stats(hidden[rows, :])
            tok[rows, :] = (xhat * vec_ref[1:2, :] + vec_ref[6:7, :]).astype(jnp.bfloat16)

        store_n2.start()

    def step0():
        add_hidden()
        load_cot.start()

    def step8():
        load_qkv.wait()
        project(0, 6)
        store_qkv.start()

    def step7():
        load_qkv.start()

    def step9():
        load_out.start()
        attend(0, 4)

    def step10():
        attend(4, 8)
        store_mixed.start()

    between = {0: step0, 2: mask_cotangent, 7: first_norm, 8: step7, 9: step8, 10: step9, 11: step10,
               12: output_projection, 13: second_norm}
    run_ticks([make(k) for k in range(len(GATHER_CUTS))], [max(0, (k - 1) // 3) for k in range(len(GATHER_CUTS))], between)
    store_qkv.wait()
    store_mixed.wait()
    store_after.wait()
    store_n2.wait()
    store_gm.wait()


def gather_and_attend(shards, tok, cond, cot, mask):
    any_ = pl.BlockSpec(memory_space=pl.ANY)
    vmem = pl.BlockSpec(memory_space=pltpu.VMEM)
    count = len(GATHER_CUTS)
    bf, f32 = jnp.bfloat16, jnp.float32
    dma = pltpu.SemaphoreType.DMA
    return pl.pallas_call(
        gather_kernel,
        out_shape=[jax.ShapeDtypeStruct((2, 2, 4, 2) + s.shape, s.dtype) for s in shards]
        + [jax.ShapeDtypeStruct((D, 3 * D), bf), jax.ShapeDtypeStruct((D, D), bf), jax.ShapeDtypeStruct((D, D), f32),
           jax.ShapeDtypeStruct((D, D), bf), jax.ShapeDtypeStruct((D, D), bf),
           jax.ShapeDtypeStruct((8, D), f32), jax.ShapeDtypeStruct((1, FF), f32)],
        in_specs=[any_] * 8 + [vmem],
        out_specs=[any_] * 10 + [vmem] * 2,
        scratch_shapes=[pltpu.VMEM((D, D), bf), pltpu.VMEM((D, D), bf), pltpu.VMEM((D, D), f32), pltpu.VMEM((D, D), bf),
                        pltpu.VMEM((2, 2, 4, 2, 32, 3 * D), bf), pltpu.VMEM((2, 2, 4, 2, 32, D), bf),
                        pltpu.VMEM((D, 3 * D), bf), pltpu.VMEM((D, D), bf), pltpu.VMEM((2, 2, 4, 2, 16, 128), bf),
                        dma((count, GATHER_SEMS)), dma((count, GATHER_SEMS)), dma((5,)), dma((4,)), dma((2,)), dma((5,))],
        compiler_params=pltpu.CompilerParams(collective_id=0, has_side_effects=True, vmem_limit_bytes=60 << 20),
    )(*shards, tok, cond, cot, mask)


def own_small(gains, biases, fc_bias):
    seq = lax.axis_index("seq")
    eight = jnp.concatenate([gains, biases], axis=0)
    placed = jnp.where(jnp.arange(4)[None, :, None] == seq % 4, eight[:, None, :], 0).reshape(8, 128)
    return jnp.concatenate([placed, fc_bias.reshape(1, 128), jnp.zeros((7, 128), fc_bias.dtype)], axis=0)


DOWN_CUTS = [(r0, c0) for r0 in range(0, 128, 32) for c0 in (0, 512)]


def backward_kernel(gafter_hbm, qkv_hbm, mixed_hbm, tok_hbm, cond_hbm, wqkv_hbm, wout_hbm, gdown_hbm, vec_ref,
                    sums_ref, fcb_ref,
                    gin_hbm, gqkv_ref, gout_ref, gdown_ref, small_ref,
                    gafter, gattn, mixed, qkv, gqkv, tok, cond, normed, slots, own, lsem, dsem,
                    *rest):
    big, little, credit = rest[:6], rest[6:12], rest[12]
    place = Place()
    greet(place)
    loads = [pltpu.make_async_copy(s, d, lsem.at[i]) for i, (s, d) in enumerate((
        (gafter_hbm, gafter), (mixed_hbm, mixed), (wout_hbm, normed), (tok_hbm, tok), (cond_hbm, cond), (qkv_hbm, qkv)))]
    down_loads = [pltpu.make_async_copy(gdown_hbm.at[:, :, :, :, pl.ds(r0, 32), pl.ds(c0, 512)], slots.at[i], dsem.at[i])
                  for i, (r0, c0) in enumerate(DOWN_CUTS)]
    for c in down_loads[:2] + loads + down_loads[2:]:
        c.start()
    load_wqkv = pltpu.make_async_copy(wqkv_hbm, qkv, lsem.at[6])

    def piece(k, slot, put):
        return Scatter(place, slots.at[slot], [big[0].at[k % 8]] + [b.at[k] for b in big[1:4]], PIECE_ORDER[k],
                       big[4].at[k], big[5].at[k], put)

    def putter(ref, r0, c0):
        def put(value):
            ref[pl.ds(r0, 32), pl.ds(c0, 512)] = value
        return put

    agenda = []
    for i, (r0, c0) in enumerate(DOWN_CUTS):
        agenda.append((piece(i, i, putter(gdown_ref, r0, c0)), DOWN_STEPS[i]))
    for i in range(2):
        agenda.append((piece(8 + i, 8 + i, putter(gout_ref, 0, i * 512)), OUT_STEPS[i]))
    for i in range(6):
        col = (i % 3) * 1024 + (i // 3) * 512
        agenda.append((piece(10 + i, QKV_SLOT[i], putter(gqkv_ref, 0, col)), QKV_STEPS[i]))

    def put_small(value):
        small_ref[...] = value

    agenda.append((Scatter(place, own, [b.at[0] for b in little[:4]], 2, little[4].at[0], little[5].at[0], put_small),
                   SMALL_STEPS))
    last_step = max(steps[-1] for _, steps in agenda)

    def grad_w_out():
        for c in loads[:2]:
            c.wait()

        @pl.loop(0, 8)
        def _(i):
            rows = pl.ds(pl.multiple_of(i * 128, 128), 128)
            gattn[rows, :] = gafter[rows, :].astype(jnp.bfloat16)

        for i in range(2):
            part = dot_tn(mixed[...], gattn[:, i * 512:(i + 1) * 512])
            slots[8 + i] = part.astype(jnp.bfloat16).reshape(2, 2, 4, 2, 32, 512)

    def grad_mixed():
        for c in loads[2:]:
            c.wait()
        for i in range(2):
            cols = slice(i * 512, (i + 1) * 512)
            mixed[:, cols] = dot_nt(gattn[...], normed[cols, :]).astype(jnp.bfloat16)

        @pl.loop(0, 8)
        def _(i):
            rows = pl.ds(pl.multiple_of(i * 128, 128), 128)
            xhat, _ = norm_stats(tok[rows, :].astype(jnp.float32) + cond[rows, :].astype(jnp.float32))
            normed[rows, :] = (xhat * vec_ref[0:1, :] + vec_ref[2:3, :]).astype(jnp.bfloat16)

    def attention_back(half, first, last):
        @pl.loop(first, last)
        def _(b):
            rows = pl.ds(pl.multiple_of(b * BLOCK, BLOCK), BLOCK)
            starts = range(half * 512, half * 512 + 512, 128)
            queries = [stack_heads(qkv[rows, c:c + 128]) for c in starts]
            keys = [qkv[rows, D + c:D + c + 128] for c in starts]
            values = [qkv[rows, 2 * D + c:2 * D + c + 128] for c in starts]
            grads = [stack_heads(mixed[rows, c:c + 128]) for c in starts]
            probs = [softmax_keys(k, q) for k, q in zip(keys, queries)]
            gprobs = [dot_nt(v, g) for v, g in zip(values, grads)]
            gvalues = [dot_nn(p.astype(jnp.bfloat16), g) for p, g in zip(probs, grads)]
            gscores = [(p * (g - jnp.sum(p * g, axis=0, keepdims=True))).astype(jnp.bfloat16)
                       for p, g in zip(probs, gprobs)]
            gkeys = [dot_nn(s, q) * 0.125 for s, q in zip(gscores, queries)]
            gqueries = [merge_heads(dot_tn(s, k)) * 0.125 for s, k in zip(gscores, keys)]
            for c, gq, gk, gv in zip(starts, gqueries, gkeys, gvalues):
                gqkv[rows, c:c + 128] = gq.astype(jnp.bfloat16)
                gqkv[rows, D + c:D + c + 128] = gk.astype(jnp.bfloat16)
                gqkv[rows, 2 * D + c:2 * D + c + 128] = gv.astype(jnp.bfloat16)

    def grad_w_qkv(i):
        col = (i % 3) * 1024 + (i // 3) * 512
        part = dot_tn(normed[...], gqkv[:, col:col + 512])
        slots[QKV_SLOT[i]] = part.astype(jnp.bfloat16).reshape(2, 2, 4, 2, 32, 512)

    zero = jnp.zeros((1, D), jnp.float32)
    totals = [zero] * 4

    def input_back(h):
        if h == 0:
            load_wqkv.wait()
        rows512 = pl.ds(h * 512, 512)
        gnormed = dot_nt(gqkv[rows512, :], qkv[...])
        gafter2 = gnormed

        xhat, rstd = norm_stats(tok[rows512, :].astype(jnp.float32) + cond[rows512, :].astype(jnp.float32))
        y = gafter2 * vec_ref[0:1, :]
        m1 = jnp.mean(y, axis=-1, keepdims=True)
        m2 = jnp.mean(y * xhat, axis=-1, keepdims=True)
        normed[rows512, :] = (gafter[rows512, :] + rstd * (y - m1 - xhat * m2)).astype(jnp.bfloat16)
        add = (jnp.sum(gafter2 * xhat, axis=0, keepdims=True), jnp.sum(gafter2, axis=0, keepdims=True),
               jnp.sum(gqkv[rows512, :D].astype(jnp.float32), axis=0, keepdims=True),
               jnp.sum(gqkv[rows512, 2 * D:].astype(jnp.float32), axis=0, keepdims=True))
        for i in range(4):
            totals[i] = totals[i] + add[i]
        pltpu.make_async_copy(normed.at[rows512, :], gin_hbm.at[rows512, :], dsem.at[h]).start()

    def fill_small():
        gain1, shift1, qbias, vbias = totals
        eight = jnp.concatenate([gain1, sums_ref[0:1], shift1, qbias, vbias, sums_ref[3:4], sums_ref[1:2], sums_ref[2:3]],
                                axis=0)
        for device in range(32):
            g = device // 4
            w, s = device // 8, device % 8
            at = (w // 2, w % 2, s // 2, s % 2)
            own[at + (slice(0, 8),)] = eight[:, g * 128:(g + 1) * 128]
            own[at + (slice(8, 16),)] = jnp.broadcast_to(fcb_ref[:, device * 128:(device + 1) * 128], (8, 128))

    work = {0: [grad_w_out], 1: [grad_mixed], 2: [functools.partial(attention_back, 0, 0, 8)],
            3: [functools.partial(grad_w_qkv, i) for i in range(3)],
            4: [functools.partial(attention_back, 1, 0, 8), load_wqkv.start],
            5: [functools.partial(grad_w_qkv, i) for i in range(3, 6)],
            6: [functools.partial(input_back, 0)], 7: [functools.partial(input_back, 1), fill_small]}
    for step in range(last_step + 1):
        for f in work.get(step, ()):
            f()
        for stage_no in (4, 3, 2, 1, 0):
            for number, (p, steps) in enumerate(agenda):
                if steps[stage_no] == step:
                    if stage_no == 0 and number < 8:
                        down_loads[number].wait()
                    if stage_no == 0 and 8 <= number < 16:
                        pl.semaphore_wait(credit.at[number - 8], 1)
                    p.tick(stage_no)
                    if stage_no == 1 and number < 8:
                        pl.semaphore_signal(credit.at[number], inc=1, device_id=place.partner("c"), device_id_type=MESH)
                    if stage_no == 4:
                        p.finish()
    for h in range(2):
        rows512 = pl.ds(h * 512, 512)
        pltpu.make_async_copy(normed.at[rows512, :], gin_hbm.at[rows512, :], dsem.at[h]).wait()


DOWN_STEPS = [[s + o for o in range(5)] for s in (0, 0, 0, 1, 1, 1, 2, 2)]
OUT_STEPS = ((2, 3, 4, 5, 6), (3, 4, 5, 6, 7))
QKV_STEPS = ((3, 4, 6, 7, 8),) * 3 + ((5, 6, 8, 9, 10),) * 3
PIECE_ORDER = (2, 0, 2, 2, 1, 2, 2, 0, 2, 2, 1, 2, 2, 0, 2, 2)
QKV_SLOT = (10, 11, 12, 0, 1, 2)
SMALL_STEPS = (7, 8, 9, 10, 11)


def backward(gafter, qkv, mixed, tok, cond, wqkv, wout, gdown, vecs, sums, fcb):
    any_ = pl.BlockSpec(memory_space=pl.ANY)
    vmem = pl.BlockSpec(memory_space=pltpu.VMEM)
    bf, f32 = jnp.bfloat16, jnp.float32
    dma = pltpu.SemaphoreType.DMA
    return pl.pallas_call(
        backward_kernel,
        out_shape=[jax.ShapeDtypeStruct((D, D), bf), jax.ShapeDtypeStruct((32, 3 * D), f32),
                   jax.ShapeDtypeStruct((32, D), f32), jax.ShapeDtypeStruct((128, D), f32),
                   jax.ShapeDtypeStruct((16, 128), f32)],
        in_specs=[any_] * 8 + [vmem] * 3,
        out_specs=[any_] + [vmem] * 4,
        scratch_shapes=[pltpu.VMEM((D, D), f32), pltpu.VMEM((D, D), bf), pltpu.VMEM((D, D), bf),
                        pltpu.VMEM((D, 3 * D), bf), pltpu.VMEM((D, 3 * D), bf), pltpu.VMEM((D, D), bf),
                        pltpu.VMEM((D, D), bf), pltpu.VMEM((D, D), bf),
                        pltpu.VMEM((13, 2, 2, 4, 2, 32, 512), bf), pltpu.VMEM((2, 2, 4, 2, 16, 128), f32),
                        dma((7,)), dma((8,))]
        + scatter_bufs(16, 32, 512, cores=8) + scatter_bufs(1, 16, 128, f32)
        + [pltpu.SemaphoreType.REGULAR((8,))],
        compiler_params=pltpu.CompilerParams(collective_id=1, has_side_effects=True, vmem_limit_bytes=63 << 20),
    )(gafter, qkv, mixed, tok, cond, wqkv, wout, gdown, vecs, sums, fcb)


def own_sums(small):
    seq = lax.axis_index("seq")
    mine = lax.dynamic_slice(small, (0, (seq % 4) * 32), (8, 32))
    return mine[:2], mine[2:], small[8]


def plain_body(
    tokens,
    condition,
    valid_mask,
    w_qkv,
    w_out,
    w_fc,
    w_down,
    norm_gains,
    biases,
    fc_bias,
    cotangent,
):
    window_count, span_rows, model_width = tokens.shape
    row_total = window_count * span_rows
    head_size = model_width // HEADS
    head_shape = (row_total // BLOCK, BLOCK, HEADS, head_size)
    keep_rows = valid_mask.reshape(row_total, 1).astype(jnp.float32)
    hidden = tokens.reshape(row_total, model_width).astype(jnp.float32) + condition.reshape(
        row_total, model_width
    ).astype(jnp.float32)
    full_qkv, full_out, full_gains, full_biases = (
        lax.all_gather(w_qkv, ("win", "seq"), axis=0, tiled=True),
        lax.all_gather(w_out, ("win", "seq"), axis=0, tiled=True),
        lax.all_gather(norm_gains, ("win", "seq"), axis=1, tiled=True),
        lax.all_gather(biases, ("win", "seq"), axis=1, tiled=True),
    )
    gain_f = full_gains.astype(jnp.float32)
    bias_f = full_biases.astype(jnp.float32)
    normed_f, norm_back_one = jax.vjp(layer_norm, hidden, gain_f[0], bias_f[0])
    normed = normed_f.astype(jnp.bfloat16)
    projected = jnp.dot(normed, full_qkv, preferred_element_type=jnp.float32)
    queries = (projected[:, :model_width] + bias_f[1]).astype(jnp.bfloat16).reshape(head_shape)
    key_rows = projected[:, model_width : 2 * model_width].astype(jnp.bfloat16).reshape(head_shape)
    values = (projected[:, 2 * model_width :] + bias_f[2]).astype(jnp.bfloat16).reshape(head_shape)
    scores = masked_scores(queries, key_rows)
    row_max = jnp.max(scores, axis=-1, keepdims=True)
    log_total = row_max + jnp.log(jnp.sum(jnp.exp(scores - row_max), axis=-1, keepdims=True))
    probs = jnp.exp(scores - log_total).astype(jnp.bfloat16)
    mixed = jnp.einsum("bhqk,bkhd->bqhd", probs, values, preferred_element_type=jnp.float32)
    mixed = mixed.reshape(row_total, model_width).astype(jnp.bfloat16)
    after_attn = hidden + jnp.dot(mixed, full_out, preferred_element_type=jnp.float32) + bias_f[3]
    full_fc, full_down, full_fc_bias = (
        lax.all_gather(w_fc, ("win", "seq"), axis=0, tiled=True),
        lax.all_gather(w_down, ("win", "seq"), axis=0, tiled=True),
        lax.all_gather(fc_bias, ("win", "seq"), axis=0, tiled=True),
    )
    normed_two_f, norm_back_two = jax.vjp(layer_norm, after_attn, gain_f[1], bias_f[4])
    normed_two = normed_two_f.astype(jnp.bfloat16)
    pre_gelu = jnp.dot(
        normed_two, full_fc, preferred_element_type=jnp.float32
    ) + full_fc_bias.astype(jnp.float32)
    gelu_f, gelu_back = jax.vjp(partial(jax.nn.gelu, approximate=False), pre_gelu)
    gelu_out = gelu_f.astype(jnp.bfloat16)
    final_rows = (
        after_attn + jnp.dot(gelu_out, full_down, preferred_element_type=jnp.float32) + bias_f[5]
    )
    output = (final_rows * keep_rows).astype(jnp.bfloat16).reshape(tokens.shape)
    back_fc, back_down = (
        lax.all_gather(w_fc, ("win", "seq"), axis=0, tiled=True),
        lax.all_gather(w_down, ("win", "seq"), axis=0, tiled=True),
    )
    grad_final = cotangent.reshape(row_total, model_width).astype(jnp.float32) * keep_rows
    grad_mlp = grad_final.astype(jnp.bfloat16)
    grad_down_local = outer_sum(gelu_out, grad_mlp)
    grad_down_bias = jnp.sum(grad_mlp.astype(jnp.float32), axis=0)
    grad_gelu = times_transposed(grad_mlp, back_down)
    grad_pre = gelu_back(grad_gelu)[0].astype(jnp.bfloat16)
    grad_fc_local = outer_sum(normed_two, grad_pre)
    grad_fc_bias_local = jnp.sum(grad_pre.astype(jnp.float32), axis=0)
    grad_w_fc, grad_w_down, grad_fc_bias = (
        lax.psum_scatter(grad_fc_local, ("win", "seq"), scatter_dimension=0, tiled=True),
        lax.psum_scatter(grad_down_local, ("win", "seq"), scatter_dimension=0, tiled=True),
        lax.psum_scatter(grad_fc_bias_local, ("win", "seq"), scatter_dimension=0, tiled=True),
    )
    grad_normed_two = times_transposed(grad_pre, back_fc)
    grad_after_norm, grad_gain_two, grad_shift_two = norm_back_two(grad_normed_two)
    grad_after = grad_final + grad_after_norm
    back_qkv, back_out = (
        lax.all_gather(w_qkv, ("win", "seq"), axis=0, tiled=True),
        lax.all_gather(w_out, ("win", "seq"), axis=0, tiled=True),
    )
    grad_attn = grad_after.astype(jnp.bfloat16)
    grad_out_local = outer_sum(mixed, grad_attn)
    grad_out_bias = jnp.sum(grad_attn.astype(jnp.float32), axis=0)
    grad_mixed = times_transposed(grad_attn, back_out).astype(jnp.bfloat16).reshape(head_shape)
    probs_full = jnp.exp(masked_scores(queries, key_rows) - log_total)
    grad_probs = jnp.einsum(
        "bqhd,bkhd->bhqk", grad_mixed, values, preferred_element_type=jnp.float32
    )
    grad_values = jnp.einsum(
        "bhqk,bqhd->bkhd", probs, grad_mixed, preferred_element_type=jnp.float32
    )
    grad_values = grad_values.reshape(row_total, model_width).astype(jnp.bfloat16)
    grad_scores = probs_full * (
        grad_probs - jnp.sum(probs_full * grad_probs, axis=-1, keepdims=True)
    )
    grad_scores = grad_scores.astype(jnp.bfloat16)
    grad_queries = (
        jnp.einsum("bhqk,bkhd->bqhd", grad_scores, key_rows, preferred_element_type=jnp.float32)
        * 0.125
    )
    grad_keys = (
        jnp.einsum("bhqk,bqhd->bkhd", grad_scores, queries, preferred_element_type=jnp.float32)
        * 0.125
    )
    grad_queries = grad_queries.reshape(row_total, model_width).astype(jnp.bfloat16)
    grad_keys = grad_keys.reshape(row_total, model_width).astype(jnp.bfloat16)
    grad_query_bias = jnp.sum(grad_queries.astype(jnp.float32), axis=0)
    grad_value_bias = jnp.sum(grad_values.astype(jnp.float32), axis=0)
    grad_projected = jnp.concatenate([grad_queries, grad_keys, grad_values], axis=1)
    grad_qkv_local = outer_sum(normed, grad_projected)
    grad_normed = times_transposed(grad_projected, back_qkv)
    grad_hidden_norm, grad_gain_one, grad_shift_one = norm_back_one(grad_normed)
    grad_input = (grad_after + grad_hidden_norm).astype(jnp.bfloat16).reshape(tokens.shape)
    gains_local = jnp.stack([grad_gain_one, grad_gain_two])
    biases_local = jnp.stack(
        [
            grad_shift_one,
            grad_query_bias,
            grad_value_bias,
            grad_out_bias,
            grad_shift_two,
            grad_down_bias,
        ]
    )
    grad_w_qkv, grad_w_out, grad_gains, grad_biases = (
        lax.psum_scatter(grad_qkv_local, ("win", "seq"), scatter_dimension=0, tiled=True),
        lax.psum_scatter(grad_out_local, ("win", "seq"), scatter_dimension=0, tiled=True),
        lax.psum_scatter(gains_local, ("win", "seq"), scatter_dimension=1, tiled=True),
        lax.psum_scatter(biases_local, ("win", "seq"), scatter_dimension=1, tiled=True),
    )
    return (
        output,
        grad_input,
        grad_w_qkv,
        grad_w_out,
        grad_w_fc,
        grad_w_down,
        grad_gains,
        grad_biases,
        grad_fc_bias,
    )


GATHER_ORDER = (2, 0, 2, 2, 1, 2)


def body(
    tokens,
    condition,
    valid_mask,
    w_qkv,
    w_out,
    w_fc,
    w_down,
    norm_gains,
    biases,
    fc_bias,
    cotangent,
):
    tok, cond, cot = (a.reshape(D, D) for a in (tokens, condition, cotangent))
    keep_rows = valid_mask.reshape(D, 1).astype(jnp.float32)
    shards = (own_small(norm_gains, biases, fc_bias), w_qkv, w_out, w_fc, w_down)
    _, full_qkv, full_out, full_fc, full_down, qkv, mixed, after, n2, grad_mlp, vecs, full_fc_bias = (
        gather_and_attend(shards, tok, cond, cot, keep_rows)
    )
    output, grad_after, grad_down_local, grad_w_fc, two_sums, fc_bias_sums = mlp(
        True, after, n2, grad_mlp, keep_rows, vecs, full_fc_bias, full_fc.reshape(D, FF), full_down.reshape(FF, D)
    )
    grad_input, grad_w_qkv, grad_w_out, grad_w_down, small = backward(
        grad_after,
        qkv,
        mixed,
        tok,
        cond,
        full_qkv.reshape(D, 3 * D),
        full_out.reshape(D, D),
        grad_down_local.reshape(2, 2, 4, 2, 128, D),
        vecs,
        two_sums,
        fc_bias_sums,
    )
    grad_gains, grad_biases, grad_fc_bias = own_sums(small)
    return (
        output.reshape(tokens.shape),
        grad_input.reshape(tokens.shape),
        grad_w_qkv,
        grad_w_out,
        grad_w_fc,
        grad_w_down,
        grad_gains,
        grad_biases,
        grad_fc_bias,
    )


def solution(mesh):
    fast = mesh.shape["win"] == 4 and mesh.shape["seq"] == 8
    return jax.shard_map(
        body if fast else plain_body,
        mesh=mesh,
        in_specs=(
            P("win", "seq", None),
            P("win", "seq", None),
            P("win", "seq"),
            P(("win", "seq"), None),
            P(("win", "seq"), None),
            P(("win", "seq"), None),
            P(("win", "seq"), None),
            P(None, ("win", "seq")),
            P(None, ("win", "seq")),
            P(("win", "seq")),
            P("win", "seq", None),
        ),
        out_specs=(
            P("win", "seq", None),
            P("win", "seq", None),
            P(("win", "seq"), None),
            P(("win", "seq"), None),
            P(("win", "seq"), None),
            P(("win", "seq"), None),
            P(None, ("win", "seq")),
            P(None, ("win", "seq")),
            P(("win", "seq")),
        ),
        check_vma=False,
    )
```

```python
import functools
from functools import partial

import jax
import jax.numpy as jnp
from jax import lax
from jax.experimental import pallas as pl
from jax.experimental.pallas import tpu as pltpu
from jax.sharding import PartitionSpec as P

MESH = pl.DeviceIdType.MESH
ALL = slice(None)


class Place:
    def __init__(self):
        win, seq = lax.axis_index("win"), lax.axis_index("seq")
        self.y, self.x = win // 2, win % 2
        self.z, self.c = seq // 2, seq % 2

    def device(self, y=None, x=None, z=None, c=None):
        y = self.y if y is None else y
        x = self.x if x is None else x
        z = self.z if z is None else z
        c = self.c if c is None else c
        return (y * 2 + x, z * 2 + c)

    def partner(self, dim):
        if dim == "x":
            return self.device(x=1 - self.x)
        if dim == "y":
            return self.device(y=1 - self.y)
        return self.device(c=1 - self.c)


def greet(place):
    barrier = pltpu.get_barrier_semaphore()
    others = [place.partner(dim) for dim in "xyc"]
    others += [place.device(z=(place.z + t) % 4) for t in (1, 2, 3)]
    for device in others:
        pl.semaphore_signal(barrier, inc=1, device_id=device, device_id_type=MESH)
    pl.semaphore_wait(barrier, 6)


def guarded(cond, thunk):
    if cond is None:
        thunk()
    else:
        pl.when(cond)(thunk)


class Gather:
    def __init__(self, place, view, order, send, recv, slack=0):
        self.p, self.view, self.send, self.recv = place, view, send, recv
        self.order, self.sent = order, []
        self.ticks = self.plan(slack)

    def region(self, got, **at):
        p = self.p
        pick = lambda d, own: at[d] if d in at else (ALL if d in got else own)
        return self.view(pick("y", p.y), pick("x", p.x), pick("z", p.z), at.get("c", p.c))

    def copy(self, region, device, number):
        return pltpu.make_async_remote_copy(
            region, region, self.send.at[number], self.recv.at[number],
            device_id=device, device_id_type=MESH)

    def push(self, cond, make, device, number):
        def go():
            self.copy(make(), device, number).start()
        guarded(cond, go)

        def end():
            self.copy(make(), device, number).wait_send()
        self.sent.append((cond, end))

    def take(self, cond, make, number):
        def go():
            self.copy(make(), self.p.device(c=1 - self.p.c), number).wait_recv()
        guarded(cond, go)

    def both(self, cond, other):
        return other if cond is None else jnp.logical_and(cond, other)

    def line(self, got, tick, cond):
        z = self.p.z
        if tick > 0:
            self.take(self.both(cond, z >= tick), lambda: self.region(got, z=z - tick), 1 + tick)
            self.take(self.both(cond, z + tick <= 3), lambda: self.region(got, z=z + tick), 4 + tick)
        if tick < 3:
            self.push(self.both(cond, jnp.logical_and(z >= tick, z < 3)),
                      lambda: self.region(got, z=z - tick), self.p.device(z=z + 1), 2 + tick)
            self.push(self.both(cond, jnp.logical_and(z + tick <= 3, z > 0)),
                      lambda: self.region(got, z=z + tick), self.p.device(z=z - 1), 5 + tick)

    def plan(self, slack):
        out = []
        p = self.p
        orders = {0: (("xzy", None),), 1: (("yzx", None),),
                  2: (("zxy", p.c == 0), ("zyx", p.c == 1))}[self.order]
        lists = []
        for order, cond in orders:
            ticks = [[]]
            got = ""
            ex = 0
            for dim in order:
                if dim == "z":
                    for t in range(4):
                        ticks[-1].append(functools.partial(self.line, got, t, cond))
                        if t < 3:
                            ticks.append([])
                else:
                    ticks[-1].append(functools.partial(
                        self.push, cond, functools.partial(self.region, got), p.partner(dim), ex))
                    if ex == 1:
                        ticks.extend([] for _ in range(slack))
                    ticks.append([])
                    own = p.x if dim == "x" else p.y
                    ticks[-1].append(functools.partial(
                        self.take, cond, functools.partial(self.region, got, **{dim: 1 - own}), ex))
                    ex += 1
                got += dim
            ticks[-1].append(functools.partial(self.push, cond, functools.partial(self.region, "xyz"),
                                               p.partner("c"), 8))
            ticks.append([])
            ticks[-1].append(functools.partial(self.take, cond,
                                               functools.partial(self.region, "xyz", c=1 - p.c), 8))
            lists.append(ticks)
        n = max(len(t) for t in lists)
        for i in range(n):
            thunks = [f for t in lists if i < len(t) for f in t[i]]
            out.append(thunks)
        return out

    def tick(self, i):
        for f in self.ticks[i]:
            f()

    def finish(self):
        for cond, end in self.sent:
            guarded(cond, end)


def run_ticks(pieces, starts, between=None):
    last = max(s + len(p.ticks) for p, s in zip(pieces, starts))
    for now in range(last):
        for p, s in zip(pieces, starts):
            if 0 <= now - s < len(p.ticks):
                p.tick(now - s)
        if between and now in between:
            between[now]()
    for p in pieces:
        p.finish()


class Scatter:
    def __init__(self, place, slot, bufs, order, send, recv, put):
        self.p, self.slot, self.bufs, self.put = place, slot, bufs, put
        self.send, self.recv, self.sent = send, recv, []
        self.ticks = self.plan(order)

    def region(self, left, **at):
        p = self.p
        pick = lambda d, own: at[d] if d in at else (ALL if d in left else own)
        return self.slot.at[pick("y", p.y), pick("x", p.x), pick("z", p.z), at.get("c", p.c)]

    def push(self, cond, make, buf, device, number):
        def copy():
            return pltpu.make_async_remote_copy(
                make(), buf, self.send.at[number], self.recv.at[number],
                device_id=device, device_id_type=MESH)
        guarded(cond, lambda: copy().start())
        self.sent.append((cond, lambda: copy().wait_send()))

    def take(self, cond, makes, bufs, numbers, last):
        def go():
            for buf, number in zip(bufs, numbers):
                pltpu.make_async_remote_copy(
                    buf, buf, self.send.at[number], self.recv.at[number],
                    device_id=self.p.partner("c"), device_id_type=MESH).wait_recv()
            region = makes()
            shape = region.shape
            outer = [()]
            while len(shape) - len(outer[0]) > 3:
                outer = [o + (i,) for o in outer for i in range(shape[len(o)])]
            for o in outer:
                many = last or len(bufs) > 1
                total = region[o + (Ellipsis,)]
                total = total.astype(jnp.float32) if many else total
                for buf in bufs:
                    total = total + buf[o + (Ellipsis,)].astype(total.dtype)
                if last:
                    self.put(total)
                else:
                    region[o + (Ellipsis,)] = total.astype(region.dtype)
        guarded(cond, go)

    def plan(self, order):
        p = self.p
        core, first, second, line = self.bufs
        variants = {0: (("yzx", None),), 1: (("xzy", None),),
                    2: (("yxz", p.c == 0), ("xyz", p.c == 1))}[order]
        ticks = [[] for _ in range(5)]
        for dims, cond in variants:
            left = "xyz"
            ticks[0].append(functools.partial(
                self.push, cond, lambda: self.region("xyz", c=1 - p.c), core, p.partner("c"), 0))
            ticks[1].append(functools.partial(
                self.take, cond, lambda: self.region("xyz"), [core], [0], False))
            for i, dim in enumerate(dims):
                rest = left.replace(dim, "")
                last = i == 2
                mine = functools.partial(self.region, rest)
                if dim == "z":
                    bufs = [line.at[t - 1] if rest else line.at[t - 1, 0] for t in (1, 2, 3)]
                    for t in (1, 2, 3):
                        to = (p.z + t) % 4
                        ticks[i + 1].append(functools.partial(
                            self.push, cond, functools.partial(self.region, rest, z=to),
                            bufs[t - 1], p.device(z=to), 2 + t))
                    ticks[i + 2].append(functools.partial(
                        self.take, cond, mine, bufs, [3, 4, 5], last))
                else:
                    buf = first if i == 0 else (second if i == 1 else second.at[0])
                    number = 1 if i == 0 else 2
                    own = p.x if dim == "x" else p.y
                    ticks[i + 1].append(functools.partial(
                        self.push, cond, functools.partial(self.region, rest, **{dim: 1 - own}),
                        buf, p.partner(dim), number))
                    ticks[i + 2].append(functools.partial(
                        self.take, cond, mine, [buf], [number], last))
                left = rest
        return ticks

    def tick(self, i):
        for f in self.ticks[i]:
            f()

    def finish(self):
        for cond, end in self.sent:
            guarded(cond, end)


SCATTER_SEMS = 6
GATHER_SEMS = 9


def scatter_bufs(count, rows, cols, dtype=jnp.bfloat16, cores=None):
    return [pltpu.VMEM((cores or count, 2, 2, 4, rows, cols), dtype), pltpu.VMEM((count, 2, 4, rows, cols), dtype),
            pltpu.VMEM((count, 4, rows, cols), dtype), pltpu.VMEM((count, 3, 2, rows, cols), dtype),
            pltpu.SemaphoreType.DMA((count, SCATTER_SEMS)), pltpu.SemaphoreType.DMA((count, SCATTER_SEMS))]


D, FF, CH = 1024, 4096, 512
DELAY = (0, 1, 4, 6, 8)
TILE = 256


def dot_nn(a, b):
    return lax.dot_general(a, b, (((1,), (0,)), ((), ())), preferred_element_type=jnp.float32)


def dot_nt(a, b):
    return lax.dot_general(a, b, (((1,), (1,)), ((), ())), preferred_element_type=jnp.float32)


def dot_tn(a, b):
    return lax.dot_general(a, b, (((0,), (0,)), ((), ())), preferred_element_type=jnp.float32)


def norm_stats(rows_in):
    mean = jnp.mean(rows_in, axis=-1, keepdims=True)
    centered = rows_in - mean
    var = jnp.mean(centered * centered, axis=-1, keepdims=True)
    rstd = lax.rsqrt(var + 1e-05)
    return centered * rstd, rstd


def gelu_both(v):
    phi = 0.5 + 0.5 * lax.erf(v * 0.7071067811865476)
    slope = phi + v * (jnp.exp(-0.5 * v * v) * 0.3989422804014327)
    return (v * phi).astype(jnp.bfloat16), slope


def mlp_kernel(comm, after_hbm, n2_hbm, gm_hbm, mask_ref, vec_ref, fcb_ref, wfc_hbm, wdn_hbm,
               out_ref, gafter_hbm, gdown_hbm, gfc_ref, small_ref, gfcb_ref,
               after, gm, n2, gelu, gp, fin, gn2, wfc, wdn, stage, slots, lsem, wsem, ssem, *rest):
    place = Place()
    if comm:
        greet(place)
    load_after = pltpu.make_async_copy(after_hbm, after, lsem.at[0])
    load_gm = pltpu.make_async_copy(gm_hbm, gm, lsem.at[1])
    load_n2 = pltpu.make_async_copy(n2_hbm, n2, lsem.at[2])
    load_n2.start()

    def fetch_fc(j):
        return pltpu.make_async_copy(wfc_hbm.at[:, pl.ds(j * CH, CH)], wfc.at[j % 2], wsem.at[j % 2, 0])

    def fetch_down(i):
        j = i % (FF // CH)
        return pltpu.make_async_copy(wdn_hbm.at[pl.ds(j * CH, CH), :], wdn.at[i % 2], wsem.at[i % 2, 1])

    fetch_fc(0).start()
    fetch_down(0).start()
    load_gm.start()
    load_after.start()

    @pl.loop(0, D // 128)
    def _(i):
        rows = pl.ds(pl.multiple_of(i * 128, 128), 128)
        fin[rows, :] = jnp.zeros((128, D), jnp.float32)
        gn2[rows, :] = jnp.zeros((128, D), jnp.float32)

    load_n2.wait()
    load_gm.wait()
    n = FF // CH

    def store(j):
        return pltpu.make_async_copy(stage.at[j % 2], gdown_hbm.at[pl.ds(j * CH, CH), :], ssem.at[j % 2])

    pieces = []
    if comm:
        bufs = rest
        for j in range(n):
            def put(value, j=j):
                gfc_ref[:, pl.ds(j * CH, CH)] = value

            pieces.append(Scatter(place, slots.at[j], [b.at[j] for b in bufs[:4]],
                                  GATHER_ORDER[j % 6], bufs[4].at[j], bufs[5].at[j], put))

    def advance(step, first, last):
        if comm:
            for now in range(first, last):
                @pl.when(step == now)
                def _(now=now):
                    for stage_no in (4, 3, 2, 1, 0):
                        j = now - DELAY[stage_no]
                        if 0 <= j < n:
                            pieces[j].tick(stage_no)
                            if stage_no == 4:
                                pieces[j].finish()

    @pl.loop(0, n)
    def _(j):
        s = j % 2
        fetch_fc(j).wait()
        fetch_down(j).wait()
        fetch_down(j + 1).start()

        @pl.when(j + 1 < n)
        def _():
            fetch_fc(j + 1).start()

        cols = pl.ds(pl.multiple_of(j * CH, CH), CH)
        pre = dot_nn(n2[...], wfc[s]) + fcb_ref[:, cols]
        act, slope = gelu_both(pre)
        grad = (dot_nt(gm[...], wdn[s]) * slope).astype(jnp.bfloat16)
        gelu[:, cols] = act
        gp[...] = grad
        gfcb_ref[:, cols] = jnp.sum(grad.astype(jnp.float32), axis=0, keepdims=True)
        gn2[...] += dot_nt(gp[...], wfc[s])
        slots[j] = dot_tn(n2[...], gp[...]).astype(jnp.bfloat16).reshape(2, 2, 4, 2, 32, CH)
        advance(j, 0, n)

    @pl.loop(0, n)
    def _(j):
        s = j % 2
        fetch_down(j + n).wait()

        @pl.when(j + 1 < n)
        def _():
            fetch_down(j + n + 1).start()

        @pl.when(j >= 2)
        def _():
            store(j - 2).wait()

        cols = pl.ds(pl.multiple_of(j * CH, CH), CH)
        fin[...] += dot_nn(gelu[:, cols], wdn[s])
        stage[s] = dot_tn(gelu[:, cols], gm[...]).astype(jnp.bfloat16)
        store(j).start()
        advance(j + n, n, 2 * n)

    store(n - 2).wait()
    store(n - 1).wait()

    def norm_step(i, sums):
        rows = pl.ds(pl.multiple_of(i * 128, 128), 128)
        xhat, rstd = norm_stats(after[rows, :])
        keep = mask_ref[rows, :]
        out_ref[rows, :] = ((after[rows, :] + fin[rows, :] + vec_ref[7:8, :]) * keep).astype(jnp.bfloat16)
        g = gn2[rows, :]
        y = g * vec_ref[1:2, :]
        m1 = jnp.mean(y, axis=-1, keepdims=True)
        m2 = jnp.mean(y * xhat, axis=-1, keepdims=True)
        gmf = gm[rows, :].astype(jnp.float32)
        ga = gmf + rstd * (y - m1 - xhat * m2)
        fin[rows, :] = ga
        gattn = ga.astype(jnp.bfloat16).astype(jnp.float32)
        return tuple(s + jnp.sum(v, axis=0, keepdims=True)
                     for s, v in zip(sums, (g * xhat, g, gmf, gattn)))

    def half(h):
        return pltpu.make_async_copy(fin.at[pl.ds(h * 512, 512), :], gafter_hbm.at[pl.ds(h * 512, 512), :], lsem.at[h])

    zero = jnp.zeros((1, D), jnp.float32)
    load_after.wait()
    sums = lax.fori_loop(0, D // 256, norm_step, (zero,) * 4)
    half(0).start()
    sums = lax.fori_loop(D // 256, D // 128, norm_step, sums)
    half(1).start()
    for i in range(4):
        small_ref[i:i + 1, :] = sums[i]
    half(0).wait()
    half(1).wait()


def mlp(comm, after, n2, gm, mask, vecs, fcb, wfc, wdn):
    n = FF // CH
    any_ = pl.BlockSpec(memory_space=pl.ANY)
    vmem = pl.BlockSpec(memory_space=pltpu.VMEM)
    return pl.pallas_call(
        functools.partial(mlp_kernel, comm),
        out_shape=[jax.ShapeDtypeStruct((D, D), jnp.bfloat16), jax.ShapeDtypeStruct((D, D), jnp.float32),
                   jax.ShapeDtypeStruct((FF, D), jnp.bfloat16), jax.ShapeDtypeStruct((32, FF), jnp.float32),
                   jax.ShapeDtypeStruct((8, D), jnp.float32), jax.ShapeDtypeStruct((1, FF), jnp.float32)],
        in_specs=[any_, any_, any_, vmem, vmem, vmem, any_, any_],
        out_specs=[vmem, any_, any_, vmem, vmem, vmem],
        scratch_shapes=[pltpu.VMEM((D, D), jnp.float32), pltpu.VMEM((D, D), jnp.bfloat16),
                        pltpu.VMEM((D, D), jnp.bfloat16),
                        pltpu.VMEM((D, FF), jnp.bfloat16), pltpu.VMEM((D, CH), jnp.bfloat16),
                        pltpu.VMEM((D, D), jnp.float32), pltpu.VMEM((D, D), jnp.float32),
                        pltpu.VMEM((2, D, CH), jnp.bfloat16), pltpu.VMEM((2, CH, D), jnp.bfloat16),
                        pltpu.VMEM((2, CH, D), jnp.bfloat16),
                        pltpu.VMEM((n, 2, 2, 4, 2, 32, CH), jnp.bfloat16),
                        pltpu.SemaphoreType.DMA((3,)), pltpu.SemaphoreType.DMA((2, 2)), pltpu.SemaphoreType.DMA((2,))]
        + (scatter_bufs(n, 32, CH) if comm else []),
        compiler_params=pltpu.CompilerParams(vmem_limit_bytes=60 << 20,
            **(dict(collective_id=2, has_side_effects=True) if comm else {})),
    )(after, n2, gm, mask, vecs, fcb, wfc, wdn)


HEADS = 16
BLOCK = 128


def layer_norm(rows_in, gain_vec, shift_vec):
    row_mean = jnp.mean(rows_in, axis=-1, keepdims=True)
    centered = rows_in - row_mean
    row_var = jnp.mean(centered * centered, axis=-1, keepdims=True)
    return centered * lax.rsqrt(row_var + 1e-05) * gain_vec + shift_vec


def outer_sum(first, second):
    return lax.dot_general(
        first, second, (((0,), (0,)), ((), ())), preferred_element_type=jnp.float32
    )


def times_transposed(first, second):
    return lax.dot_general(
        first, second, (((1,), (1,)), ((), ())), preferred_element_type=jnp.float32
    )


def masked_scores(queries_h, keys_h):
    scores = (
        jnp.einsum("bqhd,bkhd->bhqk", queries_h, keys_h, preferred_element_type=jnp.float32) * 0.125
    )
    causal = lax.broadcasted_iota(jnp.int32, scores.shape, 2) >= lax.broadcasted_iota(
        jnp.int32, scores.shape, 3
    )
    return jnp.where(causal, scores, -1e30)


def lane_low(shape):
    return lax.broadcasted_iota(jnp.int32, shape, len(shape) - 1) < 64


def stack_heads(pair):
    low = lane_low(pair.shape)
    zero = jnp.zeros_like(pair)
    return jnp.concatenate([jnp.where(low, pair, zero), jnp.where(low, zero, pair)], axis=0)


def merge_heads(stacked):
    half = stacked.shape[0] // 2
    return jnp.where(lane_low((half, stacked.shape[1])), stacked[:half], stacked[half:])


def softmax_keys(key2, query2):
    scores = dot_nt(key2, query2)
    key = lax.broadcasted_iota(jnp.int32, scores.shape, 0)
    query = lax.broadcasted_iota(jnp.int32, scores.shape, 1) % BLOCK
    scores = jnp.where(key <= query, scores, -1e30)
    top = jnp.max(scores, axis=0, keepdims=True)
    raised = jnp.exp((scores - top) * 0.125)
    return raised * (1.0 / jnp.sum(raised, axis=0, keepdims=True))


GATHER_CUTS = ([(0, (0, 16), (0, 128))]
               + [(1, (0, 32), (i * 512, 512)) for i in range(6)]
               + [(2, (0, 32), (i * 512, 512)) for i in range(2)]
               + [(3, (0, 32), (i * 512, 512)) for i in range(8)]
               + [(4, (i * 16, 16), (0, 1024)) for i in range(8)])


def gather_kernel(small, wqkv_s, wout_s, wfc_s, wdn_s, tok_hbm, cond_hbm, cot_hbm, mask_ref,
                  small_f, wqkv_f, wout_f, wfc_f, wdn_f, qkv_hbm, mixed_hbm, after_hbm, n2_hbm, gm_hbm, vec_ref, fcb_ref,
                  tok, cond, hidden, normed, wqkv, wout, qkv, mixed, smallv,
                  send, recv, own_sem, lsem, wsem, osem):
    ins = (small, wqkv_s, wout_s, wfc_s, wdn_s)
    fulls = (small_f, wqkv_f, wout_f, wfc_f, wdn_f)
    place = Place()
    greet(place)
    own = [pltpu.make_async_copy(s, f.at[place.y, place.x, place.z, place.c], own_sem.at[i])
           for i, (s, f) in enumerate(zip(ins, fulls))]
    loads = [pltpu.make_async_copy(tok_hbm, tok, lsem.at[0]), pltpu.make_async_copy(cond_hbm, cond, lsem.at[1])]
    for c in own + loads:
        c.start()
    for c in own:
        c.wait()

    def make(k):
        n, (r0, r), (c0, w) = GATHER_CUTS[k]
        view = lambda y, x, z, c: fulls[n].at[y, x, z, c, pl.ds(r0, r), pl.ds(c0, w)]
        return Gather(place, view, k % 3, send.at[k], recv.at[k], 1)

    load_small = pltpu.make_async_copy(small_f, smallv, lsem.at[2])
    load_qkv = pltpu.make_async_copy(wqkv_f, wqkv, wsem.at[0])
    load_out = pltpu.make_async_copy(wout_f, wout, wsem.at[1])
    store_qkv = pltpu.make_async_copy(qkv, qkv_hbm, osem.at[0])
    store_mixed = pltpu.make_async_copy(mixed, mixed_hbm, osem.at[1])
    store_after = pltpu.make_async_copy(hidden, after_hbm, osem.at[2])

    def add_hidden():
        for c in loads:
            c.wait()

        @pl.loop(0, D // 128)
        def _(i):
            rows = pl.ds(pl.multiple_of(i * 128, 128), 128)
            hidden[rows, :] = tok[rows, :].astype(jnp.float32) + cond[rows, :].astype(jnp.float32)

    def first_norm():
        load_small.start()
        load_small.wait()
        for g in range(8):
            win, z0 = g // 2, (g % 2) * 2
            total = None
            for i in range(4):
                y, x, z, c = win // 2, win % 2, z0 + i // 2, i % 2
                one = smallv[y, x, z, c].astype(jnp.float32)
                device = g * 4 + i
                fcb_ref[:, device * 128:(device + 1) * 128] = one[8:9]
                total = one[:8] if total is None else total + one[:8]
            vec_ref[:, g * 128:(g + 1) * 128] = total

        @pl.loop(0, D // 128)
        def _(i):
            rows = pl.ds(pl.multiple_of(i * 128, 128), 128)
            xhat, _ = norm_stats(hidden[rows, :])
            normed[rows, :] = (xhat * vec_ref[0:1, :] + vec_ref[2:3, :]).astype(jnp.bfloat16)

    def project(first, last):
        for i in range(first, last):
            cols = slice(i * 512, (i + 1) * 512)
            weight = wqkv[:, :, :, :, :, cols].reshape(D, 512)
            part = dot_nn(normed[...], weight)
            if i < 2:
                part = part + vec_ref[3:4, cols]
            if i >= 4:
                part = part + vec_ref[4:5, i * 512 - 2048:i * 512 - 1536]
            qkv[:, cols] = part.astype(jnp.bfloat16)

    def attend(first, last):
        @pl.loop(first, last)
        def _(b):
            rows = pl.ds(pl.multiple_of(b * BLOCK, BLOCK), BLOCK)
            starts = range(0, D, 128)
            queries = [stack_heads(qkv[rows, c:c + 128]) for c in starts]
            keys = [qkv[rows, D + c:D + c + 128] for c in starts]
            values = [qkv[rows, 2 * D + c:2 * D + c + 128] for c in starts]
            probs = [softmax_keys(k, q).astype(jnp.bfloat16) for k, q in zip(keys, queries)]
            outs = [merge_heads(dot_tn(p, v)) for p, v in zip(probs, values)]
            for c, out in zip(starts, outs):
                mixed[rows, c:c + 128] = out.astype(jnp.bfloat16)

    def output_projection():
        load_out.wait()
        for i in range(2):
            cols = slice(i * 512, (i + 1) * 512)
            part = dot_nn(mixed[...], wout[:, :, :, :, :, cols].reshape(D, 512))
            hidden[:, cols] += part + vec_ref[5:6, cols]
        store_after.start()

    store_n2 = pltpu.make_async_copy(tok, n2_hbm, osem.at[3])
    store_gm = pltpu.make_async_copy(cond, gm_hbm, osem.at[4])
    load_cot = pltpu.make_async_copy(cot_hbm, cond, lsem.at[3])

    def mask_cotangent():
        load_cot.wait()

        @pl.loop(0, D // 128)
        def _(i):
            rows = pl.ds(pl.multiple_of(i * 128, 128), 128)
            cond[rows, :] = (cond[rows, :].astype(jnp.float32) * mask_ref[rows, :]).astype(jnp.bfloat16)

        store_gm.start()

    def second_norm():
        @pl.loop(0, D // 128)
        def _(i):
            rows = pl.ds(pl.multiple_of(i * 128, 128), 128)
            xhat, _ = norm_stats(hidden[rows, :])
            tok[rows, :] = (xhat * vec_ref[1:2, :] + vec_ref[6:7, :]).astype(jnp.bfloat16)

        store_n2.start()

    def step0():
        add_hidden()
        load_cot.start()

    def step8():
        load_qkv.wait()
        project(0, 6)
        store_qkv.start()

    def step7():
        load_qkv.start()

    def step9():
        load_out.start()
        attend(0, 4)

    def step10():
        attend(4, 8)
        store_mixed.start()

    between = {0: step0, 2: mask_cotangent, 7: first_norm, 8: step7, 9: step8, 10: step9, 11: step10,
               12: output_projection, 13: second_norm}
    run_ticks([make(k) for k in range(len(GATHER_CUTS))], [max(0, (k - 1) // 3) for k in range(len(GATHER_CUTS))], between)
    store_qkv.wait()
    store_mixed.wait()
    store_after.wait()
    store_n2.wait()
    store_gm.wait()


def gather_and_attend(shards, tok, cond, cot, mask):
    any_ = pl.BlockSpec(memory_space=pl.ANY)
    vmem = pl.BlockSpec(memory_space=pltpu.VMEM)
    count = len(GATHER_CUTS)
    bf, f32 = jnp.bfloat16, jnp.float32
    dma = pltpu.SemaphoreType.DMA
    return pl.pallas_call(
        gather_kernel,
        out_shape=[jax.ShapeDtypeStruct((2, 2, 4, 2) + s.shape, s.dtype) for s in shards]
        + [jax.ShapeDtypeStruct((D, 3 * D), bf), jax.ShapeDtypeStruct((D, D), bf), jax.ShapeDtypeStruct((D, D), f32),
           jax.ShapeDtypeStruct((D, D), bf), jax.ShapeDtypeStruct((D, D), bf),
           jax.ShapeDtypeStruct((8, D), f32), jax.ShapeDtypeStruct((1, FF), f32)],
        in_specs=[any_] * 8 + [vmem],
        out_specs=[any_] * 10 + [vmem] * 2,
        scratch_shapes=[pltpu.VMEM((D, D), bf), pltpu.VMEM((D, D), bf), pltpu.VMEM((D, D), f32), pltpu.VMEM((D, D), bf),
                        pltpu.VMEM((2, 2, 4, 2, 32, 3 * D), bf), pltpu.VMEM((2, 2, 4, 2, 32, D), bf),
                        pltpu.VMEM((D, 3 * D), bf), pltpu.VMEM((D, D), bf), pltpu.VMEM((2, 2, 4, 2, 16, 128), bf),
                        dma((count, GATHER_SEMS)), dma((count, GATHER_SEMS)), dma((5,)), dma((4,)), dma((2,)), dma((5,))],
        compiler_params=pltpu.CompilerParams(collective_id=0, has_side_effects=True, vmem_limit_bytes=60 << 20),
    )(*shards, tok, cond, cot, mask)


def own_small(gains, biases, fc_bias):
    seq = lax.axis_index("seq")
    eight = jnp.concatenate([gains, biases], axis=0)
    placed = jnp.where(jnp.arange(4)[None, :, None] == seq % 4, eight[:, None, :], 0).reshape(8, 128)
    return jnp.concatenate([placed, fc_bias.reshape(1, 128), jnp.zeros((7, 128), fc_bias.dtype)], axis=0)


DOWN_CUTS = [(r0, c0) for r0 in range(0, 128, 32) for c0 in (0, 512)]


def backward_kernel(gafter_hbm, qkv_hbm, mixed_hbm, tok_hbm, cond_hbm, wqkv_hbm, wout_hbm, gdown_hbm, vec_ref,
                    sums_ref, fcb_ref,
                    gin_hbm, gqkv_ref, gout_ref, gdown_ref, small_ref,
                    gafter, gattn, mixed, qkv, gqkv, tok, cond, normed, slots, own, lsem, dsem,
                    *rest):
    big, little, credit = rest[:6], rest[6:12], rest[12]
    place = Place()
    greet(place)
    loads = [pltpu.make_async_copy(s, d, lsem.at[i]) for i, (s, d) in enumerate((
        (gafter_hbm, gafter), (mixed_hbm, mixed), (wout_hbm, normed), (tok_hbm, tok), (cond_hbm, cond), (qkv_hbm, qkv)))]
    down_loads = [pltpu.make_async_copy(gdown_hbm.at[:, :, :, :, pl.ds(r0, 32), pl.ds(c0, 512)], slots.at[i], dsem.at[i])
                  for i, (r0, c0) in enumerate(DOWN_CUTS)]
    for c in down_loads[:2] + loads + down_loads[2:]:
        c.start()
    load_wqkv = pltpu.make_async_copy(wqkv_hbm, qkv, lsem.at[6])

    def piece(k, slot, put):
        return Scatter(place, slots.at[slot], [big[0].at[k % 8]] + [b.at[k] for b in big[1:4]], PIECE_ORDER[k],
                       big[4].at[k], big[5].at[k], put)

    def putter(ref, r0, c0):
        def put(value):
            ref[pl.ds(r0, 32), pl.ds(c0, 512)] = value
        return put

    agenda = []
    for i, (r0, c0) in enumerate(DOWN_CUTS):
        agenda.append((piece(i, i, putter(gdown_ref, r0, c0)), DOWN_STEPS[i]))
    for i in range(2):
        agenda.append((piece(8 + i, 8 + i, putter(gout_ref, 0, i * 512)), OUT_STEPS[i]))
    for i in range(6):
        col = (i % 3) * 1024 + (i // 3) * 512
        agenda.append((piece(10 + i, QKV_SLOT[i], putter(gqkv_ref, 0, col)), QKV_STEPS[i]))

    def put_small(value):
        small_ref[...] = value

    agenda.append((Scatter(place, own, [b.at[0] for b in little[:4]], 2, little[4].at[0], little[5].at[0], put_small),
                   SMALL_STEPS))
    last_step = max(steps[-1] for _, steps in agenda)

    def grad_w_out():
        for c in loads[:2]:
            c.wait()

        @pl.loop(0, 8)
        def _(i):
            rows = pl.ds(pl.multiple_of(i * 128, 128), 128)
            gattn[rows, :] = gafter[rows, :].astype(jnp.bfloat16)

        for i in range(2):
            part = dot_tn(mixed[...], gattn[:, i * 512:(i + 1) * 512])
            slots[8 + i] = part.astype(jnp.bfloat16).reshape(2, 2, 4, 2, 32, 512)

    def grad_mixed():
        for c in loads[2:]:
            c.wait()
        for i in range(2):
            cols = slice(i * 512, (i + 1) * 512)
            mixed[:, cols] = dot_nt(gattn[...], normed[cols, :]).astype(jnp.bfloat16)

        @pl.loop(0, 8)
        def _(i):
            rows = pl.ds(pl.multiple_of(i * 128, 128), 128)
            xhat, _ = norm_stats(tok[rows, :].astype(jnp.float32) + cond[rows, :].astype(jnp.float32))
            normed[rows, :] = (xhat * vec_ref[0:1, :] + vec_ref[2:3, :]).astype(jnp.bfloat16)

    def attention_back(half, first, last):
        @pl.loop(first, last)
        def _(b):
            rows = pl.ds(pl.multiple_of(b * BLOCK, BLOCK), BLOCK)
            starts = range(half * 512, half * 512 + 512, 128)
            queries = [stack_heads(qkv[rows, c:c + 128]) for c in starts]
            keys = [qkv[rows, D + c:D + c + 128] for c in starts]
            values = [qkv[rows, 2 * D + c:2 * D + c + 128] for c in starts]
            grads = [stack_heads(mixed[rows, c:c + 128]) for c in starts]
            probs = [softmax_keys(k, q) for k, q in zip(keys, queries)]
            gprobs = [dot_nt(v, g) for v, g in zip(values, grads)]
            gvalues = [dot_nn(p.astype(jnp.bfloat16), g) for p, g in zip(probs, grads)]
            gscores = [(p * (g - jnp.sum(p * g, axis=0, keepdims=True))).astype(jnp.bfloat16)
                       for p, g in zip(probs, gprobs)]
            gkeys = [dot_nn(s, q) * 0.125 for s, q in zip(gscores, queries)]
            gqueries = [merge_heads(dot_tn(s, k)) * 0.125 for s, k in zip(gscores, keys)]
            for c, gq, gk, gv in zip(starts, gqueries, gkeys, gvalues):
                gqkv[rows, c:c + 128] = gq.astype(jnp.bfloat16)
                gqkv[rows, D + c:D + c + 128] = gk.astype(jnp.bfloat16)
                gqkv[rows, 2 * D + c:2 * D + c + 128] = gv.astype(jnp.bfloat16)

    def grad_w_qkv(i):
        col = (i % 3) * 1024 + (i // 3) * 512
        part = dot_tn(normed[...], gqkv[:, col:col + 512])
        slots[QKV_SLOT[i]] = part.astype(jnp.bfloat16).reshape(2, 2, 4, 2, 32, 512)

    zero = jnp.zeros((1, D), jnp.float32)
    totals = [zero] * 4

    def input_back(h):
        if h == 0:
            load_wqkv.wait()
        rows512 = pl.ds(h * 512, 512)
        gnormed = dot_nt(gqkv[rows512, :], qkv[...])
        gafter2 = gnormed

        xhat, rstd = norm_stats(tok[rows512, :].astype(jnp.float32) + cond[rows512, :].astype(jnp.float32))
        y = gafter2 * vec_ref[0:1, :]
        m1 = jnp.mean(y, axis=-1, keepdims=True)
        m2 = jnp.mean(y * xhat, axis=-1, keepdims=True)
        normed[rows512, :] = (gafter[rows512, :] + rstd * (y - m1 - xhat * m2)).astype(jnp.bfloat16)
        add = (jnp.sum(gafter2 * xhat, axis=0, keepdims=True), jnp.sum(gafter2, axis=0, keepdims=True),
               jnp.sum(gqkv[rows512, :D].astype(jnp.float32), axis=0, keepdims=True),
               jnp.sum(gqkv[rows512, 2 * D:].astype(jnp.float32), axis=0, keepdims=True))
        for i in range(4):
            totals[i] = totals[i] + add[i]
        pltpu.make_async_copy(normed.at[rows512, :], gin_hbm.at[rows512, :], dsem.at[h]).start()

    def fill_small():
        gain1, shift1, qbias, vbias = totals
        eight = jnp.concatenate([gain1, sums_ref[0:1], shift1, qbias, vbias, sums_ref[3:4], sums_ref[1:2], sums_ref[2:3]],
                                axis=0)
        for device in range(32):
            g = device // 4
            w, s = device // 8, device % 8
            at = (w // 2, w % 2, s // 2, s % 2)
            own[at + (slice(0, 8),)] = eight[:, g * 128:(g + 1) * 128]
            own[at + (slice(8, 16),)] = jnp.broadcast_to(fcb_ref[:, device * 128:(device + 1) * 128], (8, 128))

    work = {0: [grad_w_out], 1: [grad_mixed], 2: [functools.partial(attention_back, 0, 0, 8)],
            3: [functools.partial(grad_w_qkv, i) for i in range(3)],
            4: [functools.partial(attention_back, 1, 0, 8), load_wqkv.start],
            5: [functools.partial(grad_w_qkv, i) for i in range(3, 6)],
            6: [functools.partial(input_back, 0)], 7: [functools.partial(input_back, 1), fill_small]}
    for step in range(last_step + 1):
        for f in work.get(step, ()):
            f()
        for stage_no in (4, 3, 2, 1, 0):
            for number, (p, steps) in enumerate(agenda):
                if steps[stage_no] == step:
                    if stage_no == 0 and number < 8:
                        down_loads[number].wait()
                    if stage_no == 0 and 8 <= number < 16:
                        pl.semaphore_wait(credit.at[number - 8], 1)
                    p.tick(stage_no)
                    if stage_no == 1 and number < 8:
                        pl.semaphore_signal(credit.at[number], inc=1, device_id=place.partner("c"), device_id_type=MESH)
                    if stage_no == 4:
                        p.finish()
    for h in range(2):
        rows512 = pl.ds(h * 512, 512)
        pltpu.make_async_copy(normed.at[rows512, :], gin_hbm.at[rows512, :], dsem.at[h]).wait()


DOWN_STEPS = ((0, 1, 2, 3, 4),
    (0, 1, 2, 3, 4),
    (0, 1, 2, 3, 4),
    (0, 1, 2, 3, 4),
    (1, 2, 3, 5, 6),
    (2, 4, 6, 7, 8),
    (1, 2, 3, 5, 6),
    (1, 2, 3, 4, 5))
OUT_STEPS = ((2, 3, 4, 5, 7),
    (1, 3, 6, 7, 8))
QKV_STEPS = ((4, 5, 7, 8, 9),
    (3, 5, 7, 8, 9),
    (3, 4, 6, 7, 8),
    (6, 7, 9, 11, 12),
    (6, 7, 9, 11, 12),
    (5, 6, 9, 11, 12))
PIECE_ORDER = (2, 0, 2, 1, 2, 2, 2, 2, 2, 2, 2, 2, 1, 2, 2, 2)
QKV_SLOT = (10, 11, 12, 0, 1, 2)
SMALL_STEPS = (7, 9, 10, 11, 12)


def backward(gafter, qkv, mixed, tok, cond, wqkv, wout, gdown, vecs, sums, fcb):
    any_ = pl.BlockSpec(memory_space=pl.ANY)
    vmem = pl.BlockSpec(memory_space=pltpu.VMEM)
    bf, f32 = jnp.bfloat16, jnp.float32
    dma = pltpu.SemaphoreType.DMA
    return pl.pallas_call(
        backward_kernel,
        out_shape=[jax.ShapeDtypeStruct((D, D), bf), jax.ShapeDtypeStruct((32, 3 * D), f32),
                   jax.ShapeDtypeStruct((32, D), f32), jax.ShapeDtypeStruct((128, D), f32),
                   jax.ShapeDtypeStruct((16, 128), f32)],
        in_specs=[any_] * 8 + [vmem] * 3,
        out_specs=[any_] + [vmem] * 4,
        scratch_shapes=[pltpu.VMEM((D, D), f32), pltpu.VMEM((D, D), bf), pltpu.VMEM((D, D), bf),
                        pltpu.VMEM((D, 3 * D), bf), pltpu.VMEM((D, 3 * D), bf), pltpu.VMEM((D, D), bf),
                        pltpu.VMEM((D, D), bf), pltpu.VMEM((D, D), bf),
                        pltpu.VMEM((13, 2, 2, 4, 2, 32, 512), bf), pltpu.VMEM((2, 2, 4, 2, 16, 128), f32),
                        dma((7,)), dma((8,))]
        + scatter_bufs(16, 32, 512, cores=8) + scatter_bufs(1, 16, 128, f32)
        + [pltpu.SemaphoreType.REGULAR((8,))],
        compiler_params=pltpu.CompilerParams(collective_id=1, has_side_effects=True, vmem_limit_bytes=63 << 20),
    )(gafter, qkv, mixed, tok, cond, wqkv, wout, gdown, vecs, sums, fcb)


def own_sums(small):
    seq = lax.axis_index("seq")
    mine = lax.dynamic_slice(small, (0, (seq % 4) * 32), (8, 32))
    return mine[:2], mine[2:], small[8]


def plain_body(
    tokens,
    condition,
    valid_mask,
    w_qkv,
    w_out,
    w_fc,
    w_down,
    norm_gains,
    biases,
    fc_bias,
    cotangent,
):
    window_count, span_rows, model_width = tokens.shape
    row_total = window_count * span_rows
    head_size = model_width // HEADS
    head_shape = (row_total // BLOCK, BLOCK, HEADS, head_size)
    keep_rows = valid_mask.reshape(row_total, 1).astype(jnp.float32)
    hidden = tokens.reshape(row_total, model_width).astype(jnp.float32) + condition.reshape(
        row_total, model_width
    ).astype(jnp.float32)
    full_qkv, full_out, full_gains, full_biases = (
        lax.all_gather(w_qkv, ("win", "seq"), axis=0, tiled=True),
        lax.all_gather(w_out, ("win", "seq"), axis=0, tiled=True),
        lax.all_gather(norm_gains, ("win", "seq"), axis=1, tiled=True),
        lax.all_gather(biases, ("win", "seq"), axis=1, tiled=True),
    )
    gain_f = full_gains.astype(jnp.float32)
    bias_f = full_biases.astype(jnp.float32)
    normed_f, norm_back_one = jax.vjp(layer_norm, hidden, gain_f[0], bias_f[0])
    normed = normed_f.astype(jnp.bfloat16)
    projected = jnp.dot(normed, full_qkv, preferred_element_type=jnp.float32)
    queries = (projected[:, :model_width] + bias_f[1]).astype(jnp.bfloat16).reshape(head_shape)
    key_rows = projected[:, model_width : 2 * model_width].astype(jnp.bfloat16).reshape(head_shape)
    values = (projected[:, 2 * model_width :] + bias_f[2]).astype(jnp.bfloat16).reshape(head_shape)
    scores = masked_scores(queries, key_rows)
    row_max = jnp.max(scores, axis=-1, keepdims=True)
    log_total = row_max + jnp.log(jnp.sum(jnp.exp(scores - row_max), axis=-1, keepdims=True))
    probs = jnp.exp(scores - log_total).astype(jnp.bfloat16)
    mixed = jnp.einsum("bhqk,bkhd->bqhd", probs, values, preferred_element_type=jnp.float32)
    mixed = mixed.reshape(row_total, model_width).astype(jnp.bfloat16)
    after_attn = hidden + jnp.dot(mixed, full_out, preferred_element_type=jnp.float32) + bias_f[3]
    full_fc, full_down, full_fc_bias = (
        lax.all_gather(w_fc, ("win", "seq"), axis=0, tiled=True),
        lax.all_gather(w_down, ("win", "seq"), axis=0, tiled=True),
        lax.all_gather(fc_bias, ("win", "seq"), axis=0, tiled=True),
    )
    normed_two_f, norm_back_two = jax.vjp(layer_norm, after_attn, gain_f[1], bias_f[4])
    normed_two = normed_two_f.astype(jnp.bfloat16)
    pre_gelu = jnp.dot(
        normed_two, full_fc, preferred_element_type=jnp.float32
    ) + full_fc_bias.astype(jnp.float32)
    gelu_f, gelu_back = jax.vjp(partial(jax.nn.gelu, approximate=False), pre_gelu)
    gelu_out = gelu_f.astype(jnp.bfloat16)
    final_rows = (
        after_attn + jnp.dot(gelu_out, full_down, preferred_element_type=jnp.float32) + bias_f[5]
    )
    output = (final_rows * keep_rows).astype(jnp.bfloat16).reshape(tokens.shape)
    back_fc, back_down = (
        lax.all_gather(w_fc, ("win", "seq"), axis=0, tiled=True),
        lax.all_gather(w_down, ("win", "seq"), axis=0, tiled=True),
    )
    grad_final = cotangent.reshape(row_total, model_width).astype(jnp.float32) * keep_rows
    grad_mlp = grad_final.astype(jnp.bfloat16)
    grad_down_local = outer_sum(gelu_out, grad_mlp)
    grad_down_bias = jnp.sum(grad_mlp.astype(jnp.float32), axis=0)
    grad_gelu = times_transposed(grad_mlp, back_down)
    grad_pre = gelu_back(grad_gelu)[0].astype(jnp.bfloat16)
    grad_fc_local = outer_sum(normed_two, grad_pre)
    grad_fc_bias_local = jnp.sum(grad_pre.astype(jnp.float32), axis=0)
    grad_w_fc, grad_w_down, grad_fc_bias = (
        lax.psum_scatter(grad_fc_local, ("win", "seq"), scatter_dimension=0, tiled=True),
        lax.psum_scatter(grad_down_local, ("win", "seq"), scatter_dimension=0, tiled=True),
        lax.psum_scatter(grad_fc_bias_local, ("win", "seq"), scatter_dimension=0, tiled=True),
    )
    grad_normed_two = times_transposed(grad_pre, back_fc)
    grad_after_norm, grad_gain_two, grad_shift_two = norm_back_two(grad_normed_two)
    grad_after = grad_final + grad_after_norm
    back_qkv, back_out = (
        lax.all_gather(w_qkv, ("win", "seq"), axis=0, tiled=True),
        lax.all_gather(w_out, ("win", "seq"), axis=0, tiled=True),
    )
    grad_attn = grad_after.astype(jnp.bfloat16)
    grad_out_local = outer_sum(mixed, grad_attn)
    grad_out_bias = jnp.sum(grad_attn.astype(jnp.float32), axis=0)
    grad_mixed = times_transposed(grad_attn, back_out).astype(jnp.bfloat16).reshape(head_shape)
    probs_full = jnp.exp(masked_scores(queries, key_rows) - log_total)
    grad_probs = jnp.einsum(
        "bqhd,bkhd->bhqk", grad_mixed, values, preferred_element_type=jnp.float32
    )
    grad_values = jnp.einsum(
        "bhqk,bqhd->bkhd", probs, grad_mixed, preferred_element_type=jnp.float32
    )
    grad_values = grad_values.reshape(row_total, model_width).astype(jnp.bfloat16)
    grad_scores = probs_full * (
        grad_probs - jnp.sum(probs_full * grad_probs, axis=-1, keepdims=True)
    )
    grad_scores = grad_scores.astype(jnp.bfloat16)
    grad_queries = (
        jnp.einsum("bhqk,bkhd->bqhd", grad_scores, key_rows, preferred_element_type=jnp.float32)
        * 0.125
    )
    grad_keys = (
        jnp.einsum("bhqk,bqhd->bkhd", grad_scores, queries, preferred_element_type=jnp.float32)
        * 0.125
    )
    grad_queries = grad_queries.reshape(row_total, model_width).astype(jnp.bfloat16)
    grad_keys = grad_keys.reshape(row_total, model_width).astype(jnp.bfloat16)
    grad_query_bias = jnp.sum(grad_queries.astype(jnp.float32), axis=0)
    grad_value_bias = jnp.sum(grad_values.astype(jnp.float32), axis=0)
    grad_projected = jnp.concatenate([grad_queries, grad_keys, grad_values], axis=1)
    grad_qkv_local = outer_sum(normed, grad_projected)
    grad_normed = times_transposed(grad_projected, back_qkv)
    grad_hidden_norm, grad_gain_one, grad_shift_one = norm_back_one(grad_normed)
    grad_input = (grad_after + grad_hidden_norm).astype(jnp.bfloat16).reshape(tokens.shape)
    gains_local = jnp.stack([grad_gain_one, grad_gain_two])
    biases_local = jnp.stack(
        [
            grad_shift_one,
            grad_query_bias,
            grad_value_bias,
            grad_out_bias,
            grad_shift_two,
            grad_down_bias,
        ]
    )
    grad_w_qkv, grad_w_out, grad_gains, grad_biases = (
        lax.psum_scatter(grad_qkv_local, ("win", "seq"), scatter_dimension=0, tiled=True),
        lax.psum_scatter(grad_out_local, ("win", "seq"), scatter_dimension=0, tiled=True),
        lax.psum_scatter(gains_local, ("win", "seq"), scatter_dimension=1, tiled=True),
        lax.psum_scatter(biases_local, ("win", "seq"), scatter_dimension=1, tiled=True),
    )
    return (
        output,
        grad_input,
        grad_w_qkv,
        grad_w_out,
        grad_w_fc,
        grad_w_down,
        grad_gains,
        grad_biases,
        grad_fc_bias,
    )


GATHER_ORDER = (2, 0, 2, 2, 1, 2)


def body(
    tokens,
    condition,
    valid_mask,
    w_qkv,
    w_out,
    w_fc,
    w_down,
    norm_gains,
    biases,
    fc_bias,
    cotangent,
):
    tok, cond, cot = (a.reshape(D, D) for a in (tokens, condition, cotangent))
    keep_rows = valid_mask.reshape(D, 1).astype(jnp.float32)
    shards = (own_small(norm_gains, biases, fc_bias), w_qkv, w_out, w_fc, w_down)
    _, full_qkv, full_out, full_fc, full_down, qkv, mixed, after, n2, grad_mlp, vecs, full_fc_bias = (
        gather_and_attend(shards, tok, cond, cot, keep_rows)
    )
    output, grad_after, grad_down_local, grad_w_fc, two_sums, fc_bias_sums = mlp(
        True, after, n2, grad_mlp, keep_rows, vecs, full_fc_bias, full_fc.reshape(D, FF), full_down.reshape(FF, D)
    )
    grad_input, grad_w_qkv, grad_w_out, grad_w_down, small = backward(
        grad_after,
        qkv,
        mixed,
        tok,
        cond,
        full_qkv.reshape(D, 3 * D),
        full_out.reshape(D, D),
        grad_down_local.reshape(2, 2, 4, 2, 128, D),
        vecs,
        two_sums,
        fc_bias_sums,
    )
    grad_gains, grad_biases, grad_fc_bias = own_sums(small)
    return (
        output.reshape(tokens.shape),
        grad_input.reshape(tokens.shape),
        grad_w_qkv,
        grad_w_out,
        grad_w_fc,
        grad_w_down,
        grad_gains,
        grad_biases,
        grad_fc_bias,
    )


def solution(mesh):
    fast = mesh.shape["win"] == 4 and mesh.shape["seq"] == 8
    return jax.shard_map(
        body if fast else plain_body,
        mesh=mesh,
        in_specs=(
            P("win", "seq", None),
            P("win", "seq", None),
            P("win", "seq"),
            P(("win", "seq"), None),
            P(("win", "seq"), None),
            P(("win", "seq"), None),
            P(("win", "seq"), None),
            P(None, ("win", "seq")),
            P(None, ("win", "seq")),
            P(("win", "seq")),
            P("win", "seq", None),
        ),
        out_specs=(
            P("win", "seq", None),
            P("win", "seq", None),
            P(("win", "seq"), None),
            P(("win", "seq"), None),
            P(("win", "seq"), None),
            P(("win", "seq"), None),
            P(None, ("win", "seq")),
            P(None, ("win", "seq")),
            P(("win", "seq")),
        ),
        check_vma=False,
    )
```
